32 devices in a mesh: section: 4 (over x, core), ctx: 8 (over z, y).
Axes of the slice: x: 2, y: 2, z: 4, core: 2. Of those that a mesh axis runs over, the one named last changes fastest.
Arguments:
- queries: bfloat16 [4, 1024, 4096], P('section', 'ctx'), may hold values from -8 to 8
- keys: bfloat16 [4, 1024, 512], P('section', 'ctx'), may hold values from -8 to 8
- values: bfloat16 [4, 1024, 512], P('section', 'ctx'), may hold values from -6 to 6
- token_pos: int32 [1024], P('ctx'), may hold values from 0 to 1023, as said below
- segment: int32 [1024], replicated, may hold values from 0 to 7, never falling along the last dimension, each value on 1 to 256 neighbouring positions
Outputs:
- handed: bfloat16 [4, 1024, 4096], P('section', 'ctx')
The draws below stay inside these ranges and needn't reach their ends.
Inputs may be any that keep to these rules, and one draw needn't show every extreme that they name: `token_pos`: a permutation of the 1024 positions; the 128 rows of one index of ctx are two runs of 64 consecutive positions, starting at b * 64 and at (15 - b) * 64, each b used by one index. `segment`: document numbers never fall along the positions; each document covers 1 to 256 positions, one exactly that many.
All inputs are finite; a program needn't handle non-finite values.
Results may differ from the reference program's by a relative error of at most 0.0059.
Values may be sent and summed in bfloat16 or wider, within the bound.
No kernel may reach another device: no remote copies, remote signals or barrier semaphores. Data moves between devices by JAX's collectives and lax.ppermute only.
A program may use at most 64 MiB of HBM per device.

```python
import math
import jax
import jax.numpy as jnp
import numpy as np
from jax import lax

HEAD_SIZE = 128
QUERY_HEADS = 32
KEY_VALUE_HEADS = 4
TOK_DEV = 128
DOCS = 8
SEQUENCE_TOKENS = 1024
MICRO_BATCHES = 4


def draw_keys(key, part):
    root_random_key = jax.random.fold_in(key, 13)
    random_draw_result = jnp.clip(jax.random.normal(root_random_key, (MICRO_BATCHES, SEQUENCE_TOKENS, KEY_VALUE_HEADS * HEAD_SIZE), jnp.float32), -6.0, 6.0)
    return random_draw_result.astype(jnp.bfloat16)


def draw_queries(key, part):
    root_random_key = jax.random.fold_in(key, 21)
    random_draw_result = jnp.clip(jax.random.normal(root_random_key, (MICRO_BATCHES, SEQUENCE_TOKENS, QUERY_HEADS * HEAD_SIZE), jnp.float32), -6.0, 6.0)
    return random_draw_result.astype(jnp.bfloat16)


def draw_token_pos(key, part):
    block_count = SEQUENCE_TOKENS // TOK_DEV
    rows_per_half = TOK_DEV // 2
    block_order = jax.random.permutation(key, block_count)
    offsets = jnp.arange(rows_per_half)
    early_run = block_order[:, None] * rows_per_half + offsets[None, :]
    late_run = (2 * block_count - 1 - block_order)[:, None] * rows_per_half + offsets[None, :]
    return jnp.concatenate([early_run, late_run], axis=1).reshape(SEQUENCE_TOKENS).astype(jnp.int32)


def block_levels(key, shape, pieces, least, top_value):
    level = 1.0
    for dim, shards_of in pieces:
        draws = jax.random.uniform(jax.random.fold_in(jax.random.fold_in(key, 6), dim), (shards_of,), jnp.float32, least / len(pieces), top_value / len(pieces))
        level = level * jnp.repeat(jnp.exp(draws), shape[dim] // shards_of).reshape((-1,) + (1,) * (len(shape) - 1 - dim))
    return level


def profile(count, total, limit, lean):
    loads = [(1 << 20) // math.isqrt(rank ** lean) + 1 for rank in range(2, count + 1)]
    surplus, counts = total - limit - (count - 1), [1] * (count - 1)
    while surplus > 0:
        free = [i for i in range(count - 1) if counts[i] < limit]
        whole, left = sum([loads[i] for i in free]), surplus
        for i in free:
            more = min(limit - counts[i], max(1, left * loads[i] // whole), surplus)
            counts[i] = counts[i] + more
            surplus = surplus - more
    return np.array([limit] + counts)


def uneven_parts(stream_key, number_of, total, most, skew):
    if number_of == 2:
        one = jax.random.randint(stream_key, (), max(1, total - most), min(most, total - 1) + 1)
        return jnp.stack([one, total - one])
    tallies = jnp.asarray(profile(number_of, total, most, skew), jnp.int32)
    couples = (number_of - 1) // 2
    donor, taker = tallies[1:1 + 2 * couples:2], tallies[2:2 + 2 * couples:2]
    room = jnp.minimum(donor - 1, most - taker)
    moved = jax.random.randint(jax.random.fold_in(stream_key, 1), (couples,), 0, 1 << 20) % (room + 1)
    tallies = tallies.at[1:1 + 2 * couples:2].set(donor - moved).at[2:2 + 2 * couples:2].set(taker + moved)
    return tallies[jax.random.permutation(jax.random.fold_in(stream_key, 2), number_of)]


def scatter_about(own_key, dims, scale, limit, split=(), held_as=jnp.bfloat16):
    factor_of = block_levels(own_key, dims, split, -0.22, 0.18) if split else 1.0
    values = jax.random.normal(own_key, dims, jnp.float32) * scale * factor_of
    return jnp.minimum(jnp.maximum(values, -limit), limit).astype(held_as)


def setup_inputs(seed: int = 0) -> dict:
    splits = jax.random.split(jax.random.key(seed), 6)
    return {
        "queries": draw_queries(jax.random.fold_in(splits[5], 71), 0),
        "keys": draw_keys(jax.random.fold_in(splits[5], 71), 0),
        "values": scatter_about(splits[2], (MICRO_BATCHES, SEQUENCE_TOKENS, KEY_VALUE_HEADS * HEAD_SIZE), 1.0, 6.0, ((0, 4), (1, 8))),
        "token_pos": draw_token_pos(jax.random.fold_in(splits[5], 71), 0),
        "segment": jnp.searchsorted(jnp.cumsum(uneven_parts(splits[4], DOCS, SEQUENCE_TOKENS, SEQUENCE_TOKENS // 4, 2)), jnp.arange(SEQUENCE_TOKENS), side="right").astype(jnp.int32),
    }


def reference(queries, keys, values, token_pos, segment):
    inv_scale = 1.0 / math.sqrt(HEAD_SIZE)
    query_group_count = QUERY_HEADS // KEY_VALUE_HEADS
    doc_ids = jnp.take(segment, token_pos)
    allowed = (token_pos[None, :] <= token_pos[:, None]) & (doc_ids[None, :] == doc_ids[:, None])

    def one_head(operands):
        head_query, head_key, head_value = operands
        scores = jnp.dot(head_query.astype(jnp.float32), head_key.astype(jnp.float32).T, precision=lax.Precision.HIGHEST) * inv_scale
        scores = jnp.where(allowed, scores, jnp.float32(-1e+30))
        row_max = lax.optimization_barrier(jnp.max(scores, axis=1, keepdims=True))
        probabilities = jnp.where(allowed, jnp.exp(scores - row_max), jnp.float32(0.0))
        row_total = lax.optimization_barrier(jnp.sum(probabilities, axis=1, keepdims=True))
        weights = lax.optimization_barrier(probabilities.astype(jnp.bfloat16))
        summed = jnp.dot(weights.astype(jnp.float32), head_value.astype(jnp.float32), precision=lax.Precision.HIGHEST)
        return summed / row_total

    def one_section(operands):
        section_query, keys_of_section, values_of_section = operands
        head_queries = section_query.reshape(SEQUENCE_TOKENS, QUERY_HEADS, HEAD_SIZE).transpose(1, 0, 2)
        per_head_keys = jnp.repeat(keys_of_section.reshape(SEQUENCE_TOKENS, KEY_VALUE_HEADS, HEAD_SIZE).transpose(1, 0, 2), query_group_count, axis=0)
        per_head_values = jnp.repeat(values_of_section.reshape(SEQUENCE_TOKENS, KEY_VALUE_HEADS, HEAD_SIZE).transpose(1, 0, 2), query_group_count, axis=0)
        section_out = lax.map(one_head, (head_queries, per_head_keys, per_head_values))
        return section_out.transpose(1, 0, 2).reshape(SEQUENCE_TOKENS, QUERY_HEADS * HEAD_SIZE).astype(jnp.bfloat16)
    attended = lax.map(one_section, (queries, keys, values))
    return jnp.roll(attended, 1, axis=0)
```

```python
import functools
import math

import jax
import jax.numpy as jnp
from jax import lax
from jax.experimental import pallas as pl
from jax.experimental.pallas import tpu as pltpu
from jax.sharding import PartitionSpec as P

HEAD_SIZE = 128
QUERY_HEADS = 32
KEY_VALUE_HEADS = 4
GROUP = QUERY_HEADS // KEY_VALUE_HEADS
RUN = 64
TOK_DEV = 2 * RUN
KV_COLUMNS = KEY_VALUE_HEADS * HEAD_SIZE
TAG_ROWS = 16
BLOCK_ROWS = 2 * TOK_DEV + TAG_ROWS

masked_fill = -1e30


def attention_kernel(runs, pos_ref, segment_ref, query_ref, *refs):
    count = runs // 2
    block_refs, (out_ref, key_buf, value_buf) = refs[:count], refs[count:]
    reach = runs // 4
    span = (reach + 1) * RUN
    for block_ref in block_refs:
        tag = jnp.max(block_ref[2 * TOK_DEV :, :HEAD_SIZE].astype(jnp.float32)).astype(jnp.int32)
        for half, run in enumerate((tag, runs - 1 - tag)):
            key_buf[run] = block_ref[half * RUN : (half + 1) * RUN, :]
            value_buf[run] = block_ref[TOK_DEV + half * RUN : TOK_DEV + (half + 1) * RUN, :]

    total_positions = runs * RUN
    segment = segment_ref[...].astype(jnp.float32)
    scale = math.log2(math.e) / math.sqrt(HEAD_SIZE)
    ones = jnp.ones((span, HEAD_SIZE), jnp.bfloat16)
    for half in range(2):
        run = lax.div(pos_ref[half * RUN], RUN)
        start = jnp.maximum(run - reach, 0)
        row_pos = run * RUN + lax.broadcasted_iota(jnp.int32, (RUN, 1), 0)
        at = lax.broadcasted_iota(jnp.int32, (RUN, total_positions), 1) == row_pos
        row_doc = jnp.sum(jnp.where(at, segment, 0.0), axis=1, keepdims=True)
        doc_start = jnp.sum(jnp.where(segment < row_doc, 1.0, 0.0), axis=1, keepdims=True).astype(jnp.int32)
        key_pos = start * RUN + lax.broadcasted_iota(jnp.int32, (RUN, span), 1)
        bias = jnp.where((key_pos <= row_pos) & (key_pos >= doc_start), 0.0, masked_fill)
        bias = jnp.concatenate([bias] * GROUP, axis=0)
        rows = slice(half * RUN, (half + 1) * RUN)
        for kv in range(KEY_VALUE_HEADS):
            columns = slice(kv * HEAD_SIZE, (kv + 1) * HEAD_SIZE)
            heads = [kv * GROUP + i for i in range(GROUP)]
            query = jnp.concatenate(
                [query_ref[rows, h * HEAD_SIZE : (h + 1) * HEAD_SIZE] for h in heads], axis=0
            )
            key = key_buf[pl.ds(start, reach + 1), :, columns].reshape(span, HEAD_SIZE)
            value = value_buf[pl.ds(start, reach + 1), :, columns].reshape(span, HEAD_SIZE)
            scores = bias + lax.dot_general(
                query, key, (((1,), (1,)), ((), ())), preferred_element_type=jnp.float32
            )
            row_max = jnp.max(scores, axis=1, keepdims=True)
            weights = jnp.exp2((scores - row_max) * scale).astype(jnp.bfloat16)
            summed = jnp.dot(
                weights, jnp.concatenate([value, ones], axis=1), preferred_element_type=jnp.float32
            )
            result = (summed[:, :HEAD_SIZE] / summed[:, HEAD_SIZE:]).astype(jnp.bfloat16)
            for i, h in enumerate(heads):
                out_ref[rows, h * HEAD_SIZE : (h + 1) * HEAD_SIZE] = result[i * RUN : (i + 1) * RUN]


def per_device(queries, keys, values, token_pos, segment):
    sections, places = lax.axis_size("section"), lax.axis_size("ctx")
    runs = segment.shape[0] // RUN
    depth = places // 2

    def along(block, section_by, z_by, flip):
        pairs = []
        for s in range(sections):
            for z in range(depth):
                for y in range(2):
                    source = s * places + z * 2 + y
                    target = ((s + section_by) % sections) * places + ((z + z_by) % depth) * 2 + (y ^ flip)
                    pairs.append((source, target))
        return lax.ppermute(block, ("section", "ctx"), pairs)

    tag = jnp.broadcast_to((token_pos[0] // RUN).astype(jnp.bfloat16), (TAG_ROWS, KV_COLUMNS))
    own = jnp.concatenate([keys[0], values[0], tag], axis=0)
    column = [along(own, 1, by, 0) for by in range(depth)]
    query = along(queries[0], 1, 0, 0)
    other = [along(block, 0, 0, 1) for block in column]
    blocks = column + other
    vmem = pl.BlockSpec(memory_space=pltpu.VMEM)
    out = pl.pallas_call(
        functools.partial(attention_kernel, runs),
        out_shape=jax.ShapeDtypeStruct((TOK_DEV, QUERY_HEADS * HEAD_SIZE), jnp.bfloat16),
        in_specs=[pl.BlockSpec(memory_space=pltpu.SMEM)] + [vmem] * (2 + places),
        out_specs=vmem,
        scratch_shapes=[
            pltpu.VMEM((runs, RUN, KV_COLUMNS), jnp.bfloat16),
            pltpu.VMEM((runs, RUN, KV_COLUMNS), jnp.bfloat16),
        ],
        compiler_params=pltpu.CompilerParams(vmem_limit_bytes=40 * 1024 * 1024),
    )(token_pos, segment.reshape(1, -1), query, *blocks)
    return out[None]


def solution(mesh):
    return jax.shard_map(
        per_device,
        mesh=mesh,
        in_specs=(
            P("section", "ctx", None),
            P("section", "ctx", None),
            P("section", "ctx", None),
            P("ctx"),
            P(),
        ),
        out_specs=P("section", "ctx", None),
        check_vma=False,
    )
```

```python
import functools
import math

import jax
import jax.numpy as jnp
from jax import lax
from jax.experimental import pallas as pl
from jax.experimental.pallas import tpu as pltpu
from jax.sharding import PartitionSpec as P

HEAD_SIZE = 128
QUERY_HEADS = 32
KEY_VALUE_HEADS = 4
GROUP = QUERY_HEADS // KEY_VALUE_HEADS
RUN = 64
TOK_DEV = 2 * RUN
KV_COLUMNS = KEY_VALUE_HEADS * HEAD_SIZE

masked_fill = -1e30


def column_slots(depth):
    slots = [[(0, 0, depth)]]
    for step in range(1, depth):
        below, above = (-step, step, depth), (step, 0, depth - step)
        slots.extend([[below], [above]] if 2 * step < depth else [[below, above]])
    return slots


def slot_runs(depth, runs, tags_ref, place_ref):
    place = place_ref[0]
    z, y = lax.div(place, 2), lax.rem(place, 2)
    numbers = []
    for flip in range(2):
        column = jnp.where(flip == 0, y, 1 - y)
        for sources in column_slots(depth):
            first, second = jnp.int32(runs), jnp.int32(runs)
            for by, low, high in sources:
                exists = (z >= low) & (z < high)
                tag = tags_ref[jnp.clip(z + by, 0, depth - 1) * 2 + column]
                first = jnp.where(exists, tag, first)
                second = jnp.where(exists, runs - 1 - tag, second)
            numbers.append((first, second))
    return numbers


def sort_runs(numbers, block_refs, sorted_buf):
    for (first, second), block_ref in zip(numbers, block_refs):
        sorted_buf[first] = block_ref[:RUN, :]
        sorted_buf[second] = block_ref[RUN:, :]


def own_span(half, runs, tags_ref, place_ref):
    tag = tags_ref[place_ref[0]]
    run = tag if half == 0 else runs - 1 - tag
    return run, jnp.maximum(run - runs // 4, 0)


def weights_kernel(runs, depth, tags_ref, place_ref, segment_ref, query_ref, *refs):
    key_refs, (weights_ref, key_buf) = refs[:-2], refs[-2:]
    reach = runs // 4
    span = (reach + 1) * RUN
    sort_runs(slot_runs(depth, runs, tags_ref, place_ref), key_refs, key_buf)
    segment = segment_ref[...].astype(jnp.float32)
    scale = math.log2(math.e) / math.sqrt(HEAD_SIZE)
    for half in range(2):
        run, start = own_span(half, runs, tags_ref, place_ref)
        row_pos = run * RUN + lax.broadcasted_iota(jnp.int32, (RUN, 1), 0)
        at = lax.broadcasted_iota(jnp.int32, (RUN, runs * RUN), 1) == row_pos
        row_doc = jnp.sum(jnp.where(at, segment, 0.0), axis=1, keepdims=True)
        doc_start = jnp.sum(jnp.where(segment < row_doc, 1.0, 0.0), axis=1, keepdims=True).astype(jnp.int32)
        key_pos = start * RUN + lax.broadcasted_iota(jnp.int32, (RUN, span), 1)
        bias = jnp.where((key_pos <= row_pos) & (key_pos >= doc_start), 0.0, masked_fill)
        bias = jnp.concatenate([bias] * GROUP, axis=0)
        for kv in range(KEY_VALUE_HEADS):
            query = jnp.concatenate(
                [
                    query_ref[half * RUN : (half + 1) * RUN, h * HEAD_SIZE : (h + 1) * HEAD_SIZE]
                    for h in range(kv * GROUP, (kv + 1) * GROUP)
                ],
                axis=0,
            )
            key = key_buf[pl.ds(start, reach + 1), :, kv * HEAD_SIZE : (kv + 1) * HEAD_SIZE]
            scores = bias + lax.dot_general(
                query,
                key.reshape(span, HEAD_SIZE),
                (((1,), (1,)), ((), ())),
                preferred_element_type=jnp.float32,
            )
            row_max = jnp.max(scores, axis=1, keepdims=True)
            weights_ref[half * KEY_VALUE_HEADS + kv] = jnp.exp2((scores - row_max) * scale).astype(jnp.bfloat16)


def values_kernel(runs, depth, tags_ref, place_ref, weights_ref, *refs):
    value_refs, (out_ref, value_buf) = refs[:-2], refs[-2:]
    reach = runs // 4
    span = (reach + 1) * RUN
    sort_runs(slot_runs(depth, runs, tags_ref, place_ref), value_refs, value_buf)
    ones = jnp.ones((span, HEAD_SIZE), jnp.bfloat16)
    for half in range(2):
        _, start = own_span(half, runs, tags_ref, place_ref)
        for kv in range(KEY_VALUE_HEADS):
            value = value_buf[pl.ds(start, reach + 1), :, kv * HEAD_SIZE : (kv + 1) * HEAD_SIZE]
            summed = jnp.dot(
                weights_ref[half * KEY_VALUE_HEADS + kv],
                jnp.concatenate([value.reshape(span, HEAD_SIZE), ones], axis=1),
                preferred_element_type=jnp.float32,
            )
            result = (summed[:, :HEAD_SIZE] / summed[:, HEAD_SIZE:]).astype(jnp.bfloat16)
            for i in range(GROUP):
                h = kv * GROUP + i
                out_ref[half * RUN : (half + 1) * RUN, h * HEAD_SIZE : (h + 1) * HEAD_SIZE] = result[
                    i * RUN : (i + 1) * RUN
                ]


def per_device(queries, keys, values, token_pos, segment):
    sections, places = lax.axis_size("section"), lax.axis_size("ctx")
    runs = segment.shape[0] // RUN
    depth = places // 2

    def to_next_section(block):
        return lax.ppermute(block, "section", [(s, (s + 1) % sections) for s in range(sections)])

    def hop(block, moves):
        return lax.ppermute(block, "ctx", [(z * 2 + y, (z + by) * 2 + y) for z, by in moves for y in range(2)])

    def across(block, sources):
        here = [z for z in range(depth) if any(low <= z < high for _, low, high in sources)]
        return lax.ppermute(block, "ctx", [(z * 2 + y, z * 2 + 1 - y) for z in here for y in range(2)])

    def gather(block):
        column = [block]
        up, down, both = block, block, None
        for step in range(1, depth):
            up_moves = [(z, 1) for z in range(step - 1, depth - 1)]
            down_moves = [(z, -1) for z in range(1, depth - step + 1)]
            if both is None:
                up, down = hop(up, up_moves), hop(down, down_moves)
                if 2 * step < depth:
                    column.extend([up, down])
                    continue
                both = up + down
            else:
                both = hop(both, up_moves + down_moves)
            column.append(both)
        return column + [across(b, sources) for b, sources in zip(column, column_slots(depth))]

    all_keys = gather(to_next_section(keys[0]))
    all_values = gather(to_next_section(values[0]))
    query = to_next_section(queries[0])
    place = lax.axis_index("ctx").astype(jnp.int32)
    tags = jnp.where(jnp.arange(places, dtype=jnp.int32) == place, token_pos[0] // RUN, 0)
    bit = 1
    while bit < places:
        tags = tags + lax.ppermute(tags, "ctx", [(i, i ^ bit) for i in range(places)])
        bit *= 2
    place = place.reshape(1)

    smem, vmem = pl.BlockSpec(memory_space=pltpu.SMEM), pl.BlockSpec(memory_space=pltpu.VMEM)
    params = pltpu.CompilerParams(vmem_limit_bytes=40 * 1024 * 1024)
    sorted_buf = pltpu.VMEM((runs + 1, RUN, KV_COLUMNS), jnp.bfloat16)
    weights = pl.pallas_call(
        functools.partial(weights_kernel, runs, depth),
        out_shape=jax.ShapeDtypeStruct((2 * KEY_VALUE_HEADS, GROUP * RUN, (runs // 4 + 1) * RUN), jnp.bfloat16),
        in_specs=[smem, smem] + [vmem] * (2 + len(all_keys)),
        out_specs=vmem,
        scratch_shapes=[sorted_buf],
        compiler_params=params,
    )(tags, place, segment.reshape(1, -1), query, *all_keys)
    out = pl.pallas_call(
        functools.partial(values_kernel, runs, depth),
        out_shape=jax.ShapeDtypeStruct((TOK_DEV, QUERY_HEADS * HEAD_SIZE), jnp.bfloat16),
        in_specs=[smem, smem] + [vmem] * (1 + len(all_values)),
        out_specs=vmem,
        scratch_shapes=[sorted_buf],
        compiler_params=params,
    )(tags, place, weights, *all_values)
    return out[None]


def solution(mesh):
    return jax.shard_map(
        per_device,
        mesh=mesh,
        in_specs=(
            P("section", "ctx", None),
            P("section", "ctx", None),
            P("section", "ctx", None),
            P("ctx"),
            P(),
        ),
        out_specs=P("section", "ctx", None),
        check_vma=False,
    )
```

```python
import functools
import math

import jax
import jax.numpy as jnp
from jax import lax
from jax.experimental import pallas as pl
from jax.experimental.pallas import tpu as pltpu
from jax.sharding import PartitionSpec as P

HEAD_SIZE = 128
QUERY_HEADS = 32
KEY_VALUE_HEADS = 4
GROUP = QUERY_HEADS // KEY_VALUE_HEADS
RUN = 64
TOK_DEV = 2 * RUN
KV_COLUMNS = KEY_VALUE_HEADS * HEAD_SIZE
TAG_ROWS = 16

masked_fill = -1e30


def attention_kernel(runs, pos_ref, segment_ref, query_ref, *refs):
    count = runs // 2
    key_refs, value_refs, (out_ref, key_buf, value_buf) = refs[:count], refs[count:-3], refs[-3:]
    reach = runs // 4
    span = (reach + 1) * RUN
    for key_ref, value_ref in zip(key_refs, value_refs):
        tag = jnp.max(key_ref[TOK_DEV:, :HEAD_SIZE].astype(jnp.float32)).astype(jnp.int32)
        for half, run in enumerate((tag, runs - 1 - tag)):
            key_buf[run] = key_ref[half * RUN : (half + 1) * RUN, :]
            value_buf[run] = value_ref[half * RUN : (half + 1) * RUN, :]

    total_positions = runs * RUN
    segment = segment_ref[...].astype(jnp.float32)
    scale = math.log2(math.e) / math.sqrt(HEAD_SIZE)
    ones = jnp.ones((span, HEAD_SIZE), jnp.bfloat16)
    for half in range(2):
        run = lax.div(pos_ref[half * RUN], RUN)
        start = jnp.maximum(run - reach, 0)
        row_pos = run * RUN + lax.broadcasted_iota(jnp.int32, (RUN, 1), 0)
        at = lax.broadcasted_iota(jnp.int32, (RUN, total_positions), 1) == row_pos
        row_doc = jnp.sum(jnp.where(at, segment, 0.0), axis=1, keepdims=True)
        doc_start = jnp.sum(jnp.where(segment < row_doc, 1.0, 0.0), axis=1, keepdims=True).astype(jnp.int32)
        key_pos = start * RUN + lax.broadcasted_iota(jnp.int32, (RUN, span), 1)
        bias = jnp.where((key_pos <= row_pos) & (key_pos >= doc_start), 0.0, masked_fill)
        bias = jnp.concatenate([bias] * GROUP, axis=0)
        rows = slice(half * RUN, (half + 1) * RUN)
        for kv in range(KEY_VALUE_HEADS):
            columns = slice(kv * HEAD_SIZE, (kv + 1) * HEAD_SIZE)
            heads = [kv * GROUP + i for i in range(GROUP)]
            query = jnp.concatenate(
                [query_ref[rows, h * HEAD_SIZE : (h + 1) * HEAD_SIZE] for h in heads], axis=0
            )
            key = key_buf[pl.ds(start, reach + 1), :, columns].reshape(span, HEAD_SIZE)
            value = value_buf[pl.ds(start, reach + 1), :, columns].reshape(span, HEAD_SIZE)
            scores = bias + lax.dot_general(
                query, key, (((1,), (1,)), ((), ())), preferred_element_type=jnp.float32
            )
            row_max = jnp.max(scores, axis=1, keepdims=True)
            weights = jnp.exp2((scores - row_max) * scale).astype(jnp.bfloat16)
            summed = jnp.dot(
                weights, jnp.concatenate([value, ones], axis=1), preferred_element_type=jnp.float32
            )
            result = (summed[:, :HEAD_SIZE] / summed[:, HEAD_SIZE:]).astype(jnp.bfloat16)
            for i, h in enumerate(heads):
                out_ref[rows, h * HEAD_SIZE : (h + 1) * HEAD_SIZE] = result[i * RUN : (i + 1) * RUN]


def per_device(queries, keys, values, token_pos, segment):
    sections, places = lax.axis_size("section"), lax.axis_size("ctx")
    runs = segment.shape[0] // RUN
    depth = places // 2

    ring = [z * 2 for z in range(depth)] + [z * 2 + 1 for z in reversed(range(depth))]

    def to_next_section(block):
        return lax.ppermute(block, "section", [(s, (s + 1) % sections) for s in range(sections)])

    def turn(block, by):
        return lax.ppermute(block, "ctx", [(ring[i], ring[(i + by) % places]) for i in range(places)])

    def around(block, last_by):
        held = [block]
        ahead, back = block, block
        for _ in range(places // 2 - 1):
            ahead, back = turn(ahead, 1), turn(back, -1)
            held.extend([ahead, back])
        held.append(turn(ahead if last_by == 1 else back, last_by))
        return held

    tag = jnp.broadcast_to((token_pos[0] // RUN).astype(jnp.bfloat16), (TAG_ROWS, KV_COLUMNS))
    value = to_next_section(values[0])
    key = to_next_section(jnp.concatenate([keys[0], tag], axis=0))
    late_queries, key, value = lax.optimization_barrier((queries[0], key, value))
    query = to_next_section(late_queries)
    blocks = around(key, 1) + around(value, -1)
    vmem = pl.BlockSpec(memory_space=pltpu.VMEM)
    out = pl.pallas_call(
        functools.partial(attention_kernel, runs),
        out_shape=jax.ShapeDtypeStruct((TOK_DEV, QUERY_HEADS * HEAD_SIZE), jnp.bfloat16),
        in_specs=[pl.BlockSpec(memory_space=pltpu.SMEM)] + [vmem] * (2 + len(blocks)),
        out_specs=vmem,
        scratch_shapes=[
            pltpu.VMEM((runs, RUN, KV_COLUMNS), jnp.bfloat16),
            pltpu.VMEM((runs, RUN, KV_COLUMNS), jnp.bfloat16),
        ],
        compiler_params=pltpu.CompilerParams(vmem_limit_bytes=40 * 1024 * 1024),
    )(token_pos, segment.reshape(1, -1), query, *blocks)
    return out[None]


def solution(mesh):
    return jax.shard_map(
        per_device,
        mesh=mesh,
        in_specs=(
            P("section", "ctx", None),
            P("section", "ctx", None),
            P("section", "ctx", None),
            P("ctx"),
            P(),
        ),
        out_specs=P("section", "ctx", None),
        check_vma=False,
    )
```

```python
import functools
import math

import jax
import jax.numpy as jnp
from jax import lax
from jax.experimental import pallas as pl
from jax.experimental.pallas import tpu as pltpu
from jax.sharding import PartitionSpec as P

HEAD_SIZE = 128
QUERY_HEADS = 32
KEY_VALUE_HEADS = 4
GROUP = QUERY_HEADS // KEY_VALUE_HEADS
RUN = 64
TOK_DEV = 2 * RUN
KV_COLUMNS = KEY_VALUE_HEADS * HEAD_SIZE
VALUE_ROWS = KEY_VALUE_HEADS * TOK_DEV
TAG_ROWS = 16

masked_fill = -1e30


def pack_kernel(pos_ref, value_ref, out_ref, pos_buf, tag_buf, pos_sem, tag_sem, value_sem):
    pos_copy = pltpu.make_async_copy(pos_ref, pos_buf, pos_sem)
    pos_copy.start()
    value_copies = [
        pltpu.make_async_copy(
            value_ref.at[:, pl.ds(kv * HEAD_SIZE, HEAD_SIZE)],
            out_ref.at[pl.ds(kv * TOK_DEV, TOK_DEV), :],
            value_sem.at[kv],
        )
        for kv in range(KEY_VALUE_HEADS)
    ]
    for copy in value_copies:
        copy.start()
    pos_copy.wait()
    tag = lax.div(pos_buf[0], RUN).astype(jnp.float32)
    tag_buf[...] = jnp.full((TAG_ROWS, HEAD_SIZE), tag).astype(jnp.bfloat16)
    tag_copy = pltpu.make_async_copy(tag_buf, out_ref.at[pl.ds(VALUE_ROWS, TAG_ROWS), :], tag_sem)
    tag_copy.start()
    tag_copy.wait()
    for copy in value_copies:
        copy.wait()


def attention_kernel(runs, pos_ref, segment_ref, query_ref, *refs):
    count = runs // 2
    key_refs, value_refs, (out_ref, key_buf, value_buf) = refs[:count], refs[count:-3], refs[-3:]
    reach = runs // 4
    span = (reach + 1) * RUN
    for key_ref, value_ref in zip(key_refs, value_refs):
        tag = jnp.max(value_ref[VALUE_ROWS:, :].astype(jnp.float32)).astype(jnp.int32)
        for half, run in enumerate((tag, runs - 1 - tag)):
            key_buf[run] = key_ref[half * RUN : (half + 1) * RUN, :]
            for kv in range(KEY_VALUE_HEADS):
                first = kv * TOK_DEV + half * RUN
                value_buf[kv, run] = value_ref[first : first + RUN, :]

    total_positions = runs * RUN
    segment = segment_ref[...].astype(jnp.float32)
    scale = math.log2(math.e) / math.sqrt(HEAD_SIZE)
    ones = jnp.ones((span, HEAD_SIZE), jnp.bfloat16)
    for half in range(2):
        run = lax.div(pos_ref[half * RUN], RUN)
        start = jnp.maximum(run - reach, 0)
        row_pos = run * RUN + lax.broadcasted_iota(jnp.int32, (RUN, 1), 0)
        at = lax.broadcasted_iota(jnp.int32, (RUN, total_positions), 1) == row_pos
        row_doc = jnp.sum(jnp.where(at, segment, 0.0), axis=1, keepdims=True)
        doc_start = jnp.sum(jnp.where(segment < row_doc, 1.0, 0.0), axis=1, keepdims=True).astype(jnp.int32)
        key_pos = start * RUN + lax.broadcasted_iota(jnp.int32, (RUN, span), 1)
        bias = jnp.where((key_pos <= row_pos) & (key_pos >= doc_start), 0.0, masked_fill)
        bias = jnp.concatenate([bias] * GROUP, axis=0)
        rows = slice(half * RUN, (half + 1) * RUN)
        for kv in range(KEY_VALUE_HEADS):
            columns = slice(kv * HEAD_SIZE, (kv + 1) * HEAD_SIZE)
            heads = [kv * GROUP + i for i in range(GROUP)]
            query = jnp.concatenate(
                [query_ref[rows, h * HEAD_SIZE : (h + 1) * HEAD_SIZE] for h in heads], axis=0
            )
            key = key_buf[pl.ds(start, reach + 1), :, columns].reshape(span, HEAD_SIZE)
            value = value_buf[kv, pl.ds(start, reach + 1)].reshape(span, HEAD_SIZE)
            scores = bias + lax.dot_general(
                query, key, (((1,), (1,)), ((), ())), preferred_element_type=jnp.float32
            )
            row_max = jnp.max(scores, axis=1, keepdims=True)
            weights = jnp.exp2((scores - row_max) * scale).astype(jnp.bfloat16)
            summed = jnp.dot(
                weights, jnp.concatenate([value, ones], axis=1), preferred_element_type=jnp.float32
            )
            result = (summed[:, :HEAD_SIZE] / summed[:, HEAD_SIZE:]).astype(jnp.bfloat16)
            for i, h in enumerate(heads):
                out_ref[rows, h * HEAD_SIZE : (h + 1) * HEAD_SIZE] = result[i * RUN : (i + 1) * RUN]


def per_device(queries, keys, values, token_pos, segment):
    sections, places = lax.axis_size("section"), lax.axis_size("ctx")
    runs = segment.shape[0] // RUN
    depth = places // 2

    ring = [z * 2 for z in range(depth)] + [z * 2 + 1 for z in reversed(range(depth))]

    def to_next_section(block):
        return lax.ppermute(block, "section", [(s, (s + 1) % sections) for s in range(sections)])

    def turn(block, by):
        return lax.ppermute(block, "ctx", [(ring[i], ring[(i + by) % places]) for i in range(places)])

    smem, vmem = pl.BlockSpec(memory_space=pltpu.SMEM), pl.BlockSpec(memory_space=pltpu.VMEM)
    anywhere = pl.BlockSpec(memory_space=pl.ANY)
    own_values = pl.pallas_call(
        pack_kernel,
        out_shape=jax.ShapeDtypeStruct((VALUE_ROWS + TAG_ROWS, HEAD_SIZE), jnp.bfloat16),
        in_specs=[anywhere, anywhere],
        out_specs=anywhere,
        scratch_shapes=[
            pltpu.SMEM((TOK_DEV,), jnp.int32),
            pltpu.VMEM((TAG_ROWS, HEAD_SIZE), jnp.bfloat16),
            pltpu.SemaphoreType.DMA,
            pltpu.SemaphoreType.DMA,
            pltpu.SemaphoreType.DMA((KEY_VALUE_HEADS,)),
        ],
        compiler_params=pltpu.CompilerParams(vmem_limit_bytes=60 * 1024 * 1024),
        cost_estimate=pl.CostEstimate(flops=1 << 24, bytes_accessed=1 << 22, transcendentals=0),
    )(token_pos, values[0])
    own_keys, own_values = lax.optimization_barrier((keys[0], own_values))
    key, value, late_queries = lax.optimization_barrier(
        (to_next_section(own_keys), to_next_section(own_values), queries[0])
    )
    query = to_next_section(late_queries)
    key_blocks, value_blocks = [key], [value]
    key_ahead, key_back, value_ahead, value_back = key, key, value, value
    for step in range(1, places // 2):
        key_ahead, key_back = lax.optimization_barrier((turn(key_ahead, 1), turn(key_back, -1)))
        value_ahead, value_back = lax.optimization_barrier((turn(value_ahead, 1), turn(value_back, -1)))
        key_blocks.extend([key_ahead, key_back])
        value_blocks.extend([value_ahead, value_back])
    key_blocks.append(turn(key_ahead, 1))
    value_blocks.append(turn(value_back, -1))
    blocks = key_blocks + value_blocks
    out = pl.pallas_call(
        functools.partial(attention_kernel, runs),
        out_shape=jax.ShapeDtypeStruct((TOK_DEV, QUERY_HEADS * HEAD_SIZE), jnp.bfloat16),
        in_specs=[smem] + [vmem] * (2 + len(blocks)),
        out_specs=vmem,
        scratch_shapes=[
            pltpu.VMEM((runs, RUN, KV_COLUMNS), jnp.bfloat16),
            pltpu.VMEM((KEY_VALUE_HEADS, runs, RUN, HEAD_SIZE), jnp.bfloat16),
        ],
        compiler_params=pltpu.CompilerParams(vmem_limit_bytes=40 * 1024 * 1024),
    )(token_pos, segment.reshape(1, -1), query, *blocks)
    return out[None]


def solution(mesh):
    return jax.shard_map(
        per_device,
        mesh=mesh,
        in_specs=(
            P("section", "ctx", None),
            P("section", "ctx", None),
            P("section", "ctx", None),
            P("ctx"),
            P(),
        ),
        out_specs=P("section", "ctx", None),
        check_vma=False,
    )
```

```python
import functools
import math

import jax
import jax.numpy as jnp
from jax import lax
from jax.experimental import pallas as pl
from jax.experimental.pallas import tpu as pltpu
from jax.sharding import PartitionSpec as P

HEAD_SIZE = 128
QUERY_HEADS = 32
KEY_VALUE_HEADS = 4
GROUP = QUERY_HEADS // KEY_VALUE_HEADS
RUN = 64
TOK_DEV = 2 * RUN
QUERY_COLUMNS = QUERY_HEADS * HEAD_SIZE
KV_COLUMNS = KEY_VALUE_HEADS * HEAD_SIZE
TAG_ROWS = 16

masked_fill = -1e30


def run_numbers(pos_ref, key_refs):
    numbers = [(lax.div(pos_ref[0], RUN), lax.div(pos_ref[RUN], RUN))]
    for key_ref in key_refs[:-2] + key_refs[-1:]:
        tag = jnp.max(key_ref[key_ref.shape[0] - TAG_ROWS :, :TOK_DEV].astype(jnp.float32), axis=0, keepdims=True)
        column = lax.broadcasted_iota(jnp.int32, (1, TOK_DEV), 1)
        first = jnp.max(jnp.where(column < RUN, tag, 0.0)).astype(jnp.int32)
        second = jnp.max(jnp.where(column < RUN, 0.0, tag)).astype(jnp.int32)
        numbers.append((first, second))
    return numbers


def sort_runs(numbers, own_ref, own_column, block_refs, sorted_buf):
    halves = [(ref, ref, RUN) for ref in block_refs[:-2]] + [(block_refs[-2], block_refs[-1], 0)]
    for (first, second), (first_ref, second_ref, at) in zip(numbers[1:], halves):
        sorted_buf[first] = first_ref[:RUN, :]
        sorted_buf[second] = second_ref[at : at + RUN, :]
    for half, number in enumerate(numbers[0]):
        sorted_buf[number] = own_ref[half * RUN : (half + 1) * RUN, own_column : own_column + KV_COLUMNS]


def span_start(own, half, reach):
    return jnp.maximum(own[half] - reach, 0)


def weights_kernel(runs, pos_ref, segment_ref, own_ref, *refs):
    key_refs, (weights_ref, key_buf) = refs[:-2], refs[-2:]
    reach = runs // 4
    span = (reach + 1) * RUN
    numbers = run_numbers(pos_ref, key_refs)
    sort_runs(numbers, own_ref, QUERY_COLUMNS, key_refs, key_buf)
    segment = segment_ref[...].astype(jnp.float32)
    scale = math.log2(math.e) / math.sqrt(HEAD_SIZE)
    for half in range(2):
        start = span_start(numbers[0], half, reach)
        row_pos = numbers[0][half] * RUN + lax.broadcasted_iota(jnp.int32, (RUN, 1), 0)
        at = lax.broadcasted_iota(jnp.int32, (RUN, runs * RUN), 1) == row_pos
        row_doc = jnp.sum(jnp.where(at, segment, 0.0), axis=1, keepdims=True)
        doc_start = jnp.sum(jnp.where(segment < row_doc, 1.0, 0.0), axis=1, keepdims=True).astype(jnp.int32)
        key_pos = start * RUN + lax.broadcasted_iota(jnp.int32, (RUN, span), 1)
        bias = jnp.where((key_pos <= row_pos) & (key_pos >= doc_start), 0.0, masked_fill)
        bias = jnp.concatenate([bias] * GROUP, axis=0)
        for kv in range(KEY_VALUE_HEADS):
            query = jnp.concatenate(
                [
                    own_ref[half * RUN : (half + 1) * RUN, h * HEAD_SIZE : (h + 1) * HEAD_SIZE]
                    for h in range(kv * GROUP, (kv + 1) * GROUP)
                ],
                axis=0,
            )
            key = key_buf[pl.ds(start, reach + 1), :, kv * HEAD_SIZE : (kv + 1) * HEAD_SIZE]
            scores = bias + lax.dot_general(
                query,
                key.reshape(span, HEAD_SIZE),
                (((1,), (1,)), ((), ())),
                preferred_element_type=jnp.float32,
            )
            row_max = jnp.max(scores, axis=1, keepdims=True)
            weights_ref[half * KEY_VALUE_HEADS + kv] = jnp.exp2((scores - row_max) * scale).astype(jnp.bfloat16)


def values_kernel(runs, pos_ref, weights_ref, own_ref, *refs):
    blocks = runs // 2
    key_refs, value_refs, (out_ref, value_buf) = refs[:blocks], refs[blocks:-2], refs[-2:]
    reach = runs // 4
    span = (reach + 1) * RUN
    numbers = run_numbers(pos_ref, key_refs)
    sort_runs(numbers, own_ref, QUERY_COLUMNS + KV_COLUMNS, value_refs, value_buf)
    ones = jnp.ones((span, HEAD_SIZE), jnp.bfloat16)
    for half in range(2):
        start = span_start(numbers[0], half, reach)
        for kv in range(KEY_VALUE_HEADS):
            value = value_buf[pl.ds(start, reach + 1), :, kv * HEAD_SIZE : (kv + 1) * HEAD_SIZE]
            summed = jnp.dot(
                weights_ref[half * KEY_VALUE_HEADS + kv],
                jnp.concatenate([value.reshape(span, HEAD_SIZE), ones], axis=1),
                preferred_element_type=jnp.float32,
            )
            result = (summed[:, :HEAD_SIZE] / summed[:, HEAD_SIZE:]).astype(jnp.bfloat16)
            for i in range(GROUP):
                h = kv * GROUP + i
                out_ref[half * RUN : (half + 1) * RUN, h * HEAD_SIZE : (h + 1) * HEAD_SIZE] = result[
                    i * RUN : (i + 1) * RUN
                ]


def per_device(queries, keys, values, token_pos, segment):
    sections, places = lax.axis_size("section"), lax.axis_size("ctx")
    runs = segment.shape[0] // RUN
    depth = places // 2
    ring = [z * 2 for z in range(depth)] + [z * 2 + 1 for z in reversed(range(depth))]

    def shift(block, section_by, ring_by):
        pairs = []
        for s in range(sections):
            for i in range(places):
                target = (s + section_by) % sections * places + ring[(i + ring_by) % places]
                pairs.append((s * places + ring[i], target))
        return lax.ppermute(block, ("section", "ctx"), pairs)

    def around(block):
        ahead, back = shift(block, 1, 1), shift(block, 1, -1)
        held = [ahead, back]
        for _ in range(2, places // 2):
            ahead, back = shift(ahead, 0, 1), shift(back, 0, -1)
            held.extend([ahead, back])
        return held + [shift(ahead[:RUN], 0, 1), shift(back[RUN:], 0, -1)]

    tag = jnp.tile((token_pos >> (RUN.bit_length() - 1)).astype(jnp.bfloat16)[None], (TAG_ROWS, KEY_VALUE_HEADS))
    all_keys = around(jnp.concatenate([keys[0], tag], axis=0))
    all_values = around(values[0])
    own = shift(jnp.concatenate([queries[0], keys[0], values[0]], axis=1), 1, 0)

    smem, vmem = pl.BlockSpec(memory_space=pltpu.SMEM), pl.BlockSpec(memory_space=pltpu.VMEM)
    params = pltpu.CompilerParams(vmem_limit_bytes=40 * 1024 * 1024)
    sorted_buf = pltpu.VMEM((runs, RUN, KV_COLUMNS), jnp.bfloat16)
    weights = pl.pallas_call(
        functools.partial(weights_kernel, runs),
        out_shape=jax.ShapeDtypeStruct((2 * KEY_VALUE_HEADS, GROUP * RUN, (runs // 4 + 1) * RUN), jnp.bfloat16),
        in_specs=[smem] + [vmem] * (2 + len(all_keys)),
        out_specs=vmem,
        scratch_shapes=[sorted_buf],
        compiler_params=params,
        cost_estimate=pl.CostEstimate(flops=1 << 26, bytes_accessed=1 << 20, transcendentals=0),
    )(token_pos, segment.reshape(1, -1), own, *all_keys)
    out = pl.pallas_call(
        functools.partial(values_kernel, runs),
        out_shape=jax.ShapeDtypeStruct((TOK_DEV, QUERY_COLUMNS), jnp.bfloat16),
        in_specs=[smem] + [vmem] * (2 + len(all_keys) + len(all_values)),
        out_specs=vmem,
        scratch_shapes=[sorted_buf],
        compiler_params=params,
        cost_estimate=pl.CostEstimate(flops=1 << 26, bytes_accessed=1 << 20, transcendentals=0),
    )(token_pos, weights, own, *all_keys, *all_values)
    return out[None]


def solution(mesh):
    return jax.shard_map(
        per_device,
        mesh=mesh,
        in_specs=(
            P("section", "ctx", None),
            P("section", "ctx", None),
            P("section", "ctx", None),
            P("ctx"),
            P(),
        ),
        out_specs=P("section", "ctx", None),
        check_vma=False,
    )
```

```python
import functools
import math

import jax
import jax.numpy as jnp
from jax import lax
from jax.experimental import pallas as pl
from jax.experimental.pallas import tpu as pltpu
from jax.sharding import PartitionSpec as P

HEAD_SIZE = 128
QUERY_HEADS = 32
KEY_VALUE_HEADS = 4
GROUP = QUERY_HEADS // KEY_VALUE_HEADS
RUN = 64
TOK_DEV = 2 * RUN
QUERY_COLUMNS = QUERY_HEADS * HEAD_SIZE
KV_COLUMNS = KEY_VALUE_HEADS * HEAD_SIZE
TAG_ROWS = 16

masked_fill = -1e30


def run_numbers(pos_ref, key_refs):
    numbers = [(lax.div(pos_ref[0], RUN), lax.div(pos_ref[RUN], RUN))]
    for key_ref in key_refs[:-2] + key_refs[-1:]:
        tag = jnp.max(key_ref[key_ref.shape[0] - TAG_ROWS :, :TOK_DEV].astype(jnp.float32), axis=0, keepdims=True)
        column = lax.broadcasted_iota(jnp.int32, (1, TOK_DEV), 1)
        first = jnp.max(jnp.where(column < RUN, tag, 0.0)).astype(jnp.int32)
        second = jnp.max(jnp.where(column < RUN, 0.0, tag)).astype(jnp.int32)
        numbers.append((first, second))
    return numbers


def sort_runs(numbers, own_ref, own_column, block_refs, sorted_buf):
    halves = [(ref, ref, RUN) for ref in block_refs[:-2]] + [(block_refs[-2], block_refs[-1], 0)]
    for (first, second), (first_ref, second_ref, at) in zip(numbers[1:], halves):
        sorted_buf[first] = first_ref[:RUN, :]
        sorted_buf[second] = second_ref[at : at + RUN, :]
    for half, number in enumerate(numbers[0]):
        sorted_buf[number] = own_ref[half * RUN : (half + 1) * RUN, own_column : own_column + KV_COLUMNS]


def span_start(own, half, reach):
    return jnp.maximum(own[half] - reach, 0)


def weights_kernel(runs, pos_ref, segment_ref, own_ref, *refs):
    key_refs, (weights_ref, key_buf) = refs[:-2], refs[-2:]
    reach = runs // 4
    span = (reach + 1) * RUN
    numbers = run_numbers(pos_ref, key_refs)
    sort_runs(numbers, own_ref, QUERY_COLUMNS, key_refs, key_buf)
    segment = segment_ref[...].astype(jnp.float32)
    scale = math.log2(math.e) / math.sqrt(HEAD_SIZE)
    for half in range(2):
        start = span_start(numbers[0], half, reach)
        row_pos = numbers[0][half] * RUN + lax.broadcasted_iota(jnp.int32, (RUN, 1), 0)
        at = lax.broadcasted_iota(jnp.int32, (RUN, runs * RUN), 1) == row_pos
        row_doc = jnp.sum(jnp.where(at, segment, 0.0), axis=1, keepdims=True)
        doc_start = jnp.sum(jnp.where(segment < row_doc, 1.0, 0.0), axis=1, keepdims=True).astype(jnp.int32)
        key_pos = start * RUN + lax.broadcasted_iota(jnp.int32, (RUN, span), 1)
        bias = jnp.where((key_pos <= row_pos) & (key_pos >= doc_start), 0.0, masked_fill)
        bias = jnp.concatenate([bias] * GROUP, axis=0)
        for kv in range(KEY_VALUE_HEADS):
            query = jnp.concatenate(
                [
                    own_ref[half * RUN : (half + 1) * RUN, h * HEAD_SIZE : (h + 1) * HEAD_SIZE]
                    for h in range(kv * GROUP, (kv + 1) * GROUP)
                ],
                axis=0,
            )
            key = key_buf[pl.ds(start, reach + 1), :, kv * HEAD_SIZE : (kv + 1) * HEAD_SIZE]
            scores = bias + lax.dot_general(
                query,
                key.reshape(span, HEAD_SIZE),
                (((1,), (1,)), ((), ())),
                preferred_element_type=jnp.float32,
            )
            row_max = jnp.max(scores, axis=1, keepdims=True)
            weights_ref[half * KEY_VALUE_HEADS + kv] = jnp.exp2((scores - row_max) * scale).astype(jnp.bfloat16)


def values_kernel(runs, pos_ref, weights_ref, own_ref, *refs):
    blocks = runs // 2
    key_refs, value_refs, (out_ref, value_buf) = refs[:blocks], refs[blocks:-2], refs[-2:]
    reach = runs // 4
    span = (reach + 1) * RUN
    numbers = run_numbers(pos_ref, key_refs)
    sort_runs(numbers, own_ref, QUERY_COLUMNS + KV_COLUMNS, value_refs, value_buf)
    ones = jnp.ones((span, HEAD_SIZE), jnp.bfloat16)
    for half in range(2):
        start = span_start(numbers[0], half, reach)
        for kv in range(KEY_VALUE_HEADS):
            value = value_buf[pl.ds(start, reach + 1), :, kv * HEAD_SIZE : (kv + 1) * HEAD_SIZE]
            summed = jnp.dot(
                weights_ref[half * KEY_VALUE_HEADS + kv],
                jnp.concatenate([value.reshape(span, HEAD_SIZE), ones], axis=1),
                preferred_element_type=jnp.float32,
            )
            result = (summed[:, :HEAD_SIZE] / summed[:, HEAD_SIZE:]).astype(jnp.bfloat16)
            for i in range(GROUP):
                h = kv * GROUP + i
                out_ref[half * RUN : (half + 1) * RUN, h * HEAD_SIZE : (h + 1) * HEAD_SIZE] = result[
                    i * RUN : (i + 1) * RUN
                ]


def per_device(queries, keys, values, token_pos, segment):
    sections, places = lax.axis_size("section"), lax.axis_size("ctx")
    runs = segment.shape[0] // RUN
    depth = places // 2
    ring = [z * 2 for z in range(depth)] + [z * 2 + 1 for z in reversed(range(depth))]

    def shift(block, section_by, ring_by):
        pairs = []
        for s in range(sections):
            for i in range(places):
                target = (s + section_by) % sections * places + ring[(i + ring_by) % places]
                pairs.append((s * places + ring[i], target))
        return lax.ppermute(block, ("section", "ctx"), pairs)

    def around(block):
        ahead, back = shift(block, 1, 1), shift(block, 1, -1)
        held = [ahead, back]
        for _ in range(2, places // 2):
            ahead, back = shift(ahead, 0, 1), shift(back, 0, -1)
            held.extend([ahead, back])
        return held + [shift(ahead[:RUN], 0, 1), shift(back[RUN:], 0, -1)]

    tag = jnp.tile((token_pos >> (RUN.bit_length() - 1)).astype(jnp.bfloat16)[None], (TAG_ROWS, KEY_VALUE_HEADS))
    all_keys = around(jnp.concatenate([keys[0], tag], axis=0))
    all_values = around(values[0])

    own = jnp.concatenate([queries[0], keys[0], values[0]], axis=1)
    own = shift(lax.optimization_barrier((own, *all_keys[:2], *all_values[:2]))[0], 1, 0)

    smem, vmem = pl.BlockSpec(memory_space=pltpu.SMEM), pl.BlockSpec(memory_space=pltpu.VMEM)
    params = pltpu.CompilerParams(vmem_limit_bytes=40 * 1024 * 1024)
    sorted_buf = pltpu.VMEM((runs, RUN, KV_COLUMNS), jnp.bfloat16)
    weights = pl.pallas_call(
        functools.partial(weights_kernel, runs),
        out_shape=jax.ShapeDtypeStruct((2 * KEY_VALUE_HEADS, GROUP * RUN, (runs // 4 + 1) * RUN), jnp.bfloat16),
        in_specs=[smem] + [vmem] * (2 + len(all_keys)),
        out_specs=vmem,
        scratch_shapes=[sorted_buf],
        compiler_params=params,
        cost_estimate=pl.CostEstimate(flops=1 << 26, bytes_accessed=1 << 20, transcendentals=0),
    )(token_pos, segment.reshape(1, -1), own, *all_keys)
    out = pl.pallas_call(
        functools.partial(values_kernel, runs),
        out_shape=jax.ShapeDtypeStruct((TOK_DEV, QUERY_COLUMNS), jnp.bfloat16),
        in_specs=[smem] + [vmem] * (2 + len(all_keys) + len(all_values)),
        out_specs=vmem,
        scratch_shapes=[sorted_buf],
        compiler_params=params,
        cost_estimate=pl.CostEstimate(flops=1 << 26, bytes_accessed=1 << 20, transcendentals=0),
    )(token_pos, weights, own, *all_keys, *all_values)
    return out[None]


def solution(mesh):
    return jax.shard_map(
        per_device,
        mesh=mesh,
        in_specs=(
            P("section", "ctx", None),
            P("section", "ctx", None),
            P("section", "ctx", None),
            P("ctx"),
            P(),
        ),
        out_specs=P("section", "ctx", None),
        check_vma=False,
    )
```

```python
import functools
import math

import jax
import jax.numpy as jnp
from jax import lax
from jax.experimental import pallas as pl
from jax.experimental.pallas import tpu as pltpu
from jax.sharding import PartitionSpec as P

HEAD_SIZE = 128
QUERY_HEADS = 32
KEY_VALUE_HEADS = 4
GROUP = QUERY_HEADS // KEY_VALUE_HEADS
RUN = 64
TOK_DEV = 2 * RUN
QUERY_COLUMNS = QUERY_HEADS * HEAD_SIZE
KV_COLUMNS = KEY_VALUE_HEADS * HEAD_SIZE
TAG_ROWS = 16

masked_fill = -1e30


def run_numbers(pos_ref, key_refs):
    numbers = [(lax.div(pos_ref[0], RUN), lax.div(pos_ref[RUN], RUN))]
    for key_ref in key_refs[:-2] + key_refs[-1:]:
        tag = jnp.max(key_ref[key_ref.shape[0] - TAG_ROWS :, :TOK_DEV].astype(jnp.float32), axis=0, keepdims=True)
        column = lax.broadcasted_iota(jnp.int32, (1, TOK_DEV), 1)
        first = jnp.max(jnp.where(column < RUN, tag, 0.0)).astype(jnp.int32)
        second = jnp.max(jnp.where(column < RUN, 0.0, tag)).astype(jnp.int32)
        numbers.append((first, second))
    return numbers


def sort_runs(numbers, own_ref, own_column, block_refs, sorted_buf):
    halves = [(ref, ref, RUN) for ref in block_refs[:-2]] + [(block_refs[-2], block_refs[-1], 0)]
    for (first, second), (first_ref, second_ref, at) in zip(numbers[1:], halves):
        sorted_buf[first] = first_ref[:RUN, :]
        sorted_buf[second] = second_ref[at : at + RUN, :]
    for half, number in enumerate(numbers[0]):
        sorted_buf[number] = own_ref[half * RUN : (half + 1) * RUN, own_column : own_column + KV_COLUMNS]


def span_start(own, half, reach):
    return jnp.maximum(own[half] - reach, 0)


def bias_kernel(runs, pos_ref, segment_ref, bias_ref):
    reach = runs // 4
    segment = segment_ref[...].astype(jnp.float32)
    for half in range(2):
        run = lax.div(pos_ref[half * RUN], RUN)
        row_pos = run * RUN + lax.broadcasted_iota(jnp.int32, (RUN, 1), 0)
        at = lax.broadcasted_iota(jnp.int32, (RUN, runs * RUN), 1) == row_pos
        row_doc = jnp.sum(jnp.where(at, segment, 0.0), axis=1, keepdims=True)
        doc_start = jnp.sum(jnp.where(segment < row_doc, 1.0, 0.0), axis=1, keepdims=True).astype(jnp.int32)
        key_pos = jnp.maximum(run - reach, 0) * RUN + lax.broadcasted_iota(jnp.int32, bias_ref.shape[1:], 1)
        bias_ref[half] = jnp.where((key_pos <= row_pos) & (key_pos >= doc_start), 0.0, masked_fill)


def weights_kernel(runs, pos_ref, bias_ref, own_ref, *refs):
    key_refs, (weights_ref, key_buf) = refs[:-2], refs[-2:]
    reach = runs // 4
    span = (reach + 1) * RUN
    numbers = run_numbers(pos_ref, key_refs)
    sort_runs(numbers, own_ref, QUERY_COLUMNS, key_refs, key_buf)
    scale = math.log2(math.e) / math.sqrt(HEAD_SIZE)
    for half in range(2):
        start = span_start(numbers[0], half, reach)
        bias = jnp.concatenate([bias_ref[half]] * GROUP, axis=0)
        for kv in range(KEY_VALUE_HEADS):
            query = jnp.concatenate(
                [
                    own_ref[half * RUN : (half + 1) * RUN, h * HEAD_SIZE : (h + 1) * HEAD_SIZE]
                    for h in range(kv * GROUP, (kv + 1) * GROUP)
                ],
                axis=0,
            )
            key = key_buf[pl.ds(start, reach + 1), :, kv * HEAD_SIZE : (kv + 1) * HEAD_SIZE]
            scores = bias + lax.dot_general(
                query,
                key.reshape(span, HEAD_SIZE),
                (((1,), (1,)), ((), ())),
                preferred_element_type=jnp.float32,
            )
            row_max = jnp.max(scores, axis=1, keepdims=True)
            weights_ref[half * KEY_VALUE_HEADS + kv] = jnp.exp2((scores - row_max) * scale).astype(jnp.bfloat16)


def values_kernel(runs, pos_ref, weights_ref, own_ref, *refs):
    blocks = runs // 2
    key_refs, value_refs, (out_ref, value_buf) = refs[:blocks], refs[blocks:-2], refs[-2:]
    reach = runs // 4
    span = (reach + 1) * RUN
    numbers = run_numbers(pos_ref, key_refs)
    sort_runs(numbers, own_ref, QUERY_COLUMNS + KV_COLUMNS, value_refs, value_buf)
    ones = jnp.ones((span, HEAD_SIZE), jnp.bfloat16)
    for half in range(2):
        start = span_start(numbers[0], half, reach)
        for kv in range(KEY_VALUE_HEADS):
            value = value_buf[pl.ds(start, reach + 1), :, kv * HEAD_SIZE : (kv + 1) * HEAD_SIZE]
            summed = jnp.dot(
                weights_ref[half * KEY_VALUE_HEADS + kv],
                jnp.concatenate([value.reshape(span, HEAD_SIZE), ones], axis=1),
                preferred_element_type=jnp.float32,
            )
            result = (summed[:, :HEAD_SIZE] / summed[:, HEAD_SIZE:]).astype(jnp.bfloat16)
            for i in range(GROUP):
                h = kv * GROUP + i
                out_ref[half * RUN : (half + 1) * RUN, h * HEAD_SIZE : (h + 1) * HEAD_SIZE] = result[
                    i * RUN : (i + 1) * RUN
                ]


def per_device(queries, keys, values, token_pos, segment):
    sections, places = lax.axis_size("section"), lax.axis_size("ctx")
    runs = segment.shape[0] // RUN
    depth = places // 2
    ring = [z * 2 for z in range(depth)] + [z * 2 + 1 for z in reversed(range(depth))]

    def shift(block, section_by, ring_by):
        pairs = []
        for s in range(sections):
            for i in range(places):
                target = (s + section_by) % sections * places + ring[(i + ring_by) % places]
                pairs.append((s * places + ring[i], target))
        return lax.ppermute(block, ("section", "ctx"), pairs)

    def around(block):
        ahead, back = shift(block, 1, 1), shift(block, 1, -1)
        held = [ahead, back]
        for _ in range(2, places // 2):
            ahead, back = shift(ahead, 0, 1), shift(back, 0, -1)
            held.extend([ahead, back])
        return held + [shift(ahead[:RUN], 0, 1), shift(back[RUN:], 0, -1)]

    tag = jnp.tile((token_pos >> (RUN.bit_length() - 1)).astype(jnp.bfloat16)[None], (TAG_ROWS, KEY_VALUE_HEADS))
    all_keys = around(jnp.concatenate([keys[0], tag], axis=0))
    all_values = around(values[0])

    own = shift(jnp.concatenate([queries[0], keys[0], values[0]], axis=1), 1, 0)
    late_segment, _, _ = lax.optimization_barrier((segment, all_keys[-2:], all_values[-4:-2]))

    smem, vmem = pl.BlockSpec(memory_space=pltpu.SMEM), pl.BlockSpec(memory_space=pltpu.VMEM)
    params = pltpu.CompilerParams(vmem_limit_bytes=40 * 1024 * 1024)
    sorted_buf = pltpu.VMEM((runs, RUN, KV_COLUMNS), jnp.bfloat16)
    bias = pl.pallas_call(
        functools.partial(bias_kernel, runs),
        out_shape=jax.ShapeDtypeStruct((2, RUN, (runs // 4 + 1) * RUN), jnp.float32),
        in_specs=[smem, vmem],
        out_specs=vmem,
        cost_estimate=pl.CostEstimate(flops=10<<30, bytes_accessed=0, transcendentals=0),
    )(token_pos, late_segment.reshape(1, -1))
    weights = pl.pallas_call(
        functools.partial(weights_kernel, runs),
        out_shape=jax.ShapeDtypeStruct((2 * KEY_VALUE_HEADS, GROUP * RUN, (runs // 4 + 1) * RUN), jnp.bfloat16),
        in_specs=[smem] + [vmem] * (2 + len(all_keys)),
        out_specs=vmem,
        scratch_shapes=[sorted_buf],
        compiler_params=params,
        cost_estimate=pl.CostEstimate(flops=1 << 26, bytes_accessed=1 << 20, transcendentals=0),
    )(token_pos, bias, own, *all_keys)
    out = pl.pallas_call(
        functools.partial(values_kernel, runs),
        out_shape=jax.ShapeDtypeStruct((TOK_DEV, QUERY_COLUMNS), jnp.bfloat16),
        in_specs=[smem] + [vmem] * (2 + len(all_keys) + len(all_values)),
        out_specs=vmem,
        scratch_shapes=[sorted_buf],
        compiler_params=params,
        cost_estimate=pl.CostEstimate(flops=1 << 26, bytes_accessed=1 << 20, transcendentals=0),
    )(token_pos, weights, own, *all_keys, *all_values)
    return out[None]


def solution(mesh):
    return jax.shard_map(
        per_device,
        mesh=mesh,
        in_specs=(
            P("section", "ctx", None),
            P("section", "ctx", None),
            P("section", "ctx", None),
            P("ctx"),
            P(),
        ),
        out_specs=P("section", "ctx", None),
        check_vma=False,
    )
```

```python
import functools
import math

import jax
import jax.numpy as jnp
from jax import lax
from jax.experimental import pallas as pl
from jax.experimental.pallas import tpu as pltpu
from jax.sharding import PartitionSpec as P

HEAD_SIZE = 128
QUERY_HEADS = 32
KEY_VALUE_HEADS = 4
GROUP = QUERY_HEADS // KEY_VALUE_HEADS
RUN = 64
TOK_DEV = 2 * RUN
QUERY_COLUMNS = QUERY_HEADS * HEAD_SIZE
KV_COLUMNS = KEY_VALUE_HEADS * HEAD_SIZE
TAG_ROWS = 16

masked_fill = -1e30


def first_run(pos):
    return jnp.min(pos.astype(jnp.float32)).astype(jnp.int32) // RUN


def run_numbers(runs, pos_ref, tagged_refs):
    firsts = [first_run(pos_ref[...])]
    for ref in tagged_refs:
        firsts.append(jnp.max(ref[TOK_DEV:, :HEAD_SIZE].astype(jnp.float32)).astype(jnp.int32))
    places = runs // 2
    firsts.append(places * (places - 1) // 2 - sum(firsts))
    return [(first, runs - 1 - first) for first in firsts]


def sort_runs(numbers, own_ref, own_column, block_refs, sorted_buf):
    for half, number in enumerate(numbers[0]):
        sorted_buf[number] = own_ref[half * RUN : (half + 1) * RUN, own_column : own_column + KV_COLUMNS]
    halves = [(ref, ref, RUN) for ref in block_refs[:-2]] + [(block_refs[-2], block_refs[-1], 0)]
    for (first, second), (first_ref, second_ref, at) in zip(numbers[1:], halves):
        sorted_buf[first] = first_ref[:RUN, :]
        sorted_buf[second] = second_ref[at : at + RUN, :]


def bias_kernel(runs, pos_ref, segment_ref, bias_ref):
    reach = runs // 4
    segment = segment_ref[...].astype(jnp.float32)
    first = first_run(pos_ref[...])
    for half, run in enumerate((first, runs - 1 - first)):
        row_pos = run * RUN + lax.broadcasted_iota(jnp.int32, (RUN, 1), 0)
        at = lax.broadcasted_iota(jnp.int32, (RUN, runs * RUN), 1) == row_pos
        row_doc = jnp.sum(jnp.where(at, segment, 0.0), axis=1, keepdims=True)
        doc_start = jnp.sum(jnp.where(segment < row_doc, 1.0, 0.0), axis=1, keepdims=True).astype(jnp.int32)
        key_pos = jnp.maximum(run - reach, 0) * RUN + lax.broadcasted_iota(jnp.int32, bias_ref.shape[1:], 1)
        bias_ref[half] = jnp.where((key_pos <= row_pos) & (key_pos >= doc_start), 0.0, masked_fill)


def weights_kernel(runs, pos_ref, bias_ref, own_ref, *refs):
    blocks = runs // 2
    key_refs, tagged_refs, (weights_ref, key_buf) = refs[:blocks], refs[blocks:-2], refs[-2:]
    reach = runs // 4
    span = (reach + 1) * RUN
    numbers = run_numbers(runs, pos_ref, tagged_refs)
    sort_runs(numbers, own_ref, QUERY_COLUMNS, key_refs, key_buf)
    scale = math.log2(math.e) / math.sqrt(HEAD_SIZE)
    for half in range(2):
        start = jnp.maximum(numbers[0][half] - reach, 0)
        bias = jnp.concatenate([bias_ref[half]] * GROUP, axis=0)
        for kv in range(KEY_VALUE_HEADS):
            query = jnp.concatenate(
                [
                    own_ref[half * RUN : (half + 1) * RUN, h * HEAD_SIZE : (h + 1) * HEAD_SIZE]
                    for h in range(kv * GROUP, (kv + 1) * GROUP)
                ],
                axis=0,
            )
            key = key_buf[pl.ds(start, reach + 1), :, kv * HEAD_SIZE : (kv + 1) * HEAD_SIZE]
            scores = bias + lax.dot_general(
                query,
                key.reshape(span, HEAD_SIZE),
                (((1,), (1,)), ((), ())),
                preferred_element_type=jnp.float32,
            )
            row_max = jnp.max(scores, axis=1, keepdims=True)
            weights_ref[half * KEY_VALUE_HEADS + kv] = jnp.exp2((scores - row_max) * scale).astype(jnp.bfloat16)


def values_kernel(runs, pos_ref, weights_ref, own_ref, *refs):
    value_refs, (out_ref, value_buf, result_buf, out_sems) = refs[:-4], refs[-4:]
    reach = runs // 4
    span = (reach + 1) * RUN
    numbers = run_numbers(runs, pos_ref, value_refs[:-2])
    sort_runs(numbers, own_ref, QUERY_COLUMNS + KV_COLUMNS, value_refs, value_buf)
    ones = jnp.ones((span, HEAD_SIZE), jnp.bfloat16)
    copies = []
    for half in range(2):
        start = jnp.maximum(numbers[0][half] - reach, 0)
        for kv in range(KEY_VALUE_HEADS):
            value = value_buf[pl.ds(start, reach + 1), :, kv * HEAD_SIZE : (kv + 1) * HEAD_SIZE]
            summed = jnp.dot(
                weights_ref[half * KEY_VALUE_HEADS + kv],
                jnp.concatenate([value.reshape(span, HEAD_SIZE), ones], axis=1),
                preferred_element_type=jnp.float32,
            )
            result = (summed[:, :HEAD_SIZE] / summed[:, HEAD_SIZE:]).astype(jnp.bfloat16)
            for i in range(GROUP):
                h = kv * GROUP + i
                result_buf[half, :, h * HEAD_SIZE : (h + 1) * HEAD_SIZE] = result[i * RUN : (i + 1) * RUN]
        copies.append(
            pltpu.make_async_copy(result_buf.at[half], out_ref.at[pl.ds(half * RUN, RUN), :], out_sems.at[half])
        )
        copies[-1].start()
    for copy in copies:
        copy.wait()


def per_device(queries, keys, values, token_pos, segment):
    sections, places = lax.axis_size("section"), lax.axis_size("ctx")
    runs = segment.shape[0] // RUN
    depth = places // 2
    ring = [z * 2 for z in range(depth)] + [z * 2 + 1 for z in reversed(range(depth))]

    def shift(block, section_by, ring_by):
        pairs = []
        for s in range(sections):
            for i in range(places):
                target = (s + section_by) % sections * places + ring[(i + ring_by) % places]
                pairs.append((s * places + ring[i], target))
        return lax.ppermute(block, ("section", "ctx"), pairs)

    own = jnp.concatenate([queries[0], keys[0], values[0]], axis=1)

    def around(block, early=None):
        ahead, back = shift(block, 1, 1), shift(block, 1, -1)
        held = [ahead, back]
        if early is not None:
            ahead, early = lax.optimization_barrier((ahead, early))
        for _ in range(2, places // 2):
            ahead, back = shift(ahead, 0, 1), shift(back, 0, -1)
            held.extend([ahead, back])
        return held + [shift(ahead[:RUN], 0, 1), shift(back[RUN:TOK_DEV], 0, -1)], early

    first = jnp.broadcast_to((token_pos[:TOK_DEV] >> (RUN.bit_length() - 1))[:1], (KV_COLUMNS,))
    tag = jnp.broadcast_to(first.astype(jnp.bfloat16)[None], (TAG_ROWS, KV_COLUMNS))
    all_keys, own = around(keys[0], own)
    all_values, _ = around(jnp.concatenate([values[0], tag], axis=0))
    own = shift(own, 1, 0)
    late_segment, _, _ = lax.optimization_barrier((segment, all_keys[-2:], all_values[:2]))

    pos = token_pos.reshape(1, -1)
    vmem = pl.BlockSpec(memory_space=pltpu.VMEM)
    params = pltpu.CompilerParams(vmem_limit_bytes=40 * 1024 * 1024)
    sorted_buf = pltpu.VMEM((runs, RUN, KV_COLUMNS), jnp.bfloat16)
    bias = pl.pallas_call(
        functools.partial(bias_kernel, runs),
        out_shape=jax.ShapeDtypeStruct((2, RUN, (runs // 4 + 1) * RUN), jnp.float32),
        in_specs=[vmem] * 2,
        out_specs=vmem,
        cost_estimate=pl.CostEstimate(flops=10 << 30, bytes_accessed=0, transcendentals=0),
    )(pos, late_segment.reshape(1, -1))
    weights = pl.pallas_call(
        functools.partial(weights_kernel, runs),
        out_shape=jax.ShapeDtypeStruct((2 * KEY_VALUE_HEADS, GROUP * RUN, (runs // 4 + 1) * RUN), jnp.bfloat16),
        in_specs=[vmem] * (3 + len(all_keys) + len(all_values[:-2])),
        out_specs=vmem,
        scratch_shapes=[sorted_buf],
        compiler_params=params,
        cost_estimate=pl.CostEstimate(flops=1 << 26, bytes_accessed=1 << 20, transcendentals=0),
    )(pos, bias, own, *all_keys, *all_values[:-2])
    out = pl.pallas_call(
        functools.partial(values_kernel, runs),
        out_shape=jax.ShapeDtypeStruct((TOK_DEV, QUERY_COLUMNS), jnp.bfloat16),
        in_specs=[vmem] * (3 + len(all_values)),
        out_specs=pl.BlockSpec(memory_space=pl.ANY),
        scratch_shapes=[
            sorted_buf,
            pltpu.VMEM((2, RUN, QUERY_COLUMNS), jnp.bfloat16),
            pltpu.SemaphoreType.DMA((2,)),
        ],
        compiler_params=params,
        cost_estimate=pl.CostEstimate(flops=1 << 26, bytes_accessed=1 << 20, transcendentals=0),
    )(pos, weights, own, *all_values)
    return out[None]


def solution(mesh):
    return jax.shard_map(
        per_device,
        mesh=mesh,
        in_specs=(
            P("section", "ctx", None),
            P("section", "ctx", None),
            P("section", "ctx", None),
            P("ctx"),
            P(),
        ),
        out_specs=P("section", "ctx", None),
        check_vma=False,
    )
```

```python
import functools
import math

import jax
import jax.numpy as jnp
from jax import lax
from jax.experimental import pallas as pl
from jax.experimental.pallas import tpu as pltpu
from jax.sharding import PartitionSpec as P

HEAD_SIZE = 128
QUERY_HEADS = 32
KEY_VALUE_HEADS = 4
GROUP = QUERY_HEADS // KEY_VALUE_HEADS
RUN = 64
TOK_DEV = 2 * RUN
QUERY_COLUMNS = QUERY_HEADS * HEAD_SIZE
KV_COLUMNS = KEY_VALUE_HEADS * HEAD_SIZE
TAG_ROWS = 16

masked_fill = -1e30


def first_run(pos_ref):
    return lax.div(jnp.min(pos_ref[:, :TOK_DEV]).astype(jnp.int32), RUN)


def run_numbers(runs, pos_ref, tagged_refs):
    firsts = [first_run(pos_ref)]
    for ref in tagged_refs:
        firsts.append(jnp.max(ref[TOK_DEV:, :HEAD_SIZE].astype(jnp.float32)).astype(jnp.int32))
    places = runs // 2
    firsts.append(places * (places - 1) // 2 - sum(firsts))
    return [(first, runs - 1 - first) for first in firsts]


def sort_runs(numbers, own_ref, own_column, block_refs, sorted_buf):
    for half, number in enumerate(numbers[0]):
        sorted_buf[number] = own_ref[half * RUN : (half + 1) * RUN, own_column : own_column + KV_COLUMNS]
    halves = [(ref, ref, RUN) for ref in block_refs[:-2]] + [(block_refs[-2], block_refs[-1], 0)]
    for (first, second), (first_ref, second_ref, at) in zip(numbers[1:], halves):
        sorted_buf[first] = first_ref[:RUN, :]
        sorted_buf[second] = second_ref[at : at + RUN, :]


def bias_kernel(runs, pos_ref, *refs):
    bias_ref = refs[-1]
    reach = runs // 4
    segment = pos_ref[:, TOK_DEV:]
    first = first_run(pos_ref)
    for half, run in enumerate((first, runs - 1 - first)):
        row_pos = run * RUN + lax.broadcasted_iota(jnp.int32, (RUN, 1), 0)
        at = lax.broadcasted_iota(jnp.int32, (RUN, runs * RUN), 1) == row_pos
        row_doc = jnp.sum(jnp.where(at, segment, 0.0), axis=1, keepdims=True)
        doc_start = jnp.sum(jnp.where(segment < row_doc, 1.0, 0.0), axis=1, keepdims=True).astype(jnp.int32)
        key_pos = jnp.maximum(run - reach, 0) * RUN + lax.broadcasted_iota(jnp.int32, bias_ref.shape[1:], 1)
        bias_ref[half] = jnp.where((key_pos <= row_pos) & (key_pos >= doc_start), 0.0, masked_fill)


def weights_kernel(runs, pos_ref, bias_ref, own_ref, *refs):
    blocks = runs // 2
    key_refs, tagged_refs, (weights_ref, key_buf) = refs[:blocks], refs[blocks:-2], refs[-2:]
    reach = runs // 4
    span = (reach + 1) * RUN
    numbers = run_numbers(runs, pos_ref, tagged_refs)
    sort_runs(numbers, own_ref, QUERY_COLUMNS, key_refs, key_buf)
    scale = math.log2(math.e) / math.sqrt(HEAD_SIZE)
    for half in range(2):
        start = jnp.maximum(numbers[0][half] - reach, 0)
        bias = jnp.concatenate([bias_ref[half]] * GROUP, axis=0)
        for kv in range(KEY_VALUE_HEADS):
            query = jnp.concatenate(
                [
                    own_ref[half * RUN : (half + 1) * RUN, h * HEAD_SIZE : (h + 1) * HEAD_SIZE]
                    for h in range(kv * GROUP, (kv + 1) * GROUP)
                ],
                axis=0,
            )
            key = key_buf[pl.ds(start, reach + 1), :, kv * HEAD_SIZE : (kv + 1) * HEAD_SIZE]
            scores = bias + lax.dot_general(
                query,
                key.reshape(span, HEAD_SIZE),
                (((1,), (1,)), ((), ())),
                preferred_element_type=jnp.float32,
            )
            row_max = jnp.max(scores, axis=1, keepdims=True)
            weights_ref[half * KEY_VALUE_HEADS + kv] = jnp.exp2((scores - row_max) * scale).astype(jnp.bfloat16)


def values_kernel(runs, pos_ref, weights_ref, own_ref, *refs):
    value_refs, (out_ref, value_buf, result_buf, out_sems) = refs[:-4], refs[-4:]
    reach = runs // 4
    span = (reach + 1) * RUN
    numbers = run_numbers(runs, pos_ref, value_refs[:-2])
    sort_runs(numbers, own_ref, QUERY_COLUMNS + KV_COLUMNS, value_refs, value_buf)
    ones = jnp.ones((span, HEAD_SIZE), jnp.bfloat16)
    copies = []
    for half in range(2):
        start = jnp.maximum(numbers[0][half] - reach, 0)
        for kv in range(KEY_VALUE_HEADS):
            value = value_buf[pl.ds(start, reach + 1), :, kv * HEAD_SIZE : (kv + 1) * HEAD_SIZE]
            summed = jnp.dot(
                weights_ref[half * KEY_VALUE_HEADS + kv],
                jnp.concatenate([value.reshape(span, HEAD_SIZE), ones], axis=1),
                preferred_element_type=jnp.float32,
            )
            result = (summed[:, :HEAD_SIZE] / summed[:, HEAD_SIZE:]).astype(jnp.bfloat16)
            for i in range(GROUP):
                h = kv * GROUP + i
                result_buf[half, :, h * HEAD_SIZE : (h + 1) * HEAD_SIZE] = result[i * RUN : (i + 1) * RUN]
        copies.append(
            pltpu.make_async_copy(result_buf.at[half], out_ref.at[pl.ds(half * RUN, RUN), :], out_sems.at[half])
        )
        copies[-1].start()
    for copy in copies:
        copy.wait()


def per_device(queries, keys, values, token_pos, segment):
    sections, places = lax.axis_size("section"), lax.axis_size("ctx")
    runs = segment.shape[0] // RUN
    depth = places // 2
    ring = [z * 2 for z in range(depth)] + [z * 2 + 1 for z in reversed(range(depth))]

    def shift(block, section_by, ring_by):
        pairs = []
        for s in range(sections):
            for i in range(places):
                target = (s + section_by) % sections * places + ring[(i + ring_by) % places]
                pairs.append((s * places + ring[i], target))
        return lax.ppermute(block, ("section", "ctx"), pairs)

    own = jnp.concatenate([queries[0], keys[0], values[0]], axis=1)

    def around(block, early=None):
        ahead, back = shift(block, 1, 1), shift(block, 1, -1)
        held = [ahead, back]
        if early is not None:
            ahead, early = lax.optimization_barrier((ahead, early))
        for _ in range(2, places // 2):
            ahead, back = shift(ahead, 0, 1), shift(back, 0, -1)
            held.extend([ahead, back])
        return held + [shift(ahead[:RUN], 0, 1), shift(back[RUN:TOK_DEV], 0, -1)], early

    pos = lax.optimization_barrier(jnp.concatenate([token_pos, segment]).astype(jnp.float32)[None])
    tag = jnp.broadcast_to((pos[:, :1] / RUN).astype(jnp.bfloat16), (TAG_ROWS, KV_COLUMNS))
    all_keys, own = around(keys[0], own)
    all_values, _ = around(jnp.concatenate([values[0], tag], axis=0))
    own = shift(own, 1, 0)
    vmem = pl.BlockSpec(memory_space=pltpu.VMEM)
    params = pltpu.CompilerParams(vmem_limit_bytes=(12 + runs // 4) * 1024 * 1024)
    sorted_buf = pltpu.VMEM((runs, RUN, KV_COLUMNS), jnp.bfloat16)
    before_mask = all_keys[-2:]
    bias = pl.pallas_call(
        functools.partial(bias_kernel, runs),
        out_shape=jax.ShapeDtypeStruct((2, RUN, (runs // 4 + 1) * RUN), jnp.float32),
        in_specs=[vmem] * (1 + len(before_mask)),
        out_specs=vmem,
        compiler_params=pltpu.CompilerParams(vmem_limit_bytes=8 * 1024 * 1024),
        cost_estimate=pl.CostEstimate(flops=10 << 30, bytes_accessed=0, transcendentals=0),
    )(pos, *before_mask)
    weights = pl.pallas_call(
        functools.partial(weights_kernel, runs),
        out_shape=jax.ShapeDtypeStruct((2 * KEY_VALUE_HEADS, GROUP * RUN, (runs // 4 + 1) * RUN), jnp.bfloat16),
        in_specs=[vmem] * (3 + len(all_keys) + len(all_values[:-2])),
        out_specs=vmem,
        scratch_shapes=[sorted_buf],
        compiler_params=params,
        cost_estimate=pl.CostEstimate(flops=1 << 26, bytes_accessed=1 << 20, transcendentals=0),
    )(pos, bias, own, *all_keys, *all_values[:-2])
    out = pl.pallas_call(
        functools.partial(values_kernel, runs),
        out_shape=jax.ShapeDtypeStruct((TOK_DEV, QUERY_COLUMNS), jnp.bfloat16),
        in_specs=[vmem] * (3 + len(all_values)),
        out_specs=pl.BlockSpec(memory_space=pl.ANY),
        scratch_shapes=[
            sorted_buf,
            pltpu.VMEM((2, RUN, QUERY_COLUMNS), jnp.bfloat16),
            pltpu.SemaphoreType.DMA((2,)),
        ],
        compiler_params=params,
        cost_estimate=pl.CostEstimate(flops=1 << 26, bytes_accessed=1 << 20, transcendentals=0),
    )(pos, weights, own, *all_values)
    return out[None]


def solution(mesh):
    return jax.shard_map(
        per_device,
        mesh=mesh,
        in_specs=(
            P("section", "ctx", None),
            P("section", "ctx", None),
            P("section", "ctx", None),
            P("ctx"),
            P(),
        ),
        out_specs=P("section", "ctx", None),
        check_vma=False,
    )
```

```python
import functools
import math

import jax
import jax.numpy as jnp
from jax import lax
from jax.experimental import pallas as pl
from jax.experimental.pallas import tpu as pltpu
from jax.sharding import PartitionSpec as P

HEAD_SIZE = 128
QUERY_HEADS = 32
KEY_VALUE_HEADS = 4
GROUP = QUERY_HEADS // KEY_VALUE_HEADS
RUN = 64
TOK_DEV = 2 * RUN
QUERY_COLUMNS = QUERY_HEADS * HEAD_SIZE
KV_COLUMNS = KEY_VALUE_HEADS * HEAD_SIZE
TAG_ROWS = 16

masked_fill = -1e30


def first_run(pos_ref):
    return lax.div(jnp.min(pos_ref[:, :TOK_DEV]).astype(jnp.int32), RUN)


def run_numbers(runs, pos_ref, tagged_refs):
    firsts = [first_run(pos_ref)]
    for ref in tagged_refs:
        firsts.append(jnp.min(ref[TOK_DEV:, :TOK_DEV].astype(jnp.float32)).astype(jnp.int32))
    places = runs // 2
    firsts.append(places * (places - 1) // 2 - sum(firsts))
    return [(first, runs - 1 - first) for first in firsts]


def sort_runs(numbers, own_ref, own_column, block_refs, sorted_ref):
    for half, number in enumerate(numbers[0]):
        sorted_ref[number] = own_ref[half * RUN : (half + 1) * RUN, own_column : own_column + KV_COLUMNS]
    for (first, second), ref in zip(numbers[1:], block_refs):
        sorted_ref[first] = ref[:RUN, :]
        sorted_ref[second] = ref[RUN:TOK_DEV, :]


def bias_kernel(runs, pos_ref, *refs):
    bias_ref = refs[-1]
    reach = runs // 4
    segment = pos_ref[:, TOK_DEV:]
    first = first_run(pos_ref)
    for half, run in enumerate((first, runs - 1 - first)):
        row_pos = run * RUN + lax.broadcasted_iota(jnp.int32, (RUN, 1), 0)
        at = lax.broadcasted_iota(jnp.int32, (RUN, runs * RUN), 1) == row_pos
        row_doc = jnp.sum(jnp.where(at, segment, 0.0), axis=1, keepdims=True)
        doc_start = jnp.sum(jnp.where(segment < row_doc, 1.0, 0.0), axis=1, keepdims=True).astype(jnp.int32)
        key_pos = jnp.maximum(run - reach, 0) * RUN + lax.broadcasted_iota(jnp.int32, bias_ref.shape[1:], 1)
        bias_ref[half] = jnp.where((key_pos <= row_pos) & (key_pos >= doc_start), 0.0, masked_fill)


def weights_kernel(runs, pos_ref, bias_ref, own_ref, *refs):
    blocks = runs // 2
    key_refs, tagged_refs = refs[:blocks], refs[blocks:-4]
    weights_ref, inverse_ref, sorted_ref, key_buf = refs[-4:]
    reach = runs // 4
    span = (reach + 1) * RUN
    numbers = run_numbers(runs, pos_ref, tagged_refs)
    sort_runs(numbers, own_ref, QUERY_COLUMNS, key_refs[:-2], key_buf)
    for number, ref in zip(numbers[-1], key_refs[-2:]):
        key_buf[number] = ref[...]
    sort_runs(numbers, own_ref, QUERY_COLUMNS + KV_COLUMNS, tagged_refs, sorted_ref)
    ones = jnp.ones((span, HEAD_SIZE), jnp.bfloat16)
    scale = math.log2(math.e) / math.sqrt(HEAD_SIZE)
    for half in range(2):
        start = jnp.maximum(numbers[0][half] - reach, 0)
        bias = jnp.concatenate([bias_ref[half]] * GROUP, axis=0)
        for kv in range(KEY_VALUE_HEADS):
            query = jnp.concatenate(
                [
                    own_ref[half * RUN : (half + 1) * RUN, h * HEAD_SIZE : (h + 1) * HEAD_SIZE]
                    for h in range(kv * GROUP, (kv + 1) * GROUP)
                ],
                axis=0,
            )
            key = key_buf[pl.ds(start, reach + 1), :, kv * HEAD_SIZE : (kv + 1) * HEAD_SIZE]
            scores = bias + lax.dot_general(
                query,
                key.reshape(span, HEAD_SIZE),
                (((1,), (1,)), ((), ())),
                preferred_element_type=jnp.float32,
            )
            row_max = jnp.max(scores, axis=1, keepdims=True)
            weights = jnp.exp2((scores - row_max) * scale).astype(jnp.bfloat16)
            weights_ref[half * KEY_VALUE_HEADS + kv] = weights
            total = jnp.dot(weights, ones, preferred_element_type=jnp.float32)
            inverse_ref[half * KEY_VALUE_HEADS + kv] = 1.0 / total


def values_kernel(runs, pos_ref, weights_ref, inverse_ref, sorted_ref, *refs):
    tagged_refs, last_refs, (out_ref, result_buf, out_sems) = refs[:-5], refs[-5:-3], refs[-3:]
    reach = runs // 4
    numbers = run_numbers(runs, pos_ref, tagged_refs)
    copies = []
    for half in range(2):
        start = jnp.maximum(numbers[0][half] - reach, 0)
        for kv in range(KEY_VALUE_HEADS):
            columns = slice(kv * HEAD_SIZE, (kv + 1) * HEAD_SIZE)
            parts = []
            for i in range(reach + 1):
                part = sorted_ref[start + i, :, columns]
                for number, last_ref in zip(numbers[-1], last_refs):
                    part = jnp.where(start + i == number, last_ref[:, columns], part)
                parts.append(part)
            summed = jnp.dot(
                weights_ref[half * KEY_VALUE_HEADS + kv],
                jnp.concatenate(parts, axis=0),
                preferred_element_type=jnp.float32,
            )
            result = (summed * inverse_ref[half * KEY_VALUE_HEADS + kv]).astype(jnp.bfloat16)
            for i in range(GROUP):
                h = kv * GROUP + i
                result_buf[half, :, h * HEAD_SIZE : (h + 1) * HEAD_SIZE] = result[i * RUN : (i + 1) * RUN]
        copies.append(
            pltpu.make_async_copy(result_buf.at[half], out_ref.at[pl.ds(half * RUN, RUN), :], out_sems.at[half])
        )
        copies[-1].start()
    for copy in copies:
        copy.wait()


def per_device(queries, keys, values, token_pos, segment):
    sections, places = lax.axis_size("section"), lax.axis_size("ctx")
    runs = segment.shape[0] // RUN
    depth = places // 2
    ring = [z * 2 for z in range(depth)] + [z * 2 + 1 for z in reversed(range(depth))]

    def shift(block, section_by, ring_by):
        pairs = []
        for s in range(sections):
            for i in range(places):
                target = (s + section_by) % sections * places + ring[(i + ring_by) % places]
                pairs.append((s * places + ring[i], target))
        return lax.ppermute(block, ("section", "ctx"), pairs)

    own = jnp.concatenate([queries[0], keys[0], values[0]], axis=1)

    def around(block, early=None):
        ahead, back = shift(block, 1, 1), shift(block, 1, -1)
        held = [ahead, back]
        if early is not None:
            ahead, early = lax.optimization_barrier((ahead, early))
        for _ in range(2, places // 2):
            ahead, back = shift(ahead, 0, 1), shift(back, 0, -1)
            held.extend([ahead, back])
        return held + [shift(ahead[:RUN], 0, 1), shift(back[RUN:TOK_DEV], 0, -1)], early

    tag = jnp.broadcast_to((token_pos >> (RUN.bit_length() - 1)).astype(jnp.bfloat16)[None], (TAG_ROWS, TOK_DEV))
    tag = jnp.pad(tag, ((0, 0), (0, KV_COLUMNS - TOK_DEV)))
    all_keys, own = around(keys[0], own)
    all_values, _ = around(jnp.concatenate([values[0], tag], axis=0))
    own = shift(own, 1, 0)
    pos = lax.optimization_barrier(jnp.concatenate([token_pos, segment]).astype(jnp.float32)[None])
    vmem = pl.BlockSpec(memory_space=pltpu.VMEM)
    params = pltpu.CompilerParams(vmem_limit_bytes=(12 + runs // 4) * 1024 * 1024)
    before_mask = all_keys[-2:]
    bias = pl.pallas_call(
        functools.partial(bias_kernel, runs),
        out_shape=jax.ShapeDtypeStruct((2, RUN, (runs // 4 + 1) * RUN), jnp.float32),
        in_specs=[vmem] * (1 + len(before_mask)),
        out_specs=vmem,
        compiler_params=pltpu.CompilerParams(vmem_limit_bytes=8 * 1024 * 1024),
        cost_estimate=pl.CostEstimate(flops=35 << 28, bytes_accessed=0, transcendentals=0),
    )(pos, *before_mask)
    weights, inverse, sorted_values = pl.pallas_call(
        functools.partial(weights_kernel, runs),
        out_shape=(
            jax.ShapeDtypeStruct((2 * KEY_VALUE_HEADS, GROUP * RUN, (runs // 4 + 1) * RUN), jnp.bfloat16),
            jax.ShapeDtypeStruct((2 * KEY_VALUE_HEADS, GROUP * RUN, HEAD_SIZE), jnp.float32),
            jax.ShapeDtypeStruct((runs, RUN, KV_COLUMNS), jnp.bfloat16),
        ),
        in_specs=[vmem] * (3 + len(all_keys) + len(all_values[:-2])),
        out_specs=(vmem,) * 3,
        scratch_shapes=[pltpu.VMEM((runs, RUN, KV_COLUMNS), jnp.bfloat16)],
        compiler_params=params,
        cost_estimate=pl.CostEstimate(flops=1 << 26, bytes_accessed=1 << 20, transcendentals=0),
    )(pos, bias, own, *all_keys, *all_values[:-2])
    out = pl.pallas_call(
        functools.partial(values_kernel, runs),
        out_shape=jax.ShapeDtypeStruct((TOK_DEV, QUERY_COLUMNS), jnp.bfloat16),
        in_specs=[vmem] * (4 + len(all_values)),
        out_specs=pl.BlockSpec(memory_space=pl.ANY),
        scratch_shapes=[
            pltpu.VMEM((2, RUN, QUERY_COLUMNS), jnp.bfloat16),
            pltpu.SemaphoreType.DMA((2,)),
        ],
        compiler_params=params,
        cost_estimate=pl.CostEstimate(flops=1 << 26, bytes_accessed=1 << 20, transcendentals=0),
    )(pos, weights, inverse, sorted_values, *all_values)
    return out[None]


def solution(mesh):
    return jax.shard_map(
        per_device,
        mesh=mesh,
        in_specs=(
            P("section", "ctx", None),
            P("section", "ctx", None),
            P("section", "ctx", None),
            P("ctx"),
            P(),
        ),
        out_specs=P("section", "ctx", None),
        check_vma=False,
    )
```

```python
import functools
import math

import jax
import jax.numpy as jnp
from jax import lax
from jax.experimental import pallas as pl
from jax.experimental.pallas import tpu as pltpu
from jax.sharding import PartitionSpec as P

HEAD_SIZE = 128
QUERY_HEADS = 32
KEY_VALUE_HEADS = 4
GROUP = QUERY_HEADS // KEY_VALUE_HEADS
RUN = 64
TOK_DEV = 2 * RUN
QUERY_COLUMNS = QUERY_HEADS * HEAD_SIZE
KV_COLUMNS = KEY_VALUE_HEADS * HEAD_SIZE
TAG_ROWS = 16

masked_fill = -1e30


def first_run(pos_ref):
    return lax.div(jnp.min(pos_ref[:, :TOK_DEV]).astype(jnp.int32), RUN)


def run_numbers(runs, pos_ref, tagged_refs):
    firsts = [first_run(pos_ref)]
    for ref in tagged_refs:
        firsts.append(jnp.min(ref[TOK_DEV:, :TOK_DEV].astype(jnp.float32)).astype(jnp.int32))
    places = runs // 2
    firsts.append(places * (places - 1) // 2 - sum(firsts))
    return [(first, runs - 1 - first) for first in firsts]


def sort_runs(numbers, own_ref, own_column, block_refs, sorted_ref):
    for half, number in enumerate(numbers[0]):
        sorted_ref[number] = own_ref[half * RUN : (half + 1) * RUN, own_column : own_column + KV_COLUMNS]
    for (first, second), ref in zip(numbers[1:], block_refs):
        sorted_ref[first] = ref[:RUN, :]
        sorted_ref[second] = ref[RUN:TOK_DEV, :]


def pack_kernel(pos_ref, query_ref, key_ref, value_ref, tagged_ref, own_ref, pos_buf, sems):
    sources = [(pos_ref, pos_buf), (value_ref, tagged_ref.at[pl.ds(0, TOK_DEV), :])]
    column = 0
    for ref in (query_ref, key_ref, value_ref):
        sources.append((ref, own_ref.at[:, pl.ds(column, ref.shape[1])]))
        column += ref.shape[1]
    copies = [pltpu.make_async_copy(source, target, sems.at[i]) for i, (source, target) in enumerate(sources)]
    for copy in copies:
        copy.start()
    copies[0].wait()
    tag = jnp.floor(pos_buf[...].astype(jnp.float32) * (1.0 / RUN)).astype(jnp.bfloat16)
    for i in range(KEY_VALUE_HEADS):
        tagged_ref[TOK_DEV:, i * TOK_DEV : (i + 1) * TOK_DEV] = jnp.broadcast_to(tag, (TAG_ROWS, TOK_DEV))
    for copy in copies[1:]:
        copy.wait()


def bias_kernel(runs, pos_ref, *refs):
    bias_ref = refs[-1]
    reach = runs // 4
    segment = pos_ref[:, TOK_DEV:]
    first = first_run(pos_ref)
    for half, run in enumerate((first, runs - 1 - first)):
        row_pos = run * RUN + lax.broadcasted_iota(jnp.int32, (RUN, 1), 0)
        at = lax.broadcasted_iota(jnp.int32, (RUN, runs * RUN), 1) == row_pos
        row_doc = jnp.sum(jnp.where(at, segment, 0.0), axis=1, keepdims=True)
        doc_start = jnp.sum(jnp.where(segment < row_doc, 1.0, 0.0), axis=1, keepdims=True).astype(jnp.int32)
        key_pos = jnp.maximum(run - reach, 0) * RUN + lax.broadcasted_iota(jnp.int32, bias_ref.shape[1:], 1)
        bias_ref[half] = jnp.where((key_pos <= row_pos) & (key_pos >= doc_start), 0.0, masked_fill)


def weights_kernel(runs, pos_ref, bias_ref, own_ref, *refs):
    blocks = runs // 2
    key_refs, tagged_refs = refs[:blocks], refs[blocks:-3]
    weights_ref, sorted_ref, key_buf = refs[-3:]
    reach = runs // 4
    span = (reach + 1) * RUN
    numbers = run_numbers(runs, pos_ref, tagged_refs)
    sort_runs(numbers, own_ref, QUERY_COLUMNS, key_refs[:-2], key_buf)
    for number, ref in zip(numbers[-1], key_refs[-2:]):
        key_buf[number] = ref[...]
    sort_runs(numbers, own_ref, QUERY_COLUMNS + KV_COLUMNS, tagged_refs, sorted_ref)
    scale = math.log2(math.e) / math.sqrt(HEAD_SIZE)
    for half in range(2):
        start = jnp.maximum(numbers[0][half] - reach, 0)
        bias = jnp.concatenate([bias_ref[half]] * GROUP, axis=0)
        for kv in range(KEY_VALUE_HEADS):
            query = jnp.concatenate(
                [
                    own_ref[half * RUN : (half + 1) * RUN, h * HEAD_SIZE : (h + 1) * HEAD_SIZE]
                    for h in range(kv * GROUP, (kv + 1) * GROUP)
                ],
                axis=0,
            )
            key = key_buf[pl.ds(start, reach + 1), :, kv * HEAD_SIZE : (kv + 1) * HEAD_SIZE]
            scores = bias + lax.dot_general(
                query,
                key.reshape(span, HEAD_SIZE),
                (((1,), (1,)), ((), ())),
                preferred_element_type=jnp.float32,
            )
            row_max = jnp.max(scores, axis=1, keepdims=True)
            weights_ref[half * KEY_VALUE_HEADS + kv] = jnp.exp2((scores - row_max) * scale).astype(jnp.bfloat16)


def values_kernel(runs, pos_ref, weights_ref, sorted_ref, *refs):
    tagged_refs, last_refs, (out_ref, result_buf, out_sems) = refs[:-5], refs[-5:-3], refs[-3:]
    reach = runs // 4
    numbers = run_numbers(runs, pos_ref, tagged_refs)
    ones = jnp.ones(((reach + 1) * RUN, HEAD_SIZE), jnp.bfloat16)
    copies = []
    for half in range(2):
        start = jnp.maximum(numbers[0][half] - reach, 0)
        for kv in range(KEY_VALUE_HEADS):
            columns = slice(kv * HEAD_SIZE, (kv + 1) * HEAD_SIZE)
            parts = []
            for i in range(reach + 1):
                part = sorted_ref[start + i, :, columns]
                for number, last_ref in zip(numbers[-1], last_refs):
                    part = jnp.where(start + i == number, last_ref[:, columns], part)
                parts.append(part)
            summed = jnp.dot(
                weights_ref[half * KEY_VALUE_HEADS + kv],
                jnp.concatenate([jnp.concatenate(parts, axis=0), ones], axis=1),
                preferred_element_type=jnp.float32,
            )
            result = (summed[:, :HEAD_SIZE] / summed[:, HEAD_SIZE:]).astype(jnp.bfloat16)
            for i in range(GROUP):
                h = kv * GROUP + i
                result_buf[half, :, h * HEAD_SIZE : (h + 1) * HEAD_SIZE] = result[i * RUN : (i + 1) * RUN]
        copies.append(
            pltpu.make_async_copy(result_buf.at[half], out_ref.at[pl.ds(half * RUN, RUN), :], out_sems.at[half])
        )
        copies[-1].start()
    for copy in copies:
        copy.wait()


def per_device(queries, keys, values, token_pos, segment):
    sections, places = lax.axis_size("section"), lax.axis_size("ctx")
    runs = segment.shape[0] // RUN
    depth = places // 2
    ring = [z * 2 for z in range(depth)] + [z * 2 + 1 for z in reversed(range(depth))]

    def shift(block, section_by, ring_by):
        pairs = []
        for s in range(sections):
            for i in range(places):
                target = (s + section_by) % sections * places + ring[(i + ring_by) % places]
                pairs.append((s * places + ring[i], target))
        return lax.ppermute(block, ("section", "ctx"), pairs)

    def around(block):
        ahead, back = shift(block, 1, 1), shift(block, 1, -1)
        held = [ahead, back]
        for _ in range(2, places // 2):
            ahead, back = shift(ahead, 0, 1), shift(back, 0, -1)
            held.extend([ahead, back])
        return held + [shift(ahead[:RUN], 0, 1), shift(back[RUN:TOK_DEV], 0, -1)]

    vmem, anywhere = pl.BlockSpec(memory_space=pltpu.VMEM), pl.BlockSpec(memory_space=pl.ANY)
    tagged, own = pl.pallas_call(
        pack_kernel,
        out_shape=(
            jax.ShapeDtypeStruct((TOK_DEV + TAG_ROWS, KV_COLUMNS), jnp.bfloat16),
            jax.ShapeDtypeStruct((TOK_DEV, QUERY_COLUMNS + 2 * KV_COLUMNS), jnp.bfloat16),
        ),
        in_specs=[anywhere] * 4,
        out_specs=(vmem,) * 2,
        scratch_shapes=[pltpu.VMEM((1, TOK_DEV), jnp.int32), pltpu.SemaphoreType.DMA((5,))],
        compiler_params=pltpu.CompilerParams(vmem_limit_bytes=58 * 1024 * 1024),
        cost_estimate=pl.CostEstimate(flops=0, bytes_accessed=1 << 22, transcendentals=0),
    )(token_pos[None], queries[0], keys[0], values[0])
    all_keys, all_values = around(keys[0]), around(tagged)
    own = shift(own, 1, 0)
    pos = lax.optimization_barrier(jnp.concatenate([token_pos, segment]).astype(jnp.float32)[None])
    params = pltpu.CompilerParams(vmem_limit_bytes=(12 + runs // 4) * 1024 * 1024)
    before_mask = all_keys[-2:]
    bias = pl.pallas_call(
        functools.partial(bias_kernel, runs),
        out_shape=jax.ShapeDtypeStruct((2, RUN, (runs // 4 + 1) * RUN), jnp.float32),
        in_specs=[vmem] * (1 + len(before_mask)),
        out_specs=vmem,
        compiler_params=pltpu.CompilerParams(vmem_limit_bytes=8 * 1024 * 1024),
        cost_estimate=pl.CostEstimate(flops=35 << 28, bytes_accessed=0, transcendentals=0),
    )(pos, *before_mask)
    weights, sorted_values = pl.pallas_call(
        functools.partial(weights_kernel, runs),
        out_shape=(
            jax.ShapeDtypeStruct((2 * KEY_VALUE_HEADS, GROUP * RUN, (runs // 4 + 1) * RUN), jnp.bfloat16),
            jax.ShapeDtypeStruct((runs, RUN, KV_COLUMNS), jnp.bfloat16),
        ),
        in_specs=[vmem] * (3 + len(all_keys) + len(all_values[:-2])),
        out_specs=(vmem,) * 2,
        scratch_shapes=[pltpu.VMEM((runs, RUN, KV_COLUMNS), jnp.bfloat16)],
        compiler_params=params,
        cost_estimate=pl.CostEstimate(flops=1 << 26, bytes_accessed=1 << 20, transcendentals=0),
    )(pos, bias, own, *all_keys, *all_values[:-2])
    out = pl.pallas_call(
        functools.partial(values_kernel, runs),
        out_shape=jax.ShapeDtypeStruct((TOK_DEV, QUERY_COLUMNS), jnp.bfloat16),
        in_specs=[vmem] * (3 + len(all_values)),
        out_specs=anywhere,
        scratch_shapes=[
            pltpu.VMEM((2, RUN, QUERY_COLUMNS), jnp.bfloat16),
            pltpu.SemaphoreType.DMA((2,)),
        ],
        compiler_params=params,
        cost_estimate=pl.CostEstimate(flops=1 << 26, bytes_accessed=1 << 20, transcendentals=0),
    )(pos, weights, sorted_values, *all_values)
    return out[None]


def solution(mesh):
    return jax.shard_map(
        per_device,
        mesh=mesh,
        in_specs=(
            P("section", "ctx", None),
            P("section", "ctx", None),
            P("section", "ctx", None),
            P("ctx"),
            P(),
        ),
        out_specs=P("section", "ctx", None),
        check_vma=False,
    )
```

```python
import functools
import math

import jax
import jax.numpy as jnp
from jax import lax
from jax.experimental import pallas as pl
from jax.experimental.pallas import tpu as pltpu
from jax.sharding import PartitionSpec as P

HEAD_SIZE = 128
QUERY_HEADS = 32
KEY_VALUE_HEADS = 4
GROUP = QUERY_HEADS // KEY_VALUE_HEADS
RUN = 64
TOK_DEV = 2 * RUN
QUERY_COLUMNS = QUERY_HEADS * HEAD_SIZE
KV_COLUMNS = KEY_VALUE_HEADS * HEAD_SIZE
TAG_ROWS = 16

masked_fill = -1e30


def first_run(pos_ref):
    return lax.div(jnp.min(pos_ref[:, :TOK_DEV]).astype(jnp.int32), RUN)


def run_numbers(runs, pos_ref, tagged_refs):
    firsts = [first_run(pos_ref)]
    for ref in tagged_refs:
        firsts.append(jnp.min(ref[TOK_DEV:, :TOK_DEV].astype(jnp.float32)).astype(jnp.int32))
    places = runs // 2
    firsts.append(places * (places - 1) // 2 - sum(firsts))
    return [(first, runs - 1 - first) for first in firsts]


def sort_runs(numbers, own_ref, own_column, block_refs, sorted_ref):
    for half, number in enumerate(numbers[0]):
        sorted_ref[number] = own_ref[half * RUN : (half + 1) * RUN, own_column : own_column + KV_COLUMNS]
    for (first, second), ref in zip(numbers[1:], block_refs):
        sorted_ref[first] = ref[:RUN, :]
        sorted_ref[second] = ref[RUN:TOK_DEV, :]


def bias_kernel(runs, pos_ref, *refs):
    bias_ref = refs[-1]
    reach = runs // 4
    segment = pos_ref[:, TOK_DEV:]
    first = first_run(pos_ref)
    for half, run in enumerate((first, runs - 1 - first)):
        row_pos = run * RUN + lax.broadcasted_iota(jnp.int32, (RUN, 1), 0)
        at = lax.broadcasted_iota(jnp.int32, (RUN, runs * RUN), 1) == row_pos
        row_doc = jnp.sum(jnp.where(at, segment, 0.0), axis=1, keepdims=True)
        doc_start = jnp.sum(jnp.where(segment < row_doc, 1.0, 0.0), axis=1, keepdims=True).astype(jnp.int32)
        key_pos = jnp.maximum(run - reach, 0) * RUN + lax.broadcasted_iota(jnp.int32, bias_ref.shape[1:], 1)
        bias_ref[half] = jnp.where((key_pos <= row_pos) & (key_pos >= doc_start), 0.0, masked_fill)


def weights_kernel(runs, pos_ref, bias_ref, own_ref, *refs):
    blocks = runs // 2
    key_refs, tagged_refs = refs[:blocks], refs[blocks:-3]
    weights_ref, sorted_ref, key_buf = refs[-3:]
    reach = runs // 4
    span = (reach + 1) * RUN
    numbers = run_numbers(runs, pos_ref, tagged_refs)
    sort_runs(numbers, own_ref, QUERY_COLUMNS, key_refs[:-2], key_buf)
    for number, ref in zip(numbers[-1], key_refs[-2:]):
        key_buf[number] = ref[...]
    sort_runs(numbers, own_ref, QUERY_COLUMNS + KV_COLUMNS, tagged_refs, sorted_ref)
    scale = math.log2(math.e) / math.sqrt(HEAD_SIZE)
    for half in range(2):
        start = jnp.maximum(numbers[0][half] - reach, 0)
        bias = jnp.concatenate([bias_ref[half]] * GROUP, axis=0)
        for kv in range(KEY_VALUE_HEADS):
            query = jnp.concatenate(
                [
                    own_ref[half * RUN : (half + 1) * RUN, h * HEAD_SIZE : (h + 1) * HEAD_SIZE]
                    for h in range(kv * GROUP, (kv + 1) * GROUP)
                ],
                axis=0,
            )
            key = key_buf[pl.ds(start, reach + 1), :, kv * HEAD_SIZE : (kv + 1) * HEAD_SIZE]
            scores = bias + lax.dot_general(
                query,
                key.reshape(span, HEAD_SIZE),
                (((1,), (1,)), ((), ())),
                preferred_element_type=jnp.float32,
            )
            row_max = jnp.max(scores, axis=1, keepdims=True)
            weights_ref[half * KEY_VALUE_HEADS + kv] = jnp.exp2((scores - row_max) * scale).astype(jnp.bfloat16)


def values_kernel(runs, pos_ref, weights_ref, sorted_ref, *refs):
    tagged_refs, last_refs, (out_ref, result_buf, out_sems) = refs[:-5], refs[-5:-3], refs[-3:]
    reach = runs // 4
    numbers = run_numbers(runs, pos_ref, tagged_refs)
    ones = jnp.ones(((reach + 1) * RUN, HEAD_SIZE), jnp.bfloat16)
    copies = []
    for half in range(2):
        start = jnp.maximum(numbers[0][half] - reach, 0)
        for kv in range(KEY_VALUE_HEADS):
            columns = slice(kv * HEAD_SIZE, (kv + 1) * HEAD_SIZE)
            parts = []
            for i in range(reach + 1):
                part = sorted_ref[start + i, :, columns]
                for number, last_ref in zip(numbers[-1], last_refs):
                    part = jnp.where(start + i == number, last_ref[:, columns], part)
                parts.append(part)
            summed = jnp.dot(
                weights_ref[half * KEY_VALUE_HEADS + kv],
                jnp.concatenate([jnp.concatenate(parts, axis=0), ones], axis=1),
                preferred_element_type=jnp.float32,
            )
            result = (summed[:, :HEAD_SIZE] / summed[:, HEAD_SIZE:]).astype(jnp.bfloat16)
            for i in range(GROUP):
                h = kv * GROUP + i
                result_buf[half, :, h * HEAD_SIZE : (h + 1) * HEAD_SIZE] = result[i * RUN : (i + 1) * RUN]
        copies.append(
            pltpu.make_async_copy(result_buf.at[half], out_ref.at[pl.ds(half * RUN, RUN), :], out_sems.at[half])
        )
        copies[-1].start()
    for copy in copies:
        copy.wait()


def per_device(queries, keys, values, token_pos, segment):
    sections, places = lax.axis_size("section"), lax.axis_size("ctx")
    runs = segment.shape[0] // RUN
    depth = places // 2
    ring = [z * 2 for z in range(depth)] + [z * 2 + 1 for z in reversed(range(depth))]

    def shift(block, section_by, ring_by):
        pairs = []
        for s in range(sections):
            for i in range(places):
                target = (s + section_by) % sections * places + ring[(i + ring_by) % places]
                pairs.append((s * places + ring[i], target))
        return lax.ppermute(block, ("section", "ctx"), pairs)

    def around(block):
        ahead, back = shift(block, 1, 1), shift(block, 1, -1)
        held = [ahead, back]
        for _ in range(2, places // 2):
            ahead, back = shift(ahead, 0, 1), shift(back, 0, -1)
            held.extend([ahead, back])
        return held + [shift(ahead[:RUN], 0, 1), shift(back[RUN:TOK_DEV], 0, -1)]

    own = shift(jnp.concatenate([queries[0], keys[0], values[0]], axis=1), 1, 0)
    tag = jnp.broadcast_to((token_pos >> (RUN.bit_length() - 1)).astype(jnp.bfloat16)[None], (TAG_ROWS, TOK_DEV))
    tag = jnp.pad(tag, ((0, 0), (0, KV_COLUMNS - TOK_DEV)))
    tagged = jnp.concatenate([values[0], tag], axis=0)
    all_keys, all_values = around(keys[0]), around(tagged)
    pos = lax.optimization_barrier(jnp.concatenate([token_pos, segment]).astype(jnp.float32)[None])
    params = pltpu.CompilerParams(vmem_limit_bytes=(12 + runs // 4) * 1024 * 1024)
    vmem = pl.BlockSpec(memory_space=pltpu.VMEM)
    before_mask = all_keys[-2:]
    bias = pl.pallas_call(
        functools.partial(bias_kernel, runs),
        out_shape=jax.ShapeDtypeStruct((2, RUN, (runs // 4 + 1) * RUN), jnp.float32),
        in_specs=[vmem] * (1 + len(before_mask)),
        out_specs=vmem,
        compiler_params=pltpu.CompilerParams(vmem_limit_bytes=8 * 1024 * 1024),
        cost_estimate=pl.CostEstimate(flops=35 << 28, bytes_accessed=0, transcendentals=0),
    )(pos, *before_mask)
    weights, sorted_values = pl.pallas_call(
        functools.partial(weights_kernel, runs),
        out_shape=(
            jax.ShapeDtypeStruct((2 * KEY_VALUE_HEADS, GROUP * RUN, (runs // 4 + 1) * RUN), jnp.bfloat16),
            jax.ShapeDtypeStruct((runs, RUN, KV_COLUMNS), jnp.bfloat16),
        ),
        in_specs=[vmem] * (3 + len(all_keys) + len(all_values[:-2])),
        out_specs=(vmem,) * 2,
        scratch_shapes=[pltpu.VMEM((runs, RUN, KV_COLUMNS), jnp.bfloat16)],
        compiler_params=params,
        cost_estimate=pl.CostEstimate(flops=1 << 26, bytes_accessed=1 << 20, transcendentals=0),
    )(pos, bias, own, *all_keys, *all_values[:-2])
    out = pl.pallas_call(
        functools.partial(values_kernel, runs),
        out_shape=jax.ShapeDtypeStruct((TOK_DEV, QUERY_COLUMNS), jnp.bfloat16),
        in_specs=[vmem] * (3 + len(all_values)),
        out_specs=pl.BlockSpec(memory_space=pl.ANY),
        scratch_shapes=[
            pltpu.VMEM((2, RUN, QUERY_COLUMNS), jnp.bfloat16),
            pltpu.SemaphoreType.DMA((2,)),
        ],
        compiler_params=params,
        cost_estimate=pl.CostEstimate(flops=1 << 26, bytes_accessed=1 << 20, transcendentals=0),
    )(pos, weights, sorted_values, *all_values)
    return out[None]


def solution(mesh):
    return jax.shard_map(
        per_device,
        mesh=mesh,
        in_specs=(
            P("section", "ctx", None),
            P("section", "ctx", None),
            P("section", "ctx", None),
            P("ctx"),
            P(),
        ),
        out_specs=P("section", "ctx", None),
        check_vma=False,
    )
```

```python
import functools
import math

import jax
import jax.numpy as jnp
from jax import lax
from jax.experimental import pallas as pl
from jax.experimental.pallas import tpu as pltpu
from jax.sharding import PartitionSpec as P

HEAD_SIZE = 128
QUERY_HEADS = 32
KEY_VALUE_HEADS = 4
GROUP = QUERY_HEADS // KEY_VALUE_HEADS
RUN = 64
TOK_DEV = 2 * RUN
QUERY_COLUMNS = QUERY_HEADS * HEAD_SIZE
KV_COLUMNS = KEY_VALUE_HEADS * HEAD_SIZE
TAG_ROWS = 16

masked_fill = -1e30


def first_run(pos_ref):
    return lax.div(jnp.min(pos_ref[:, :TOK_DEV]).astype(jnp.int32), RUN)


def run_numbers(runs, pos_ref, tagged_refs):
    firsts = [first_run(pos_ref)]
    for ref in tagged_refs:
        firsts.append(jnp.min(ref[TOK_DEV:, :TOK_DEV].astype(jnp.float32)).astype(jnp.int32))
    places = runs // 2
    firsts.append(places * (places - 1) // 2 - sum(firsts))
    return [(first, runs - 1 - first) for first in firsts]


def sort_runs(numbers, own_ref, own_column, block_refs, sorted_ref):
    for half, number in enumerate(numbers[0]):
        sorted_ref[number] = own_ref[half * RUN : (half + 1) * RUN, own_column : own_column + KV_COLUMNS]
    for (first, second), ref in zip(numbers[1:], block_refs):
        sorted_ref[first] = ref[:RUN, :]
        sorted_ref[second] = ref[RUN:TOK_DEV, :]


def blank_kernel(out_ref):
    out_ref[...] = jnp.zeros_like(out_ref)


def bias_kernel(runs, pos_ref, *refs):
    bias_ref = refs[-1]
    reach = runs // 4
    segment = pos_ref[:, TOK_DEV:]
    first = first_run(pos_ref)
    for half, run in enumerate((first, runs - 1 - first)):
        row_pos = run * RUN + lax.broadcasted_iota(jnp.int32, (RUN, 1), 0)
        at = lax.broadcasted_iota(jnp.int32, (RUN, runs * RUN), 1) == row_pos
        row_doc = jnp.sum(jnp.where(at, segment, 0.0), axis=1, keepdims=True)
        doc_start = jnp.sum(jnp.where(segment < row_doc, 1.0, 0.0), axis=1, keepdims=True).astype(jnp.int32)
        key_pos = jnp.maximum(run - reach, 0) * RUN + lax.broadcasted_iota(jnp.int32, bias_ref.shape[1:], 1)
        bias_ref[half] = jnp.where((key_pos <= row_pos) & (key_pos >= doc_start), 0.0, masked_fill)


def weights_kernel(runs, pos_ref, bias_ref, own_ref, *refs):
    blocks = runs // 2
    key_refs, tagged_refs = refs[:blocks], refs[blocks:-3]
    weights_ref, sorted_ref, key_buf = refs[-3:]
    reach = runs // 4
    span = (reach + 1) * RUN
    numbers = run_numbers(runs, pos_ref, tagged_refs)
    sort_runs(numbers, own_ref, QUERY_COLUMNS, key_refs[:-2], key_buf)
    for number, ref in zip(numbers[-1], key_refs[-2:]):
        key_buf[number] = ref[...]
    sort_runs(numbers, own_ref, QUERY_COLUMNS + KV_COLUMNS, tagged_refs, sorted_ref)
    scale = math.log2(math.e) / math.sqrt(HEAD_SIZE)
    for half in range(2):
        start = jnp.maximum(numbers[0][half] - reach, 0)
        bias = jnp.concatenate([bias_ref[half]] * GROUP, axis=0)
        for kv in range(KEY_VALUE_HEADS):
            query = jnp.concatenate(
                [
                    own_ref[half * RUN : (half + 1) * RUN, h * HEAD_SIZE : (h + 1) * HEAD_SIZE]
                    for h in range(kv * GROUP, (kv + 1) * GROUP)
                ],
                axis=0,
            )
            key = key_buf[pl.ds(start, reach + 1), :, kv * HEAD_SIZE : (kv + 1) * HEAD_SIZE]
            scores = bias + lax.dot_general(
                query,
                key.reshape(span, HEAD_SIZE),
                (((1,), (1,)), ((), ())),
                preferred_element_type=jnp.float32,
            )
            row_max = jnp.max(scores, axis=1, keepdims=True)
            weights_ref[half * KEY_VALUE_HEADS + kv] = jnp.exp2((scores - row_max) * scale).astype(jnp.bfloat16)


def values_kernel(runs, pos_ref, weights_ref, sorted_ref, *refs):
    tagged_refs, last_refs, (out_ref, result_buf, out_sems) = refs[:-5], refs[-5:-3], refs[-3:]
    reach = runs // 4
    numbers = run_numbers(runs, pos_ref, tagged_refs)
    ones = jnp.ones(((reach + 1) * RUN, HEAD_SIZE), jnp.bfloat16)
    copies = []
    for half in range(2):
        start = jnp.maximum(numbers[0][half] - reach, 0)
        for kv in range(KEY_VALUE_HEADS):
            columns = slice(kv * HEAD_SIZE, (kv + 1) * HEAD_SIZE)
            parts = []
            for i in range(reach + 1):
                part = sorted_ref[start + i, :, columns]
                for number, last_ref in zip(numbers[-1], last_refs):
                    part = jnp.where(start + i == number, last_ref[:, columns], part)
                parts.append(part)
            summed = jnp.dot(
                weights_ref[half * KEY_VALUE_HEADS + kv],
                jnp.concatenate([jnp.concatenate(parts, axis=0), ones], axis=1),
                preferred_element_type=jnp.float32,
            )
            result = (summed[:, :HEAD_SIZE] / summed[:, HEAD_SIZE:]).astype(jnp.bfloat16)
            for i in range(GROUP):
                h = kv * GROUP + i
                result_buf[half, :, h * HEAD_SIZE : (h + 1) * HEAD_SIZE] = result[i * RUN : (i + 1) * RUN]
        copies.append(
            pltpu.make_async_copy(result_buf.at[half], out_ref.at[pl.ds(half * RUN, RUN), :], out_sems.at[half])
        )
        copies[-1].start()
    for copy in copies:
        copy.wait()


def per_device(queries, keys, values, token_pos, segment):
    sections, places = lax.axis_size("section"), lax.axis_size("ctx")
    runs = segment.shape[0] // RUN
    depth = places // 2
    ring = [z * 2 for z in range(depth)] + [z * 2 + 1 for z in reversed(range(depth))]

    def shift(block, section_by, ring_by):
        pairs = []
        for s in range(sections):
            for i in range(places):
                target = (s + section_by) % sections * places + ring[(i + ring_by) % places]
                pairs.append((s * places + ring[i], target))
        return lax.ppermute(block, ("section", "ctx"), pairs)

    def around(block):
        ahead, back = shift(block, 1, 1), shift(block, 1, -1)
        held = [ahead, back]
        for _ in range(2, places // 2):
            ahead, back = shift(ahead, 0, 1), shift(back, 0, -1)
            held.extend([ahead, back])
        return held + [shift(ahead[:RUN], 0, 1), shift(back[RUN:TOK_DEV], 0, -1)]

    own = shift(jnp.concatenate([queries[0], keys[0], values[0]], axis=1), 1, 0)
    vmem = pl.BlockSpec(memory_space=pltpu.VMEM)
    blank = pl.pallas_call(
        blank_kernel,
        out_shape=jax.ShapeDtypeStruct((TAG_ROWS, KV_COLUMNS), jnp.bfloat16),
        out_specs=vmem,
        cost_estimate=pl.CostEstimate(flops=1 << 30, bytes_accessed=0, transcendentals=0),
    )()
    tag = jnp.pad((token_pos >> (RUN.bit_length() - 1)).astype(jnp.bfloat16), (0, KV_COLUMNS - TOK_DEV))
    tagged = jnp.concatenate([values[0], blank + tag[None]], axis=0)
    all_keys, all_values = around(keys[0]), around(tagged)
    pos = lax.optimization_barrier(jnp.concatenate([token_pos, segment]).astype(jnp.float32)[None])
    params = pltpu.CompilerParams(vmem_limit_bytes=(12 + runs // 4) * 1024 * 1024)
    before_mask = all_keys[-2:]
    bias = pl.pallas_call(
        functools.partial(bias_kernel, runs),
        out_shape=jax.ShapeDtypeStruct((2, RUN, (runs // 4 + 1) * RUN), jnp.float32),
        in_specs=[vmem] * (1 + len(before_mask)),
        out_specs=vmem,
        compiler_params=pltpu.CompilerParams(vmem_limit_bytes=8 * 1024 * 1024),
        cost_estimate=pl.CostEstimate(flops=35 << 28, bytes_accessed=0, transcendentals=0),
    )(pos, *before_mask)
    weights, sorted_values = pl.pallas_call(
        functools.partial(weights_kernel, runs),
        out_shape=(
            jax.ShapeDtypeStruct((2 * KEY_VALUE_HEADS, GROUP * RUN, (runs // 4 + 1) * RUN), jnp.bfloat16),
            jax.ShapeDtypeStruct((runs, RUN, KV_COLUMNS), jnp.bfloat16),
        ),
        in_specs=[vmem] * (3 + len(all_keys) + len(all_values[:-2])),
        out_specs=(vmem,) * 2,
        scratch_shapes=[pltpu.VMEM((runs, RUN, KV_COLUMNS), jnp.bfloat16)],
        compiler_params=params,
        cost_estimate=pl.CostEstimate(flops=1 << 26, bytes_accessed=1 << 20, transcendentals=0),
    )(pos, bias, own, *all_keys, *all_values[:-2])
    out = pl.pallas_call(
        functools.partial(values_kernel, runs),
        out_shape=jax.ShapeDtypeStruct((TOK_DEV, QUERY_COLUMNS), jnp.bfloat16),
        in_specs=[vmem] * (3 + len(all_values)),
        out_specs=pl.BlockSpec(memory_space=pl.ANY),
        scratch_shapes=[
            pltpu.VMEM((2, RUN, QUERY_COLUMNS), jnp.bfloat16),
            pltpu.SemaphoreType.DMA((2,)),
        ],
        compiler_params=params,
        cost_estimate=pl.CostEstimate(flops=1 << 26, bytes_accessed=1 << 20, transcendentals=0),
    )(pos, weights, sorted_values, *all_values)
    return out[None]


def solution(mesh):
    return jax.shard_map(
        per_device,
        mesh=mesh,
        in_specs=(
            P("section", "ctx", None),
            P("section", "ctx", None),
            P("section", "ctx", None),
            P("ctx"),
            P(),
        ),
        out_specs=P("section", "ctx", None),
        check_vma=False,
    )
```

```python
import functools
import math

import jax
import jax.numpy as jnp
from jax import lax
from jax.experimental import pallas as pl
from jax.experimental.pallas import tpu as pltpu
from jax.sharding import PartitionSpec as P

HEAD_SIZE = 128
QUERY_HEADS = 32
KEY_VALUE_HEADS = 4
GROUP = QUERY_HEADS // KEY_VALUE_HEADS
RUN = 64
TOK_DEV = 2 * RUN
QUERY_COLUMNS = QUERY_HEADS * HEAD_SIZE
KV_COLUMNS = KEY_VALUE_HEADS * HEAD_SIZE
TAG_ROWS = 16

masked_fill = -1e30


def first_run(pos_ref):
    return lax.div(jnp.min(pos_ref[:, :TOK_DEV]).astype(jnp.int32), RUN)


def run_numbers(runs, pos_ref, tagged_refs):
    firsts = [first_run(pos_ref)]
    for ref in tagged_refs:
        firsts.append(jnp.min(ref[TOK_DEV:, :TOK_DEV].astype(jnp.float32)).astype(jnp.int32))
    places = runs // 2
    firsts.append(places * (places - 1) // 2 - sum(firsts))
    return [(first, runs - 1 - first) for first in firsts]


def sort_runs(numbers, own_ref, own_column, block_refs, sorted_ref):
    for half, number in enumerate(numbers[0]):
        sorted_ref[number] = own_ref[half * RUN : (half + 1) * RUN, own_column : own_column + KV_COLUMNS]
    for (first, second), ref in zip(numbers[1:], block_refs):
        sorted_ref[first] = ref[:RUN, :]
        sorted_ref[second] = ref[RUN:TOK_DEV, :]


def blank_kernel(out_ref):
    out_ref[...] = jnp.zeros_like(out_ref)


def bias_kernel(runs, pos_ref, *refs):
    bias_ref = refs[-1]
    reach = runs // 4
    segment = pos_ref[:, TOK_DEV:]
    first = first_run(pos_ref)
    for half, run in enumerate((first, runs - 1 - first)):
        row_pos = run * RUN + lax.broadcasted_iota(jnp.int32, (RUN, 1), 0)
        at = lax.broadcasted_iota(jnp.int32, (RUN, runs * RUN), 1) == row_pos
        row_doc = jnp.sum(jnp.where(at, segment, 0.0), axis=1, keepdims=True)
        doc_start = jnp.sum(jnp.where(segment < row_doc, 1.0, 0.0), axis=1, keepdims=True).astype(jnp.int32)
        key_pos = jnp.maximum(run - reach, 0) * RUN + lax.broadcasted_iota(jnp.int32, bias_ref.shape[1:], 1)
        bias_ref[half] = jnp.where((key_pos <= row_pos) & (key_pos >= doc_start), 0.0, masked_fill)


def weights_kernel(runs, pos_ref, bias_ref, own_ref, *refs):
    blocks = runs // 2
    key_refs, tagged_refs = refs[:blocks], refs[blocks:-3]
    weights_ref, sorted_ref, key_buf = refs[-3:]
    reach = runs // 4
    span = (reach + 1) * RUN
    numbers = run_numbers(runs, pos_ref, tagged_refs)
    sort_runs(numbers, own_ref, QUERY_COLUMNS, key_refs[:-2], key_buf)
    for number, ref in zip(numbers[-1], key_refs[-2:]):
        key_buf[number] = ref[...]
    sort_runs(numbers, own_ref, QUERY_COLUMNS + KV_COLUMNS, tagged_refs, sorted_ref)
    scale = math.log2(math.e) / math.sqrt(HEAD_SIZE)
    for half in range(2):
        start = jnp.maximum(numbers[0][half] - reach, 0)
        bias = jnp.concatenate([bias_ref[half]] * GROUP, axis=0)
        for kv in range(KEY_VALUE_HEADS):
            query = jnp.concatenate(
                [
                    own_ref[half * RUN : (half + 1) * RUN, h * HEAD_SIZE : (h + 1) * HEAD_SIZE]
                    for h in range(kv * GROUP, (kv + 1) * GROUP)
                ],
                axis=0,
            )
            key = key_buf[pl.ds(start, reach + 1), :, kv * HEAD_SIZE : (kv + 1) * HEAD_SIZE]
            scores = bias + lax.dot_general(
                query,
                key.reshape(span, HEAD_SIZE),
                (((1,), (1,)), ((), ())),
                preferred_element_type=jnp.float32,
            )
            row_max = jnp.max(scores, axis=1, keepdims=True)
            weights_ref[half * KEY_VALUE_HEADS + kv] = jnp.exp2((scores - row_max) * scale).astype(jnp.bfloat16)


def values_kernel(runs, pos_ref, weights_ref, sorted_ref, *refs):
    tagged_refs, last_refs, (out_ref, result_buf, out_sems) = refs[:-5], refs[-5:-3], refs[-3:]
    reach = runs // 4
    numbers = run_numbers(runs, pos_ref, tagged_refs)
    ones = jnp.ones(((reach + 1) * RUN, HEAD_SIZE), jnp.bfloat16)
    copies = []
    for half in range(2):
        start = jnp.maximum(numbers[0][half] - reach, 0)
        for kv in range(KEY_VALUE_HEADS):
            columns = slice(kv * HEAD_SIZE, (kv + 1) * HEAD_SIZE)
            parts = []
            for i in range(reach + 1):
                part = sorted_ref[start + i, :, columns]
                for number, last_ref in zip(numbers[-1], last_refs):
                    part = jnp.where(start + i == number, last_ref[:, columns], part)
                parts.append(part)
            summed = jnp.dot(
                weights_ref[half * KEY_VALUE_HEADS + kv],
                jnp.concatenate([jnp.concatenate(parts, axis=0), ones], axis=1),
                preferred_element_type=jnp.float32,
            )
            result = (summed[:, :HEAD_SIZE] / summed[:, HEAD_SIZE:]).astype(jnp.bfloat16)
            for i in range(GROUP):
                h = kv * GROUP + i
                result_buf[half, :, h * HEAD_SIZE : (h + 1) * HEAD_SIZE] = result[i * RUN : (i + 1) * RUN]
        copies.append(
            pltpu.make_async_copy(result_buf.at[half], out_ref.at[pl.ds(half * RUN, RUN), :], out_sems.at[half])
        )
        copies[-1].start()
    for copy in copies:
        copy.wait()


def per_device(queries, keys, values, token_pos, segment):
    sections, places = lax.axis_size("section"), lax.axis_size("ctx")
    runs = segment.shape[0] // RUN
    depth = places // 2
    ring = [z * 2 for z in range(depth)] + [z * 2 + 1 for z in reversed(range(depth))]

    def shift(block, section_by, ring_by):
        pairs = []
        for s in range(sections):
            for i in range(places):
                target = (s + section_by) % sections * places + ring[(i + ring_by) % places]
                pairs.append((s * places + ring[i], target))
        return lax.ppermute(block, ("section", "ctx"), pairs)

    def around(block):
        ahead, back = shift(block, 1, 1), shift(block, 1, -1)
        held = [ahead, back]
        for _ in range(2, places // 2):
            ahead, back = shift(ahead, 0, 1), shift(back, 0, -1)
            held.extend([ahead, back])
        return held + [shift(ahead[:RUN], 0, 1), shift(back[RUN:TOK_DEV], 0, -1)]

    own = shift(jnp.concatenate([queries[0], keys[0], values[0]], axis=1), 1, 0)
    vmem = pl.BlockSpec(memory_space=pltpu.VMEM)
    blank = pl.pallas_call(
        blank_kernel,
        out_shape=jax.ShapeDtypeStruct((TAG_ROWS, KV_COLUMNS), jnp.bfloat16),
        out_specs=vmem,
        compiler_params=pltpu.CompilerParams(vmem_limit_bytes=8 * 1024 * 1024),
        cost_estimate=pl.CostEstimate(flops=1 << 30, bytes_accessed=0, transcendentals=0),
    )()
    tag = jnp.pad((token_pos >> (RUN.bit_length() - 1)).astype(jnp.bfloat16), (0, KV_COLUMNS - TOK_DEV))
    tagged = jnp.concatenate([values[0], blank + tag[None]], axis=0)
    all_keys, all_values = around(keys[0]), around(tagged)
    pos = lax.optimization_barrier(jnp.concatenate([token_pos, segment]).astype(jnp.float32)[None])
    params = pltpu.CompilerParams(vmem_limit_bytes=(12 + runs // 4) * 1024 * 1024)
    before_mask = all_keys[-2:]
    bias = pl.pallas_call(
        functools.partial(bias_kernel, runs),
        out_shape=jax.ShapeDtypeStruct((2, RUN, (runs // 4 + 1) * RUN), jnp.float32),
        in_specs=[vmem] * (1 + len(before_mask)),
        out_specs=vmem,
        compiler_params=pltpu.CompilerParams(vmem_limit_bytes=8 * 1024 * 1024),
        cost_estimate=pl.CostEstimate(flops=35 << 28, bytes_accessed=0, transcendentals=0),
    )(pos, *before_mask)
    weights, sorted_values = pl.pallas_call(
        functools.partial(weights_kernel, runs),
        out_shape=(
            jax.ShapeDtypeStruct((2 * KEY_VALUE_HEADS, GROUP * RUN, (runs // 4 + 1) * RUN), jnp.bfloat16),
            jax.ShapeDtypeStruct((runs, RUN, KV_COLUMNS), jnp.bfloat16),
        ),
        in_specs=[vmem] * (3 + len(all_keys) + len(all_values[:-2])),
        out_specs=(vmem,) * 2,
        scratch_shapes=[pltpu.VMEM((runs, RUN, KV_COLUMNS), jnp.bfloat16)],
        compiler_params=params,
        cost_estimate=pl.CostEstimate(flops=1 << 26, bytes_accessed=1 << 20, transcendentals=0),
    )(pos, bias, own, *all_keys, *all_values[:-2])
    out = pl.pallas_call(
        functools.partial(values_kernel, runs),
        out_shape=jax.ShapeDtypeStruct((TOK_DEV, QUERY_COLUMNS), jnp.bfloat16),
        in_specs=[vmem] * (3 + len(all_values)),
        out_specs=pl.BlockSpec(memory_space=pl.ANY),
        scratch_shapes=[
            pltpu.VMEM((2, RUN, QUERY_COLUMNS), jnp.bfloat16),
            pltpu.SemaphoreType.DMA((2,)),
        ],
        compiler_params=params,
        cost_estimate=pl.CostEstimate(flops=1 << 26, bytes_accessed=1 << 20, transcendentals=0),
    )(pos, weights, sorted_values, *all_values)
    return out[None]


def solution(mesh):
    return jax.shard_map(
        per_device,
        mesh=mesh,
        in_specs=(
            P("section", "ctx", None),
            P("section", "ctx", None),
            P("section", "ctx", None),
            P("ctx"),
            P(),
        ),
        out_specs=P("section", "ctx", None),
        check_vma=False,
    )
```

```python
import functools
import math

import jax
import jax.numpy as jnp
from jax import lax
from jax.experimental import pallas as pl
from jax.experimental.pallas import tpu as pltpu
from jax.sharding import PartitionSpec as P

HEAD_SIZE = 128
QUERY_HEADS = 32
KEY_VALUE_HEADS = 4
GROUP = QUERY_HEADS // KEY_VALUE_HEADS
RUN = 64
TOK_DEV = 2 * RUN
QUERY_COLUMNS = QUERY_HEADS * HEAD_SIZE
KV_COLUMNS = KEY_VALUE_HEADS * HEAD_SIZE
TAG_ROWS = 16
VALUE_ROWS = KEY_VALUE_HEADS * TOK_DEV

masked_fill = -1e30


def first_run(pos_ref):
    return lax.div(jnp.min(pos_ref[:, :TOK_DEV]).astype(jnp.int32), RUN)


def run_numbers(runs, pos_ref, tagged_refs):
    firsts = [first_run(pos_ref)]
    for ref in tagged_refs:
        firsts.append(jnp.min(ref[VALUE_ROWS:, :].astype(jnp.float32)).astype(jnp.int32))
    places = runs // 2
    firsts.append(places * (places - 1) // 2 - sum(firsts))
    return [(first, runs - 1 - first) for first in firsts]


def sort_keys(numbers, own_ref, block_refs, last_refs, sorted_ref):
    for half, number in enumerate(numbers[0]):
        sorted_ref[number] = own_ref[half * RUN : (half + 1) * RUN, QUERY_COLUMNS : QUERY_COLUMNS + KV_COLUMNS]
    for (first, second), ref in zip(numbers[1:], block_refs):
        sorted_ref[first] = ref[:RUN, :]
        sorted_ref[second] = ref[RUN:, :]
    for number, ref in zip(numbers[-1], last_refs):
        sorted_ref[number] = ref[...]


def sort_values(numbers, own_ref, block_refs, sorted_ref):
    for kv in range(KEY_VALUE_HEADS):
        column = QUERY_COLUMNS + KV_COLUMNS + kv * HEAD_SIZE
        for half, number in enumerate(numbers[0]):
            sorted_ref[kv, number] = own_ref[half * RUN : (half + 1) * RUN, column : column + HEAD_SIZE]
        for pair, ref in zip(numbers[1:], block_refs):
            for half, number in enumerate(pair):
                row = kv * TOK_DEV + half * RUN
                sorted_ref[kv, number] = ref[row : row + RUN, :]


def blank_kernel(*refs):
    refs[-1][...] = jnp.zeros_like(refs[-1])


def bias_kernel(runs, pos_ref, bias_ref):
    reach = runs // 4
    segment = pos_ref[:, TOK_DEV:]
    first = first_run(pos_ref)
    for half, run in enumerate((first, runs - 1 - first)):
        row_pos = run * RUN + lax.broadcasted_iota(jnp.int32, (RUN, 1), 0)
        at = lax.broadcasted_iota(jnp.int32, (RUN, runs * RUN), 1) == row_pos
        row_doc = jnp.sum(jnp.where(at, segment, 0.0), axis=1, keepdims=True)
        doc_start = jnp.sum(jnp.where(segment < row_doc, 1.0, 0.0), axis=1, keepdims=True).astype(jnp.int32)
        key_pos = jnp.maximum(run - reach, 0) * RUN + lax.broadcasted_iota(jnp.int32, bias_ref.shape[1:], 1)
        bias_ref[half] = jnp.where((key_pos <= row_pos) & (key_pos >= doc_start), 0.0, masked_fill)


def weights_kernel(runs, pos_ref, bias_ref, mark_ref, own_ref, *refs):
    blocks = runs // 2
    key_refs, tagged_refs = refs[:blocks], refs[blocks:-3]
    weights_ref, sorted_ref, key_buf = refs[-3:]
    reach = runs // 4
    span = (reach + 1) * RUN
    numbers = run_numbers(runs, pos_ref, tagged_refs)
    sort_keys(numbers, own_ref, key_refs[:-2], key_refs[-2:], key_buf)
    sort_values(numbers, own_ref, tagged_refs, sorted_ref)
    scale = math.log2(math.e) / math.sqrt(HEAD_SIZE)
    for half in range(2):
        start = jnp.maximum(numbers[0][half] - reach, 0)
        bias = jnp.concatenate([bias_ref[half]] * GROUP, axis=0)
        for kv in range(KEY_VALUE_HEADS):
            query = jnp.concatenate(
                [
                    own_ref[half * RUN : (half + 1) * RUN, h * HEAD_SIZE : (h + 1) * HEAD_SIZE]
                    for h in range(kv * GROUP, (kv + 1) * GROUP)
                ],
                axis=0,
            )
            key = key_buf[pl.ds(start, reach + 1), :, kv * HEAD_SIZE : (kv + 1) * HEAD_SIZE]
            scores = bias + lax.dot_general(
                query,
                key.reshape(span, HEAD_SIZE),
                (((1,), (1,)), ((), ())),
                preferred_element_type=jnp.float32,
            )
            row_max = jnp.max(scores, axis=1, keepdims=True)
            weights_ref[half * KEY_VALUE_HEADS + kv] = jnp.exp2((scores - row_max) * scale).astype(jnp.bfloat16)


def values_kernel(runs, pos_ref, weights_ref, sorted_ref, *refs):
    tagged_refs, last_refs, (out_ref, result_buf, out_sems) = refs[:-5], refs[-5:-3], refs[-3:]
    reach = runs // 4
    numbers = run_numbers(runs, pos_ref, tagged_refs)
    ones = jnp.ones(((reach + 1) * RUN, HEAD_SIZE), jnp.bfloat16)
    copies = []
    for half in range(2):
        start = jnp.maximum(numbers[0][half] - reach, 0)
        for kv in range(KEY_VALUE_HEADS):
            last_ref = last_refs[kv * 2 // KEY_VALUE_HEADS]
            parts = []
            for i in range(reach + 1):
                part = sorted_ref[kv, start + i]
                for last_half, number in enumerate(numbers[-1]):
                    row = kv % (KEY_VALUE_HEADS // 2) * TOK_DEV + last_half * RUN
                    part = jnp.where(start + i == number, last_ref[row : row + RUN, :], part)
                parts.append(part)
            summed = jnp.dot(
                weights_ref[half * KEY_VALUE_HEADS + kv],
                jnp.concatenate([jnp.concatenate(parts, axis=0), ones], axis=1),
                preferred_element_type=jnp.float32,
            )
            result = (summed[:, :HEAD_SIZE] / summed[:, HEAD_SIZE:]).astype(jnp.bfloat16)
            for i in range(GROUP):
                h = kv * GROUP + i
                result_buf[half, :, h * HEAD_SIZE : (h + 1) * HEAD_SIZE] = result[i * RUN : (i + 1) * RUN]
        copies.append(
            pltpu.make_async_copy(result_buf.at[half], out_ref.at[pl.ds(half * RUN, RUN), :], out_sems.at[half])
        )
        copies[-1].start()
    for copy in copies:
        copy.wait()


def per_device(queries, keys, values, token_pos, segment):
    sections, places = lax.axis_size("section"), lax.axis_size("ctx")
    runs = segment.shape[0] // RUN
    depth = places // 2
    ring = [z * 2 for z in range(depth)] + [z * 2 + 1 for z in reversed(range(depth))]

    def shift(block, section_by, ring_by):
        pairs = []
        for s in range(sections):
            for i in range(places):
                target = (s + section_by) % sections * places + ring[(i + ring_by) % places]
                pairs.append((s * places + ring[i], target))
        return lax.ppermute(block, ("section", "ctx"), pairs)

    def around(block, rows, before_last=None):
        ahead, back = shift(block, 1, 1), shift(block, 1, -1)
        held = [ahead, back]
        for _ in range(2, places // 2):
            ahead, back = shift(ahead, 0, 1), shift(back, 0, -1)
            held.extend([ahead, back])
        if before_last is not None:
            ahead, _ = lax.optimization_barrier((ahead, before_last))
        return held + [shift(ahead[: rows // 2], 0, 1), shift(back[rows // 2 : rows], 0, -1)]

    own = shift(jnp.concatenate([queries[0], keys[0], values[0]], axis=1), 1, 0)
    vmem = pl.BlockSpec(memory_space=pltpu.VMEM)
    blank = pl.pallas_call(
        blank_kernel,
        out_shape=jax.ShapeDtypeStruct((TAG_ROWS, TOK_DEV), jnp.bfloat16),
        out_specs=vmem,
        compiler_params=pltpu.CompilerParams(vmem_limit_bytes=8 * 1024 * 1024),
        cost_estimate=pl.CostEstimate(flops=1 << 30, bytes_accessed=0, transcendentals=0),
    )()
    tag = (token_pos >> (RUN.bit_length() - 1)).astype(jnp.bfloat16)
    by_head = [values[0, :, kv * HEAD_SIZE : (kv + 1) * HEAD_SIZE] for kv in range(KEY_VALUE_HEADS)]
    tagged = jnp.concatenate([*by_head, blank + tag[None]], axis=0)
    pos = lax.optimization_barrier(jnp.concatenate([token_pos, segment]).astype(jnp.float32)[None])
    bias = pl.pallas_call(
        functools.partial(bias_kernel, runs),
        out_shape=jax.ShapeDtypeStruct((2, RUN, (runs // 4 + 1) * RUN), jnp.float32),
        in_specs=[vmem],
        out_specs=vmem,
        compiler_params=pltpu.CompilerParams(vmem_limit_bytes=8 * 1024 * 1024),
        cost_estimate=pl.CostEstimate(flops=1 << 20, bytes_accessed=1 << 10, transcendentals=0),
    )(pos)
    all_keys = around(keys[0], TOK_DEV)
    all_values = around(tagged, VALUE_ROWS, bias)
    params = pltpu.CompilerParams(vmem_limit_bytes=(12 + runs // 4) * 1024 * 1024)
    mark = pl.pallas_call(
        blank_kernel,
        out_shape=jax.ShapeDtypeStruct((8, HEAD_SIZE), jnp.float32),
        in_specs=[vmem] * 2,
        out_specs=vmem,
        compiler_params=pltpu.CompilerParams(vmem_limit_bytes=8 * 1024 * 1024),
        cost_estimate=pl.CostEstimate(flops=35 << 28, bytes_accessed=0, transcendentals=0),
    )(*all_keys[-2:])
    weights, sorted_values = pl.pallas_call(
        functools.partial(weights_kernel, runs),
        out_shape=(
            jax.ShapeDtypeStruct((2 * KEY_VALUE_HEADS, GROUP * RUN, (runs // 4 + 1) * RUN), jnp.bfloat16),
            jax.ShapeDtypeStruct((KEY_VALUE_HEADS, runs, RUN, HEAD_SIZE), jnp.bfloat16),
        ),
        in_specs=[vmem] * (4 + len(all_keys) + len(all_values[:-2])),
        out_specs=(vmem,) * 2,
        scratch_shapes=[pltpu.VMEM((runs, RUN, KV_COLUMNS), jnp.bfloat16)],
        compiler_params=params,
        cost_estimate=pl.CostEstimate(flops=1 << 26, bytes_accessed=1 << 20, transcendentals=0),
    )(pos, bias, mark, own, *all_keys, *all_values[:-2])
    out = pl.pallas_call(
        functools.partial(values_kernel, runs),
        out_shape=jax.ShapeDtypeStruct((TOK_DEV, QUERY_COLUMNS), jnp.bfloat16),
        in_specs=[vmem] * (3 + len(all_values)),
        out_specs=pl.BlockSpec(memory_space=pl.ANY),
        scratch_shapes=[
            pltpu.VMEM((2, RUN, QUERY_COLUMNS), jnp.bfloat16),
            pltpu.SemaphoreType.DMA((2,)),
        ],
        compiler_params=params,
        cost_estimate=pl.CostEstimate(flops=1 << 26, bytes_accessed=1 << 20, transcendentals=0),
    )(pos, weights, sorted_values, *all_values)
    return out[None]


def solution(mesh):
    return jax.shard_map(
        per_device,
        mesh=mesh,
        in_specs=(
            P("section", "ctx", None),
            P("section", "ctx", None),
            P("section", "ctx", None),
            P("ctx"),
            P(),
        ),
        out_specs=P("section", "ctx", None),
        check_vma=False,
    )
```

```python
import functools
import math

import jax
import jax.numpy as jnp
from jax import lax
from jax.experimental import pallas as pl
from jax.experimental.pallas import tpu as pltpu
from jax.sharding import PartitionSpec as P

HEAD_SIZE = 128
QUERY_HEADS = 32
KEY_VALUE_HEADS = 4
GROUP = QUERY_HEADS // KEY_VALUE_HEADS
RUN = 64
TOK_DEV = 2 * RUN
QUERY_COLUMNS = QUERY_HEADS * HEAD_SIZE
KV_COLUMNS = KEY_VALUE_HEADS * HEAD_SIZE
TAG_ROWS = 16
VALUE_ROWS = KEY_VALUE_HEADS * TOK_DEV

masked_fill = -1e30


def first_run(pos_ref):
    return lax.div(jnp.min(pos_ref[:, :TOK_DEV]).astype(jnp.int32), RUN)


def first_in_reach(runs, pos_ref, run):
    reach = runs // 4
    segment = pos_ref[:, TOK_DEV:]
    position = lax.broadcasted_iota(jnp.int32, segment.shape, 1)
    doc = jnp.max(jnp.where(position == run * RUN, segment, -1.0))
    far_doc = jnp.max(jnp.where(position == (run - reach + 1) * RUN - 1, segment, -1.0))
    far = doc == far_doc
    return jnp.where(far, run - reach, jnp.maximum(run - reach + 1, 0)), far


def run_numbers(runs, pos_ref, tagged_refs):
    firsts = [first_run(pos_ref)]
    for ref in tagged_refs:
        firsts.append(jnp.min(ref[VALUE_ROWS:, :].astype(jnp.float32)).astype(jnp.int32))
    places = runs // 2
    firsts.append(places * (places - 1) // 2 - sum(firsts))
    return [(first, runs - 1 - first) for first in firsts]


def sort_keys(numbers, own_ref, block_refs, last_refs, sorted_ref):
    for half, number in enumerate(numbers[0]):
        sorted_ref[number] = own_ref[half * RUN : (half + 1) * RUN, QUERY_COLUMNS : QUERY_COLUMNS + KV_COLUMNS]
    for (first, second), ref in zip(numbers[1:], block_refs):
        sorted_ref[first] = ref[:RUN, :]
        sorted_ref[second] = ref[RUN:, :]
    for number, ref in zip(numbers[-1], last_refs):
        sorted_ref[number] = ref[...]


def sort_values(numbers, own_ref, block_refs, sorted_ref):
    for kv in range(KEY_VALUE_HEADS):
        column = QUERY_COLUMNS + KV_COLUMNS + kv * HEAD_SIZE
        for half, number in enumerate(numbers[0]):
            sorted_ref[kv, number] = own_ref[half * RUN : (half + 1) * RUN, column : column + HEAD_SIZE]
        for pair, ref in zip(numbers[1:], block_refs):
            for half, number in enumerate(pair):
                row = kv * TOK_DEV + half * RUN
                sorted_ref[kv, number] = ref[row : row + RUN, :]


def blank_kernel(*refs):
    refs[-1][...] = jnp.zeros_like(refs[-1])


def bias_kernel(runs, pos_ref, bias_ref):
    segment = pos_ref[:, TOK_DEV:]
    first = first_run(pos_ref)
    for half, run in enumerate((first, runs - 1 - first)):
        row_pos = run * RUN + lax.broadcasted_iota(jnp.int32, (RUN, 1), 0)
        at = lax.broadcasted_iota(jnp.int32, (RUN, runs * RUN), 1) == row_pos
        row_doc = jnp.sum(jnp.where(at, segment, 0.0), axis=1, keepdims=True)
        doc_start = jnp.sum(jnp.where(segment < row_doc, 1.0, 0.0), axis=1, keepdims=True).astype(jnp.int32)
        start, _ = first_in_reach(runs, pos_ref, run)
        key_pos = start * RUN + lax.broadcasted_iota(jnp.int32, bias_ref.shape[1:], 1)
        bias_ref[half] = jnp.where((key_pos <= row_pos) & (key_pos >= doc_start), 0.0, masked_fill)


def weights_kernel(runs, pos_ref, bias_ref, mark_ref, own_ref, *refs):
    blocks = runs // 2
    key_refs, tagged_refs = refs[:blocks], refs[blocks:-3]
    weights_ref, sorted_ref, key_buf = refs[-3:]
    numbers = run_numbers(runs, pos_ref, tagged_refs)
    sort_keys(numbers, own_ref, key_refs[:-2], key_refs[-2:], key_buf)
    sort_values(numbers, own_ref, tagged_refs, sorted_ref)
    scale = math.log2(math.e) / math.sqrt(HEAD_SIZE)

    def half_weights(half, start, count):
        span = count * RUN
        bias = jnp.concatenate([bias_ref[half, :, :span]] * GROUP, axis=0)
        for kv in range(KEY_VALUE_HEADS):
            query = jnp.concatenate(
                [
                    own_ref[half * RUN : (half + 1) * RUN, h * HEAD_SIZE : (h + 1) * HEAD_SIZE]
                    for h in range(kv * GROUP, (kv + 1) * GROUP)
                ],
                axis=0,
            )
            key = key_buf[pl.ds(start, count), :, kv * HEAD_SIZE : (kv + 1) * HEAD_SIZE]
            scores = bias + lax.dot_general(
                query,
                key.reshape(span, HEAD_SIZE),
                (((1,), (1,)), ((), ())),
                preferred_element_type=jnp.float32,
            )
            row_max = jnp.max(scores, axis=1, keepdims=True)
            weights = jnp.exp2((scores - row_max) * scale).astype(jnp.bfloat16)
            weights_ref[half * KEY_VALUE_HEADS + kv, :, :span] = weights

    for half in range(2):
        start, far = first_in_reach(runs, pos_ref, numbers[0][half])
        pl.when(far)(functools.partial(half_weights, half, start, runs // 4 + 1))
        pl.when(jnp.logical_not(far))(functools.partial(half_weights, half, start, runs // 4))


def values_kernel(runs, pos_ref, weights_ref, sorted_ref, *refs):
    tagged_refs, last_refs, (out_ref, result_buf, out_sems) = refs[:-5], refs[-5:-3], refs[-3:]
    numbers = run_numbers(runs, pos_ref, tagged_refs)

    def half_values(half, start, count):
        ones = jnp.ones((count * RUN, HEAD_SIZE), jnp.bfloat16)
        for kv in range(KEY_VALUE_HEADS):
            last_ref = last_refs[kv * 2 // KEY_VALUE_HEADS]
            parts = []
            for i in range(count):
                part = sorted_ref[kv, start + i]
                for last_half, number in enumerate(numbers[-1]):
                    row = kv % (KEY_VALUE_HEADS // 2) * TOK_DEV + last_half * RUN
                    part = jnp.where(start + i == number, last_ref[row : row + RUN, :], part)
                parts.append(part)
            summed = jnp.dot(
                weights_ref[half * KEY_VALUE_HEADS + kv, :, : count * RUN],
                jnp.concatenate([jnp.concatenate(parts, axis=0), ones], axis=1),
                preferred_element_type=jnp.float32,
            )
            result = (summed[:, :HEAD_SIZE] / summed[:, HEAD_SIZE:]).astype(jnp.bfloat16)
            for i in range(GROUP):
                h = kv * GROUP + i
                result_buf[half, :, h * HEAD_SIZE : (h + 1) * HEAD_SIZE] = result[i * RUN : (i + 1) * RUN]

    copies = []
    for half in range(2):
        start, far = first_in_reach(runs, pos_ref, numbers[0][half])
        pl.when(far)(functools.partial(half_values, half, start, runs // 4 + 1))
        pl.when(jnp.logical_not(far))(functools.partial(half_values, half, start, runs // 4))
        copies.append(
            pltpu.make_async_copy(result_buf.at[half], out_ref.at[pl.ds(half * RUN, RUN), :], out_sems.at[half])
        )
        copies[-1].start()
    for copy in copies:
        copy.wait()


def per_device(queries, keys, values, token_pos, segment):
    sections, places = lax.axis_size("section"), lax.axis_size("ctx")
    runs = segment.shape[0] // RUN
    depth = places // 2
    ring = [z * 2 for z in range(depth)] + [z * 2 + 1 for z in reversed(range(depth))]

    def shift(block, section_by, ring_by):
        pairs = []
        for s in range(sections):
            for i in range(places):
                target = (s + section_by) % sections * places + ring[(i + ring_by) % places]
                pairs.append((s * places + ring[i], target))
        return lax.ppermute(block, ("section", "ctx"), pairs)

    def around(block, rows, before_last=None):
        ahead, back = shift(block, 1, 1), shift(block, 1, -1)
        held = [ahead, back]
        for _ in range(2, places // 2):
            ahead, back = shift(ahead, 0, 1), shift(back, 0, -1)
            held.extend([ahead, back])
        if before_last is not None:
            ahead, _ = lax.optimization_barrier((ahead, before_last))
        return held + [shift(ahead[: rows // 2], 0, 1), shift(back[rows // 2 : rows], 0, -1)]

    own = shift(jnp.concatenate([queries[0], keys[0], values[0]], axis=1), 1, 0)
    vmem = pl.BlockSpec(memory_space=pltpu.VMEM)
    blank = pl.pallas_call(
        blank_kernel,
        out_shape=jax.ShapeDtypeStruct((TAG_ROWS, TOK_DEV), jnp.bfloat16),
        out_specs=vmem,
        compiler_params=pltpu.CompilerParams(vmem_limit_bytes=8 * 1024 * 1024),
        cost_estimate=pl.CostEstimate(flops=1 << 30, bytes_accessed=0, transcendentals=0),
    )()
    tag = (token_pos >> (RUN.bit_length() - 1)).astype(jnp.bfloat16)
    by_head = [values[0, :, kv * HEAD_SIZE : (kv + 1) * HEAD_SIZE] for kv in range(KEY_VALUE_HEADS)]
    tagged = jnp.concatenate([*by_head, blank + tag[None]], axis=0)
    pos = lax.optimization_barrier(jnp.concatenate([token_pos, segment]).astype(jnp.float32)[None])
    bias = pl.pallas_call(
        functools.partial(bias_kernel, runs),
        out_shape=jax.ShapeDtypeStruct((2, RUN, (runs // 4 + 1) * RUN), jnp.float32),
        in_specs=[vmem],
        out_specs=vmem,
        compiler_params=pltpu.CompilerParams(vmem_limit_bytes=8 * 1024 * 1024),
        cost_estimate=pl.CostEstimate(flops=1 << 20, bytes_accessed=1 << 10, transcendentals=0),
    )(pos)
    all_keys = around(keys[0], TOK_DEV)
    all_values = around(tagged, VALUE_ROWS, bias)
    params = pltpu.CompilerParams(vmem_limit_bytes=(12 + runs // 4) * 1024 * 1024)
    mark = pl.pallas_call(
        blank_kernel,
        out_shape=jax.ShapeDtypeStruct((8, HEAD_SIZE), jnp.float32),
        in_specs=[vmem] * 2,
        out_specs=vmem,
        compiler_params=pltpu.CompilerParams(vmem_limit_bytes=8 * 1024 * 1024),
        cost_estimate=pl.CostEstimate(flops=65 << 27, bytes_accessed=0, transcendentals=0),
    )(*all_keys[-2:])
    weights, sorted_values = pl.pallas_call(
        functools.partial(weights_kernel, runs),
        out_shape=(
            jax.ShapeDtypeStruct((2 * KEY_VALUE_HEADS, GROUP * RUN, (runs // 4 + 1) * RUN), jnp.bfloat16),
            jax.ShapeDtypeStruct((KEY_VALUE_HEADS, runs, RUN, HEAD_SIZE), jnp.bfloat16),
        ),
        in_specs=[vmem] * (4 + len(all_keys) + len(all_values[:-2])),
        out_specs=(vmem,) * 2,
        scratch_shapes=[pltpu.VMEM((runs, RUN, KV_COLUMNS), jnp.bfloat16)],
        compiler_params=params,
        cost_estimate=pl.CostEstimate(flops=1 << 26, bytes_accessed=1 << 20, transcendentals=0),
    )(pos, bias, mark, own, *all_keys, *all_values[:-2])
    out = pl.pallas_call(
        functools.partial(values_kernel, runs),
        out_shape=jax.ShapeDtypeStruct((TOK_DEV, QUERY_COLUMNS), jnp.bfloat16),
        in_specs=[vmem] * (3 + len(all_values)),
        out_specs=pl.BlockSpec(memory_space=pl.ANY),
        scratch_shapes=[
            pltpu.VMEM((2, RUN, QUERY_COLUMNS), jnp.bfloat16),
            pltpu.SemaphoreType.DMA((2,)),
        ],
        compiler_params=params,
        cost_estimate=pl.CostEstimate(flops=1 << 26, bytes_accessed=1 << 20, transcendentals=0),
    )(pos, weights, sorted_values, *all_values)
    return out[None]


def solution(mesh):
    return jax.shard_map(
        per_device,
        mesh=mesh,
        in_specs=(
            P("section", "ctx", None),
            P("section", "ctx", None),
            P("section", "ctx", None),
            P("ctx"),
            P(),
        ),
        out_specs=P("section", "ctx", None),
        check_vma=False,
    )
```

```python
import functools
import math

import jax
import jax.numpy as jnp
from jax import lax
from jax.experimental import pallas as pl
from jax.experimental.pallas import tpu as pltpu
from jax.sharding import PartitionSpec as P

HEAD_SIZE = 128
QUERY_HEADS = 32
KEY_VALUE_HEADS = 4
GROUP = QUERY_HEADS // KEY_VALUE_HEADS
RUN = 64
TOK_DEV = 2 * RUN
QUERY_COLUMNS = QUERY_HEADS * HEAD_SIZE
KV_COLUMNS = KEY_VALUE_HEADS * HEAD_SIZE
TAG_ROWS = 16
VALUE_ROWS = KEY_VALUE_HEADS * TOK_DEV

masked_fill = -1e30


def first_run(pos_ref):
    return lax.div(pos_ref[:, :TOK_DEV][0, 0].astype(jnp.int32), RUN)


def first_in_reach(runs, pos_ref, run):
    reach = runs // 4
    segment = pos_ref[:, TOK_DEV:]
    position = lax.broadcasted_iota(jnp.int32, segment.shape, 1)
    doc = jnp.max(jnp.where(position == run * RUN, segment, -1.0))
    far_doc = jnp.max(jnp.where(position == (run - reach + 1) * RUN - 1, segment, -1.0))
    far = doc == far_doc
    return jnp.where(far, run - reach, jnp.maximum(run - reach + 1, 0)), far


def run_numbers(runs, pos_ref, tagged_refs):
    firsts = [first_run(pos_ref)]
    for ref in tagged_refs:
        firsts.append(ref[VALUE_ROWS:, :].astype(jnp.float32)[0, 0].astype(jnp.int32))
    places = runs // 2
    firsts.append(places * (places - 1) // 2 - sum(firsts))
    return [(first, runs - 1 - first) for first in firsts]


def sort_keys(numbers, own_ref, block_refs, last_refs, sorted_ref):
    for half, number in enumerate(numbers[0]):
        sorted_ref[number] = own_ref[half * RUN : (half + 1) * RUN, QUERY_COLUMNS : QUERY_COLUMNS + KV_COLUMNS]
    for (first, second), ref in zip(numbers[1:], block_refs):
        sorted_ref[first] = ref[:RUN, :]
        sorted_ref[second] = ref[RUN:, :]
    for number, ref in zip(numbers[-1], last_refs):
        sorted_ref[number] = ref[...]


def sort_values(numbers, own_ref, block_refs, sorted_ref):
    for kv in range(KEY_VALUE_HEADS):
        column = QUERY_COLUMNS + KV_COLUMNS + kv * HEAD_SIZE
        for half, number in enumerate(numbers[0]):
            sorted_ref[kv, number] = own_ref[half * RUN : (half + 1) * RUN, column : column + HEAD_SIZE]
        for pair, ref in zip(numbers[1:], block_refs):
            for half, number in enumerate(pair):
                row = kv * TOK_DEV + half * RUN
                sorted_ref[kv, number] = ref[row : row + RUN, :]


def blank_kernel(*refs):
    refs[-1][...] = jnp.zeros_like(refs[-1])


def bias_kernel(runs, pos_ref, bias_ref):
    segment = pos_ref[:, TOK_DEV:]
    first = first_run(pos_ref)
    for half, run in enumerate((first, runs - 1 - first)):
        row_pos = run * RUN + lax.broadcasted_iota(jnp.int32, (RUN, 1), 0)
        at = lax.broadcasted_iota(jnp.int32, (RUN, runs * RUN), 1) == row_pos
        row_doc = jnp.sum(jnp.where(at, segment, 0.0), axis=1, keepdims=True)
        doc_start = jnp.sum(jnp.where(segment < row_doc, 1.0, 0.0), axis=1, keepdims=True).astype(jnp.int32)
        start, _ = first_in_reach(runs, pos_ref, run)
        key_pos = start * RUN + lax.broadcasted_iota(jnp.int32, bias_ref.shape[1:], 1)
        bias_ref[half] = jnp.where((key_pos <= row_pos) & (key_pos >= doc_start), 0.0, masked_fill)


def weights_kernel(runs, pos_ref, bias_ref, mark_ref, own_ref, *refs):
    blocks = runs // 2
    key_refs, tagged_refs = refs[:blocks], refs[blocks:-3]
    weights_ref, sorted_ref, key_buf = refs[-3:]
    numbers = run_numbers(runs, pos_ref, tagged_refs)
    sort_keys(numbers, own_ref, key_refs[:-2], key_refs[-2:], key_buf)
    sort_values(numbers, own_ref, tagged_refs, sorted_ref)
    scale = math.log2(math.e) / math.sqrt(HEAD_SIZE)

    def half_weights(half, start, count):
        span = count * RUN
        bias = jnp.concatenate([bias_ref[half, :, :span]] * GROUP, axis=0)
        for kv in range(KEY_VALUE_HEADS):
            query = jnp.concatenate(
                [
                    own_ref[half * RUN : (half + 1) * RUN, h * HEAD_SIZE : (h + 1) * HEAD_SIZE]
                    for h in range(kv * GROUP, (kv + 1) * GROUP)
                ],
                axis=0,
            )
            key = key_buf[pl.ds(start, count), :, kv * HEAD_SIZE : (kv + 1) * HEAD_SIZE]
            scores = bias + lax.dot_general(
                query,
                key.reshape(span, HEAD_SIZE),
                (((1,), (1,)), ((), ())),
                preferred_element_type=jnp.float32,
            )
            row_max = jnp.max(scores, axis=1, keepdims=True)
            weights = jnp.exp2((scores - row_max) * scale).astype(jnp.bfloat16)
            weights_ref[half * KEY_VALUE_HEADS + kv, :, :span] = weights

    for half in range(2):
        start, far = first_in_reach(runs, pos_ref, numbers[0][half])
        pl.when(far)(functools.partial(half_weights, half, start, runs // 4 + 1))
        pl.when(jnp.logical_not(far))(functools.partial(half_weights, half, start, runs // 4))


def values_kernel(runs, pos_ref, weights_ref, sorted_ref, *refs):
    tagged_refs, (last_ref, out_ref, result_buf, out_sems) = refs[:-4], refs[-4:]
    numbers = run_numbers(runs, pos_ref, tagged_refs)

    def half_values(half, start, count):
        ones = jnp.ones((count * RUN, HEAD_SIZE), jnp.bfloat16)
        for kv in range(KEY_VALUE_HEADS):
            parts = []
            for i in range(count):
                part = sorted_ref[kv, start + i]
                for last_half, number in enumerate(numbers[-1]):
                    row = kv * TOK_DEV + last_half * RUN
                    part = jnp.where(start + i == number, last_ref[row : row + RUN, :], part)
                parts.append(part)
            summed = jnp.dot(
                weights_ref[half * KEY_VALUE_HEADS + kv, :, : count * RUN],
                jnp.concatenate([jnp.concatenate(parts, axis=0), ones], axis=1),
                preferred_element_type=jnp.float32,
            )
            total = summed[:, HEAD_SIZE:]
            inverse = pl.reciprocal(total, approx=True)
            inverse = inverse * (2.0 - total * inverse)
            result = (summed[:, :HEAD_SIZE] * inverse).astype(jnp.bfloat16)
            for i in range(GROUP):
                h = kv * GROUP + i
                result_buf[half, :, h * HEAD_SIZE : (h + 1) * HEAD_SIZE] = result[i * RUN : (i + 1) * RUN]

    copies = []
    for half in range(2):
        start, far = first_in_reach(runs, pos_ref, numbers[0][half])
        pl.when(far)(functools.partial(half_values, half, start, runs // 4 + 1))
        pl.when(jnp.logical_not(far))(functools.partial(half_values, half, start, runs // 4))
        copies.append(
            pltpu.make_async_copy(result_buf.at[half], out_ref.at[pl.ds(half * RUN, RUN), :], out_sems.at[half])
        )
        copies[-1].start()
    for copy in copies:
        copy.wait()


def per_device(queries, keys, values, token_pos, segment):
    sections, places = lax.axis_size("section"), lax.axis_size("ctx")
    runs = segment.shape[0] // RUN
    depth = places // 2
    ring = [z * 2 for z in range(depth)] + [z * 2 + 1 for z in reversed(range(depth))]

    def shift(block, section_by, ring_by):
        pairs = []
        for s in range(sections):
            for i in range(places):
                target = (s + section_by) % sections * places + ring[(i + ring_by) % places]
                pairs.append((s * places + ring[i], target))
        return lax.ppermute(block, ("section", "ctx"), pairs)

    def around(block):
        ahead, back = shift(block, 1, 1), shift(block, 1, -1)
        held = [ahead, back]
        for _ in range(2, places // 2):
            ahead, back = shift(ahead, 0, 1), shift(back, 0, -1)
            held.extend([ahead, back])
        return held

    own = shift(jnp.concatenate([queries[0], keys[0], values[0]], axis=1), 1, 0)
    vmem = pl.BlockSpec(memory_space=pltpu.VMEM)
    blank = pl.pallas_call(
        blank_kernel,
        out_shape=jax.ShapeDtypeStruct((TAG_ROWS, TOK_DEV), jnp.bfloat16),
        out_specs=vmem,
        compiler_params=pltpu.CompilerParams(vmem_limit_bytes=8 * 1024 * 1024),
        cost_estimate=pl.CostEstimate(flops=1 << 30, bytes_accessed=0, transcendentals=0),
    )()
    tag = (token_pos >> (RUN.bit_length() - 1)).astype(jnp.bfloat16)
    by_head = [values[0, :, kv * HEAD_SIZE : (kv + 1) * HEAD_SIZE] for kv in range(KEY_VALUE_HEADS)]
    tagged = jnp.concatenate([*by_head, blank + tag[None]], axis=0)
    pos = lax.optimization_barrier(jnp.concatenate([token_pos, segment]).astype(jnp.float32)[None])
    bias = pl.pallas_call(
        functools.partial(bias_kernel, runs),
        out_shape=jax.ShapeDtypeStruct((2, RUN, (runs // 4 + 1) * RUN), jnp.float32),
        in_specs=[vmem],
        out_specs=vmem,
        compiler_params=pltpu.CompilerParams(vmem_limit_bytes=8 * 1024 * 1024),
        cost_estimate=pl.CostEstimate(flops=1 << 20, bytes_accessed=1 << 10, transcendentals=0),
    )(pos)
    all_keys, all_values = around(keys[0]), around(tagged)
    ahead, back = all_keys[-2:]
    all_keys.extend([shift(ahead[:RUN], 0, 1), shift(back[RUN:], 0, -1)])
    ahead, back, _ = lax.optimization_barrier((*all_values[-2:], bias))
    all_values.append(shift(back[:VALUE_ROWS], 0, -1))
    params = pltpu.CompilerParams(vmem_limit_bytes=(12 + runs // 4) * 1024 * 1024)
    mark = pl.pallas_call(
        blank_kernel,
        out_shape=jax.ShapeDtypeStruct((8, HEAD_SIZE), jnp.float32),
        in_specs=[vmem] * 2,
        out_specs=vmem,
        compiler_params=pltpu.CompilerParams(vmem_limit_bytes=8 * 1024 * 1024),
        cost_estimate=pl.CostEstimate(flops=65 << 27, bytes_accessed=0, transcendentals=0),
    )(*all_keys[-2:])
    weights, sorted_values = pl.pallas_call(
        functools.partial(weights_kernel, runs),
        out_shape=(
            jax.ShapeDtypeStruct((2 * KEY_VALUE_HEADS, GROUP * RUN, (runs // 4 + 1) * RUN), jnp.bfloat16),
            jax.ShapeDtypeStruct((KEY_VALUE_HEADS, runs, RUN, HEAD_SIZE), jnp.bfloat16),
        ),
        in_specs=[vmem] * (4 + len(all_keys) + len(all_values[:-1])),
        out_specs=(vmem,) * 2,
        scratch_shapes=[pltpu.VMEM((runs, RUN, KV_COLUMNS), jnp.bfloat16)],
        compiler_params=params,
        cost_estimate=pl.CostEstimate(flops=1 << 26, bytes_accessed=1 << 20, transcendentals=0),
    )(pos, bias, mark, own, *all_keys, *all_values[:-1])
    out = pl.pallas_call(
        functools.partial(values_kernel, runs),
        out_shape=jax.ShapeDtypeStruct((TOK_DEV, QUERY_COLUMNS), jnp.bfloat16),
        in_specs=[vmem] * (3 + len(all_values)),
        out_specs=pl.BlockSpec(memory_space=pl.ANY),
        scratch_shapes=[
            pltpu.VMEM((2, RUN, QUERY_COLUMNS), jnp.bfloat16),
            pltpu.SemaphoreType.DMA((2,)),
        ],
        compiler_params=params,
        cost_estimate=pl.CostEstimate(flops=1 << 26, bytes_accessed=1 << 20, transcendentals=0),
    )(pos, weights, sorted_values, *all_values)
    return out[None]


def solution(mesh):
    return jax.shard_map(
        per_device,
        mesh=mesh,
        in_specs=(
            P("section", "ctx", None),
            P("section", "ctx", None),
            P("section", "ctx", None),
            P("ctx"),
            P(),
        ),
        out_specs=P("section", "ctx", None),
        check_vma=False,
    )
```

```python
import functools
import math

import jax
import jax.numpy as jnp
from jax import lax
from jax.experimental import pallas as pl
from jax.experimental.pallas import tpu as pltpu
from jax.sharding import PartitionSpec as P

HEAD_SIZE = 128
QUERY_HEADS = 32
KEY_VALUE_HEADS = 4
GROUP = QUERY_HEADS // KEY_VALUE_HEADS
RUN = 64
TOK_DEV = 2 * RUN
QUERY_COLUMNS = QUERY_HEADS * HEAD_SIZE
KV_COLUMNS = KEY_VALUE_HEADS * HEAD_SIZE
TAG_ROWS = 16
VALUE_ROWS = KEY_VALUE_HEADS * TOK_DEV

masked_fill = -1e30


def first_run(pos_ref):
    return lax.div(pos_ref[:, :TOK_DEV][0, 0].astype(jnp.int32), RUN)


def first_in_reach(runs, pos_ref, run):
    reach = runs // 4
    segment = pos_ref[:, TOK_DEV:]
    position = lax.broadcasted_iota(jnp.int32, segment.shape, 1)
    doc = jnp.max(jnp.where(position == run * RUN, segment, -1.0))
    far_doc = jnp.max(jnp.where(position == (run - reach + 1) * RUN - 1, segment, -1.0))
    far = doc == far_doc
    return jnp.where(far, run - reach, jnp.maximum(run - reach + 1, 0)), far


def run_numbers(runs, pos_ref, tagged_refs):
    firsts = [first_run(pos_ref)]
    for ref in tagged_refs:
        firsts.append(ref[VALUE_ROWS:, :].astype(jnp.float32)[0, 0].astype(jnp.int32))
    places = runs // 2
    firsts.append(places * (places - 1) // 2 - sum(firsts))
    return [(first, runs - 1 - first) for first in firsts]


def sort_keys(numbers, own_ref, block_refs, last_refs, sorted_ref):
    for half, number in enumerate(numbers[0]):
        sorted_ref[number] = own_ref[half * RUN : (half + 1) * RUN, QUERY_COLUMNS : QUERY_COLUMNS + KV_COLUMNS]
    for (first, second), ref in zip(numbers[1:], block_refs):
        sorted_ref[first] = ref[:RUN, :]
        sorted_ref[second] = ref[RUN:, :]
    for number, ref in zip(numbers[-1], last_refs):
        sorted_ref[number] = ref[...]


def sort_values(numbers, own_ref, block_refs, sorted_ref):
    for kv in range(KEY_VALUE_HEADS):
        column = QUERY_COLUMNS + KV_COLUMNS + kv * HEAD_SIZE
        for half, number in enumerate(numbers[0]):
            sorted_ref[kv, number] = own_ref[half * RUN : (half + 1) * RUN, column : column + HEAD_SIZE]
        for pair, ref in zip(numbers[1:], block_refs):
            for half, number in enumerate(pair):
                row = kv * TOK_DEV + half * RUN
                sorted_ref[kv, number] = ref[row : row + RUN, :]


def blank_kernel(*refs):
    refs[-1][...] = jnp.zeros_like(refs[-1])


def bias_kernel(runs, pos_ref, bias_ref):
    segment = pos_ref[:, TOK_DEV:]
    first = first_run(pos_ref)
    for half, run in enumerate((first, runs - 1 - first)):
        row_pos = run * RUN + lax.broadcasted_iota(jnp.int32, (RUN, 1), 0)
        at = lax.broadcasted_iota(jnp.int32, (RUN, runs * RUN), 1) == row_pos
        row_doc = jnp.sum(jnp.where(at, segment, 0.0), axis=1, keepdims=True)
        doc_start = jnp.sum(jnp.where(segment < row_doc, 1.0, 0.0), axis=1, keepdims=True).astype(jnp.int32)
        start, _ = first_in_reach(runs, pos_ref, run)
        key_pos = start * RUN + lax.broadcasted_iota(jnp.int32, bias_ref.shape[1:], 1)
        bias_ref[half] = jnp.where((key_pos <= row_pos) & (key_pos >= doc_start), 0.0, masked_fill)


def weights_kernel(runs, pos_ref, bias_ref, mark_ref, own_ref, *refs):
    blocks = runs // 2
    key_refs, tagged_refs = refs[:blocks], refs[blocks:-3]
    weights_ref, sorted_ref, key_buf = refs[-3:]
    numbers = run_numbers(runs, pos_ref, tagged_refs)
    sort_keys(numbers, own_ref, key_refs[:-2], key_refs[-2:], key_buf)
    sort_values(numbers, own_ref, tagged_refs, sorted_ref)
    scale = math.log2(math.e) / math.sqrt(HEAD_SIZE)

    def half_weights(half, start, count):
        span = count * RUN
        bias = jnp.concatenate([bias_ref[half, :, :span]] * GROUP, axis=0)
        for kv in range(KEY_VALUE_HEADS):
            query = jnp.concatenate(
                [
                    own_ref[half * RUN : (half + 1) * RUN, h * HEAD_SIZE : (h + 1) * HEAD_SIZE]
                    for h in range(kv * GROUP, (kv + 1) * GROUP)
                ],
                axis=0,
            )
            key = key_buf[pl.ds(start, count), :, kv * HEAD_SIZE : (kv + 1) * HEAD_SIZE]
            scores = bias + lax.dot_general(
                query,
                key.reshape(span, HEAD_SIZE),
                (((1,), (1,)), ((), ())),
                preferred_element_type=jnp.float32,
            )
            row_max = jnp.max(scores, axis=1, keepdims=True)
            weights = jnp.exp2((scores - row_max) * scale).astype(jnp.bfloat16)
            weights_ref[half * KEY_VALUE_HEADS + kv, :, :span] = weights

    for half in range(2):
        start, far = first_in_reach(runs, pos_ref, numbers[0][half])
        pl.when(far)(functools.partial(half_weights, half, start, runs // 4 + 1))
        pl.when(jnp.logical_not(far))(functools.partial(half_weights, half, start, runs // 4))


def values_kernel(runs, pos_ref, weights_ref, sorted_ref, *refs):
    tagged_refs, last_refs, (out_ref, result_buf, out_sems) = refs[:-5], refs[-5:-3], refs[-3:]
    numbers = run_numbers(runs, pos_ref, tagged_refs)

    def half_values(half, start, count):
        ones = jnp.ones((count * RUN, HEAD_SIZE), jnp.bfloat16)
        for kv in range(KEY_VALUE_HEADS):
            last_ref = last_refs[kv * 2 // KEY_VALUE_HEADS]
            parts = []
            for i in range(count):
                part = sorted_ref[kv, start + i]
                for last_half, number in enumerate(numbers[-1]):
                    row = kv % (KEY_VALUE_HEADS // 2) * TOK_DEV + last_half * RUN
                    part = jnp.where(start + i == number, last_ref[row : row + RUN, :], part)
                parts.append(part)
            summed = jnp.dot(
                weights_ref[half * KEY_VALUE_HEADS + kv, :, : count * RUN],
                jnp.concatenate([jnp.concatenate(parts, axis=0), ones], axis=1),
                preferred_element_type=jnp.float32,
            )
            total = summed[:, HEAD_SIZE:]
            inverse = pl.reciprocal(total, approx=True)
            inverse = inverse * (2.0 - total * inverse)
            result = (summed[:, :HEAD_SIZE] * inverse).astype(jnp.bfloat16)
            for i in range(GROUP):
                h = kv * GROUP + i
                result_buf[half, :, h * HEAD_SIZE : (h + 1) * HEAD_SIZE] = result[i * RUN : (i + 1) * RUN]
            copies[half * KEY_VALUE_HEADS + kv].start()

    copies = []
    for half in range(2):
        for kv in range(KEY_VALUE_HEADS):
            columns = pl.ds(kv * GROUP * HEAD_SIZE, GROUP * HEAD_SIZE)
            copies.append(
                pltpu.make_async_copy(
                    result_buf.at[half, :, columns],
                    out_ref.at[pl.ds(half * RUN, RUN), columns],
                    out_sems.at[half * KEY_VALUE_HEADS + kv],
                )
            )
    for half in range(2):
        start, far = first_in_reach(runs, pos_ref, numbers[0][half])
        reach = runs // 4
        lax.cond(
            far,
            functools.partial(half_values, half, start, reach + 1),
            functools.partial(half_values, half, start, reach),
        )
    for copy in copies:
        copy.wait()


def per_device(queries, keys, values, token_pos, segment):
    sections, places = lax.axis_size("section"), lax.axis_size("ctx")
    runs = segment.shape[0] // RUN
    depth = places // 2
    ring = [z * 2 for z in range(depth)] + [z * 2 + 1 for z in reversed(range(depth))]

    def shift(block, section_by, ring_by):
        pairs = []
        for s in range(sections):
            for i in range(places):
                target = (s + section_by) % sections * places + ring[(i + ring_by) % places]
                pairs.append((s * places + ring[i], target))
        return lax.ppermute(block, ("section", "ctx"), pairs)

    def around(block, rows, early=None):
        ahead, back = shift(block, 1, 1), shift(block, 1, -1)
        held = [ahead, back]
        for step in range(2, places // 2):
            if early is not None and step == places // 2 - 1:
                ahead, _ = lax.optimization_barrier((ahead, early))
            ahead, back = shift(ahead, 0, 1), shift(back, 0, -1)
            held.extend([ahead, back])
        return held + [shift(ahead[: rows // 2], 0, 1), shift(back[rows // 2 : rows], 0, -1)]

    own = shift(jnp.concatenate([queries[0], keys[0], values[0]], axis=1), 1, 0)
    vmem = pl.BlockSpec(memory_space=pltpu.VMEM)
    blank = pl.pallas_call(
        blank_kernel,
        out_shape=jax.ShapeDtypeStruct((TAG_ROWS, TOK_DEV), jnp.bfloat16),
        out_specs=vmem,
        compiler_params=pltpu.CompilerParams(vmem_limit_bytes=8 * 1024 * 1024),
        cost_estimate=pl.CostEstimate(flops=1 << 30, bytes_accessed=0, transcendentals=0),
    )()
    tag = (token_pos >> (RUN.bit_length() - 1)).astype(jnp.bfloat16)
    by_head = [values[0, :, kv * HEAD_SIZE : (kv + 1) * HEAD_SIZE] for kv in range(KEY_VALUE_HEADS)]
    tagged = jnp.concatenate([*by_head, blank + tag[None]], axis=0)
    pos = lax.optimization_barrier(jnp.concatenate([token_pos, segment]).astype(jnp.float32)[None])
    bias = pl.pallas_call(
        functools.partial(bias_kernel, runs),
        out_shape=jax.ShapeDtypeStruct((2, RUN, (runs // 4 + 1) * RUN), jnp.float32),
        in_specs=[vmem],
        out_specs=vmem,
        compiler_params=pltpu.CompilerParams(vmem_limit_bytes=8 * 1024 * 1024),
        cost_estimate=pl.CostEstimate(flops=1 << 20, bytes_accessed=1 << 10, transcendentals=0),
    )(pos)
    all_keys = around(keys[0], TOK_DEV)
    all_values = around(tagged, VALUE_ROWS, bias)
    params = pltpu.CompilerParams(vmem_limit_bytes=(12 + runs // 4) * 1024 * 1024)
    mark = pl.pallas_call(
        blank_kernel,
        out_shape=jax.ShapeDtypeStruct((8, HEAD_SIZE), jnp.float32),
        in_specs=[vmem] * 2,
        out_specs=vmem,
        compiler_params=pltpu.CompilerParams(vmem_limit_bytes=8 * 1024 * 1024),
        cost_estimate=pl.CostEstimate(flops=65 << 27, bytes_accessed=0, transcendentals=0),
    )(*all_keys[-2:])
    weights, sorted_values = pl.pallas_call(
        functools.partial(weights_kernel, runs),
        out_shape=(
            jax.ShapeDtypeStruct((2 * KEY_VALUE_HEADS, GROUP * RUN, (runs // 4 + 1) * RUN), jnp.bfloat16),
            jax.ShapeDtypeStruct((KEY_VALUE_HEADS, runs, RUN, HEAD_SIZE), jnp.bfloat16),
        ),
        in_specs=[vmem] * (4 + len(all_keys) + len(all_values[:-2])),
        out_specs=(vmem,) * 2,
        scratch_shapes=[pltpu.VMEM((runs, RUN, KV_COLUMNS), jnp.bfloat16)],
        compiler_params=params,
        cost_estimate=pl.CostEstimate(flops=1 << 26, bytes_accessed=1 << 20, transcendentals=0),
    )(pos, bias, mark, own, *all_keys, *all_values[:-2])
    out = pl.pallas_call(
        functools.partial(values_kernel, runs),
        out_shape=jax.ShapeDtypeStruct((TOK_DEV, QUERY_COLUMNS), jnp.bfloat16),
        in_specs=[vmem] * (3 + len(all_values)),
        out_specs=pl.BlockSpec(memory_space=pl.ANY),
        scratch_shapes=[
            pltpu.VMEM((2, RUN, QUERY_COLUMNS), jnp.bfloat16),
            pltpu.SemaphoreType.DMA((2 * KEY_VALUE_HEADS,)),
        ],
        compiler_params=params,
        cost_estimate=pl.CostEstimate(flops=1 << 26, bytes_accessed=1 << 20, transcendentals=0),
    )(pos, weights, sorted_values, *all_values)
    return out[None]


def solution(mesh):
    return jax.shard_map(
        per_device,
        mesh=mesh,
        in_specs=(
            P("section", "ctx", None),
            P("section", "ctx", None),
            P("section", "ctx", None),
            P("ctx"),
            P(),
        ),
        out_specs=P("section", "ctx", None),
        check_vma=False,
    )
```

```python
import functools
import math

import jax
import jax.numpy as jnp
from jax import lax
from jax.experimental import pallas as pl
from jax.experimental.pallas import tpu as pltpu
from jax.sharding import PartitionSpec as P

HEAD_SIZE = 128
QUERY_HEADS = 32
KEY_VALUE_HEADS = 4
GROUP = QUERY_HEADS // KEY_VALUE_HEADS
RUN = 64
TOK_DEV = 2 * RUN
QUERY_COLUMNS = QUERY_HEADS * HEAD_SIZE
KV_COLUMNS = KEY_VALUE_HEADS * HEAD_SIZE
TAG_ROWS = 16
VALUE_ROWS = KEY_VALUE_HEADS * TOK_DEV

masked_fill = -1e30


def first_run(pos_ref):
    return lax.div(pos_ref[:, :TOK_DEV][0, 0].astype(jnp.int32), RUN)


def first_in_reach(runs, pos_ref, run):
    reach = runs // 4
    segment = pos_ref[:, TOK_DEV:]
    position = lax.broadcasted_iota(jnp.int32, segment.shape, 1)
    doc = jnp.max(jnp.where(position == run * RUN, segment, -1.0))
    far_doc = jnp.max(jnp.where(position == (run - reach + 1) * RUN - 1, segment, -1.0))
    far = doc == far_doc
    return jnp.where(far, run - reach, jnp.maximum(run - reach + 1, 0)), far


def write_number(ref, row, number):
    ref[row : row + 1, :] = jnp.full((1, ref.shape[1]), number.astype(jnp.float32))


def read_number(ref, row):
    return ref[row : row + 1, :].astype(jnp.float32)[0, 0].astype(jnp.int32)


def run_numbers(runs, first, tagged_refs):
    firsts = [first]
    for ref in tagged_refs:
        firsts.append(ref[VALUE_ROWS:, :].astype(jnp.float32)[0, 0].astype(jnp.int32))
    places = runs // 2
    firsts.append(places * (places - 1) // 2 - sum(firsts))
    return [(first, runs - 1 - first) for first in firsts]


def sort_keys(numbers, own_ref, block_refs, last_refs, sorted_ref):
    for half, number in enumerate(numbers[0]):
        sorted_ref[number] = own_ref[half * RUN : (half + 1) * RUN, QUERY_COLUMNS : QUERY_COLUMNS + KV_COLUMNS]
    for (first, second), ref in zip(numbers[1:], block_refs):
        sorted_ref[first] = ref[:RUN, :]
        sorted_ref[second] = ref[RUN:, :]
    for number, ref in zip(numbers[-1], last_refs):
        sorted_ref[number] = ref[...]


def sort_values(numbers, own_ref, block_refs, sorted_ref):
    for kv in range(KEY_VALUE_HEADS):
        column = QUERY_COLUMNS + KV_COLUMNS + kv * HEAD_SIZE
        for half, number in enumerate(numbers[0]):
            sorted_ref[kv, number] = own_ref[half * RUN : (half + 1) * RUN, column : column + HEAD_SIZE]
        for pair, ref in zip(numbers[1:], block_refs):
            for half, number in enumerate(pair):
                row = kv * TOK_DEV + half * RUN
                sorted_ref[kv, number] = ref[row : row + RUN, :]


def blank_kernel(*refs):
    refs[-1][...] = jnp.zeros_like(refs[-1])


def bias_kernel(runs, pos_ref, bias_ref, plan_ref):
    segment = pos_ref[:, TOK_DEV:]
    first = first_run(pos_ref)
    write_number(plan_ref, 0, first)
    for half, run in enumerate((first, runs - 1 - first)):
        row_pos = run * RUN + lax.broadcasted_iota(jnp.int32, (RUN, 1), 0)
        at = lax.broadcasted_iota(jnp.int32, (RUN, runs * RUN), 1) == row_pos
        row_doc = jnp.sum(jnp.where(at, segment, 0.0), axis=1, keepdims=True)
        doc_start = jnp.sum(jnp.where(segment < row_doc, 1.0, 0.0), axis=1, keepdims=True).astype(jnp.int32)
        start, far = first_in_reach(runs, pos_ref, run)
        write_number(plan_ref, 1 + 2 * half, start)
        write_number(plan_ref, 2 + 2 * half, jnp.where(far, 1, 0))
        key_pos = start * RUN + lax.broadcasted_iota(jnp.int32, bias_ref.shape[1:], 1)
        bias_ref[half] = jnp.where((key_pos <= row_pos) & (key_pos >= doc_start), 0.0, masked_fill)


def weights_kernel(runs, plan_ref, bias_ref, mark_ref, own_ref, *refs):
    blocks = runs // 2
    key_refs, tagged_refs = refs[:blocks], refs[blocks:-4]
    weights_ref, sorted_ref, last_run_ref, key_buf = refs[-4:]
    numbers = run_numbers(runs, read_number(plan_ref, 0), tagged_refs)
    write_number(last_run_ref, 0, numbers[-1][0])
    plan = [(read_number(plan_ref, 1 + 2 * half), read_number(plan_ref, 2 + 2 * half) > 0) for half in range(2)]
    sort_keys(numbers, own_ref, key_refs[:-2], key_refs[-2:], key_buf)
    sort_values(numbers, own_ref, tagged_refs, sorted_ref)
    scale = math.log2(math.e) / math.sqrt(HEAD_SIZE)

    def half_weights(half, start, count):
        span = count * RUN
        bias = jnp.concatenate([bias_ref[half, :, :span]] * GROUP, axis=0)
        for kv in range(KEY_VALUE_HEADS):
            query = jnp.concatenate(
                [
                    own_ref[half * RUN : (half + 1) * RUN, h * HEAD_SIZE : (h + 1) * HEAD_SIZE]
                    for h in range(kv * GROUP, (kv + 1) * GROUP)
                ],
                axis=0,
            )
            key = key_buf[pl.ds(start, count), :, kv * HEAD_SIZE : (kv + 1) * HEAD_SIZE]
            scores = bias + lax.dot_general(
                query,
                key.reshape(span, HEAD_SIZE),
                (((1,), (1,)), ((), ())),
                preferred_element_type=jnp.float32,
            )
            row_max = jnp.max(scores, axis=1, keepdims=True)
            weights = jnp.exp2((scores - row_max) * scale).astype(jnp.bfloat16)
            weights_ref[half * KEY_VALUE_HEADS + kv, :, :span] = weights

    for half in range(2):
        start, far = plan[half]
        pl.when(far)(functools.partial(half_weights, half, start, runs // 4 + 1))
        pl.when(jnp.logical_not(far))(functools.partial(half_weights, half, start, runs // 4))


def values_kernel(runs, plan_ref, last_run_ref, weights_ref, sorted_ref, *refs):
    last_refs, (out_ref, result_buf, out_sems) = refs[:2], refs[2:]
    last_run = read_number(last_run_ref, 0)
    last_runs = (last_run, runs - 1 - last_run)
    plan = [(read_number(plan_ref, 1 + 2 * half), read_number(plan_ref, 2 + 2 * half) > 0) for half in range(2)]

    def half_values(half, start, count):
        ones = jnp.ones((count * RUN, HEAD_SIZE), jnp.bfloat16)
        for kv in range(KEY_VALUE_HEADS):
            last_ref = last_refs[kv * 2 // KEY_VALUE_HEADS]
            parts = []
            for i in range(count):
                part = sorted_ref[kv, start + i]
                for last_half, number in enumerate(last_runs):
                    row = kv % (KEY_VALUE_HEADS // 2) * TOK_DEV + last_half * RUN
                    part = jnp.where(start + i == number, last_ref[row : row + RUN, :], part)
                parts.append(part)
            summed = jnp.dot(
                weights_ref[half * KEY_VALUE_HEADS + kv, :, : count * RUN],
                jnp.concatenate([jnp.concatenate(parts, axis=0), ones], axis=1),
                preferred_element_type=jnp.float32,
            )
            total = summed[:, HEAD_SIZE:]
            inverse = pl.reciprocal(total, approx=True)
            inverse = inverse * (2.0 - total * inverse)
            result = (summed[:, :HEAD_SIZE] * inverse).astype(jnp.bfloat16)
            for i in range(GROUP):
                h = kv * GROUP + i
                result_buf[half, :, h * HEAD_SIZE : (h + 1) * HEAD_SIZE] = result[i * RUN : (i + 1) * RUN]
            copies[half * KEY_VALUE_HEADS + kv].start()

    copies = []
    for half in range(2):
        for kv in range(KEY_VALUE_HEADS):
            columns = pl.ds(kv * GROUP * HEAD_SIZE, GROUP * HEAD_SIZE)
            copies.append(
                pltpu.make_async_copy(
                    result_buf.at[half, :, columns],
                    out_ref.at[pl.ds(half * RUN, RUN), columns],
                    out_sems.at[half * KEY_VALUE_HEADS + kv],
                )
            )
    for half in range(2):
        start, far = plan[half]
        reach = runs // 4
        lax.cond(
            far,
            functools.partial(half_values, half, start, reach + 1),
            functools.partial(half_values, half, start, reach),
        )
    for copy in copies:
        copy.wait()


def per_device(queries, keys, values, token_pos, segment):
    sections, places = lax.axis_size("section"), lax.axis_size("ctx")
    runs = segment.shape[0] // RUN
    depth = places // 2
    ring = [z * 2 for z in range(depth)] + [z * 2 + 1 for z in reversed(range(depth))]

    def shift(block, section_by, ring_by):
        pairs = []
        for s in range(sections):
            for i in range(places):
                target = (s + section_by) % sections * places + ring[(i + ring_by) % places]
                pairs.append((s * places + ring[i], target))
        return lax.ppermute(block, ("section", "ctx"), pairs)

    def around(block, rows, early=None):
        ahead, back = shift(block, 1, 1), shift(block, 1, -1)
        held = [ahead, back]
        for step in range(2, places // 2):
            if early is not None and step == places // 2 - 1:
                ahead, _ = lax.optimization_barrier((ahead, early))
            ahead, back = shift(ahead, 0, 1), shift(back, 0, -1)
            held.extend([ahead, back])
        return held + [shift(ahead[: rows // 2], 0, 1), shift(back[rows // 2 : rows], 0, -1)]

    own = shift(jnp.concatenate([queries[0], keys[0], values[0]], axis=1), 1, 0)
    vmem = pl.BlockSpec(memory_space=pltpu.VMEM)
    blank = pl.pallas_call(
        blank_kernel,
        out_shape=jax.ShapeDtypeStruct((TAG_ROWS, TOK_DEV), jnp.bfloat16),
        out_specs=vmem,
        compiler_params=pltpu.CompilerParams(vmem_limit_bytes=8 * 1024 * 1024),
        cost_estimate=pl.CostEstimate(flops=1 << 30, bytes_accessed=0, transcendentals=0),
    )()
    tag = (token_pos >> (RUN.bit_length() - 1)).astype(jnp.bfloat16)
    by_head = [values[0, :, kv * HEAD_SIZE : (kv + 1) * HEAD_SIZE] for kv in range(KEY_VALUE_HEADS)]
    tagged = jnp.concatenate([*by_head, blank + tag[None]], axis=0)
    pos = lax.optimization_barrier(jnp.concatenate([token_pos, segment]).astype(jnp.float32)[None])
    bias, plan = pl.pallas_call(
        functools.partial(bias_kernel, runs),
        out_shape=(
            jax.ShapeDtypeStruct((2, RUN, (runs // 4 + 1) * RUN), jnp.float32),
            jax.ShapeDtypeStruct((8, HEAD_SIZE), jnp.float32),
        ),
        in_specs=[vmem],
        out_specs=(vmem,) * 2,
        compiler_params=pltpu.CompilerParams(vmem_limit_bytes=8 * 1024 * 1024),
        cost_estimate=pl.CostEstimate(flops=1 << 20, bytes_accessed=1 << 10, transcendentals=0),
    )(pos)
    all_keys = around(keys[0], TOK_DEV)
    all_values = around(tagged, VALUE_ROWS, bias)
    params = pltpu.CompilerParams(vmem_limit_bytes=(12 + runs // 4) * 1024 * 1024)
    mark = pl.pallas_call(
        blank_kernel,
        out_shape=jax.ShapeDtypeStruct((8, HEAD_SIZE), jnp.float32),
        in_specs=[vmem] * 2,
        out_specs=vmem,
        compiler_params=pltpu.CompilerParams(vmem_limit_bytes=8 * 1024 * 1024),
        cost_estimate=pl.CostEstimate(flops=65 << 27, bytes_accessed=0, transcendentals=0),
    )(*all_keys[-2:])
    weights, sorted_values, last_run = pl.pallas_call(
        functools.partial(weights_kernel, runs),
        out_shape=(
            jax.ShapeDtypeStruct((2 * KEY_VALUE_HEADS, GROUP * RUN, (runs // 4 + 1) * RUN), jnp.bfloat16),
            jax.ShapeDtypeStruct((KEY_VALUE_HEADS, runs, RUN, HEAD_SIZE), jnp.bfloat16),
            jax.ShapeDtypeStruct((8, HEAD_SIZE), jnp.float32),
        ),
        in_specs=[vmem] * (4 + len(all_keys) + len(all_values[:-2])),
        out_specs=(vmem,) * 3,
        scratch_shapes=[pltpu.VMEM((runs, RUN, KV_COLUMNS), jnp.bfloat16)],
        compiler_params=params,
        cost_estimate=pl.CostEstimate(flops=1 << 26, bytes_accessed=1 << 20, transcendentals=0),
    )(plan, bias, mark, own, *all_keys, *all_values[:-2])
    out = pl.pallas_call(
        functools.partial(values_kernel, runs),
        out_shape=jax.ShapeDtypeStruct((TOK_DEV, QUERY_COLUMNS), jnp.bfloat16),
        in_specs=[vmem] * 6,
        out_specs=pl.BlockSpec(memory_space=pl.ANY),
        scratch_shapes=[
            pltpu.VMEM((2, RUN, QUERY_COLUMNS), jnp.bfloat16),
            pltpu.SemaphoreType.DMA((2 * KEY_VALUE_HEADS,)),
        ],
        compiler_params=params,
        cost_estimate=pl.CostEstimate(flops=1 << 26, bytes_accessed=1 << 20, transcendentals=0),
    )(plan, last_run, weights, sorted_values, *all_values[-2:])
    return out[None]


def solution(mesh):
    return jax.shard_map(
        per_device,
        mesh=mesh,
        in_specs=(
            P("section", "ctx", None),
            P("section", "ctx", None),
            P("section", "ctx", None),
            P("ctx"),
            P(),
        ),
        out_specs=P("section", "ctx", None),
        check_vma=False,
    )
```

```python
import functools
import math

import jax
import jax.numpy as jnp
from jax import lax
from jax.experimental import pallas as pl
from jax.experimental.pallas import tpu as pltpu
from jax.sharding import PartitionSpec as P

HEAD_SIZE = 128
QUERY_HEADS = 32
KEY_VALUE_HEADS = 4
GROUP = QUERY_HEADS // KEY_VALUE_HEADS
RUN = 64
TOK_DEV = 2 * RUN
QUERY_COLUMNS = QUERY_HEADS * HEAD_SIZE
KV_COLUMNS = KEY_VALUE_HEADS * HEAD_SIZE
TAG_ROWS = 16
VALUE_ROWS = KEY_VALUE_HEADS * TOK_DEV

masked_fill = -1e30


def first_run(pos_ref):
    return lax.div(pos_ref[:, :TOK_DEV][0, 0].astype(jnp.int32), RUN)


def first_in_reach(runs, pos_ref, run):
    reach = runs // 4
    segment = pos_ref[:, TOK_DEV:]
    position = lax.broadcasted_iota(jnp.int32, segment.shape, 1)
    doc = jnp.max(jnp.where(position == run * RUN, segment, -1.0))
    far_doc = jnp.max(jnp.where(position == (run - reach + 1) * RUN - 1, segment, -1.0))
    far = doc == far_doc
    return jnp.where(far, run - reach, jnp.maximum(run - reach + 1, 0)), far


def write_number(ref, row, number):
    ref[row : row + 1, :] = jnp.full((1, ref.shape[1]), number.astype(jnp.float32))


def read_number(ref, row):
    return ref[row : row + 1, :].astype(jnp.float32)[0, 0].astype(jnp.int32)


def run_numbers(runs, first, tagged_refs):
    firsts = [first]
    for ref in tagged_refs:
        firsts.append(ref[VALUE_ROWS:, :].astype(jnp.float32)[0, 0].astype(jnp.int32))
    places = runs // 2
    firsts.append(places * (places - 1) // 2 - sum(firsts))
    return [(first, runs - 1 - first) for first in firsts]


def sort_keys(numbers, own_ref, block_refs, last_refs, sorted_ref):
    for half, number in enumerate(numbers[0]):
        sorted_ref[number] = own_ref[half * RUN : (half + 1) * RUN, QUERY_COLUMNS : QUERY_COLUMNS + KV_COLUMNS]
    for (first, second), ref in zip(numbers[1:], block_refs):
        sorted_ref[first] = ref[:RUN, :]
        sorted_ref[second] = ref[RUN:, :]
    cut = last_refs[0].shape[0] - RUN
    first, second = numbers[-1]
    sorted_ref[first] = last_refs[0][:RUN, :]
    sorted_ref[second, :cut] = last_refs[0][RUN:, :]
    sorted_ref[second, cut:] = last_refs[1][...]


def sort_values(numbers, own_ref, block_refs, sorted_ref):
    for kv in range(KEY_VALUE_HEADS):
        column = QUERY_COLUMNS + KV_COLUMNS + kv * HEAD_SIZE
        for half, number in enumerate(numbers[0]):
            sorted_ref[kv, number] = own_ref[half * RUN : (half + 1) * RUN, column : column + HEAD_SIZE]
        for pair, ref in zip(numbers[1:], block_refs):
            for half, number in enumerate(pair):
                row = kv * TOK_DEV + half * RUN
                sorted_ref[kv, number] = ref[row : row + RUN, :]


def blank_kernel(*refs):
    refs[-1][...] = jnp.zeros_like(refs[-1])


def bias_kernel(runs, pos_ref, bias_ref, plan_ref):
    segment = pos_ref[:, TOK_DEV:]
    first = first_run(pos_ref)
    write_number(plan_ref, 0, first)
    for half, run in enumerate((first, runs - 1 - first)):
        row_pos = run * RUN + lax.broadcasted_iota(jnp.int32, (RUN, 1), 0)
        at = lax.broadcasted_iota(jnp.int32, (RUN, runs * RUN), 1) == row_pos
        row_doc = jnp.sum(jnp.where(at, segment, 0.0), axis=1, keepdims=True)
        doc_start = jnp.sum(jnp.where(segment < row_doc, 1.0, 0.0), axis=1, keepdims=True).astype(jnp.int32)
        start, far = first_in_reach(runs, pos_ref, run)
        write_number(plan_ref, 1 + 2 * half, start)
        write_number(plan_ref, 2 + 2 * half, jnp.where(far, 1, 0))
        key_pos = start * RUN + lax.broadcasted_iota(jnp.int32, bias_ref.shape[1:], 1)
        bias_ref[half] = jnp.where((key_pos <= row_pos) & (key_pos >= doc_start), 0.0, masked_fill)


def weights_kernel(runs, plan_ref, bias_ref, mark_ref, own_ref, *refs):
    blocks = runs // 2
    key_refs, tagged_refs = refs[:blocks], refs[blocks:-4]
    weights_ref, sorted_ref, last_run_ref, key_buf = refs[-4:]
    numbers = run_numbers(runs, read_number(plan_ref, 0), tagged_refs)
    write_number(last_run_ref, 0, numbers[-1][0])
    plan = [(read_number(plan_ref, 1 + 2 * half), read_number(plan_ref, 2 + 2 * half) > 0) for half in range(2)]
    sort_keys(numbers, own_ref, key_refs[:-2], key_refs[-2:], key_buf)
    sort_values(numbers, own_ref, tagged_refs, sorted_ref)
    scale = math.log2(math.e) / math.sqrt(HEAD_SIZE)

    def half_weights(half, start, count):
        span = count * RUN
        bias = jnp.concatenate([bias_ref[half, :, :span]] * GROUP, axis=0)
        for kv in range(KEY_VALUE_HEADS):
            query = jnp.concatenate(
                [
                    own_ref[half * RUN : (half + 1) * RUN, h * HEAD_SIZE : (h + 1) * HEAD_SIZE]
                    for h in range(kv * GROUP, (kv + 1) * GROUP)
                ],
                axis=0,
            )
            key = key_buf[pl.ds(start, count), :, kv * HEAD_SIZE : (kv + 1) * HEAD_SIZE]
            scores = bias + lax.dot_general(
                query,
                key.reshape(span, HEAD_SIZE),
                (((1,), (1,)), ((), ())),
                preferred_element_type=jnp.float32,
            )
            row_max = jnp.max(scores, axis=1, keepdims=True)
            weights = jnp.exp2((scores - row_max) * scale).astype(jnp.bfloat16)
            weights_ref[half * KEY_VALUE_HEADS + kv, :, :span] = weights

    for half in range(2):
        start, far = plan[half]
        pl.when(far)(functools.partial(half_weights, half, start, runs // 4 + 1))
        pl.when(jnp.logical_not(far))(functools.partial(half_weights, half, start, runs // 4))


def values_kernel(runs, plan_ref, last_run_ref, weights_ref, sorted_ref, *refs):
    last_refs, (out_ref, result_buf, out_sems) = refs[:2], refs[2:]
    last_run = read_number(last_run_ref, 0)
    last_runs = (last_run, runs - 1 - last_run)
    plan = [(read_number(plan_ref, 1 + 2 * half), read_number(plan_ref, 2 + 2 * half) > 0) for half in range(2)]

    def half_values(half, start, count):
        ones = jnp.ones((count * RUN, HEAD_SIZE), jnp.bfloat16)
        for kv in range(KEY_VALUE_HEADS):
            which, place = divmod(kv, KEY_VALUE_HEADS * 3 // 4)
            last_ref = last_refs[which]
            parts = []
            for i in range(count):
                part = sorted_ref[kv, start + i]
                for last_half, number in enumerate(last_runs):
                    row = place * TOK_DEV + last_half * RUN
                    part = jnp.where(start + i == number, last_ref[row : row + RUN, :], part)
                parts.append(part)
            summed = jnp.dot(
                weights_ref[half * KEY_VALUE_HEADS + kv, :, : count * RUN],
                jnp.concatenate([jnp.concatenate(parts, axis=0), ones], axis=1),
                preferred_element_type=jnp.float32,
            )
            total = summed[:, HEAD_SIZE:]
            inverse = pl.reciprocal(total, approx=True)
            inverse = inverse * (2.0 - total * inverse)
            result = (summed[:, :HEAD_SIZE] * inverse).astype(jnp.bfloat16)
            for i in range(GROUP):
                h = kv * GROUP + i
                result_buf[half, :, h * HEAD_SIZE : (h + 1) * HEAD_SIZE] = result[i * RUN : (i + 1) * RUN]
            copies[half * KEY_VALUE_HEADS + kv].start()

    copies = []
    for half in range(2):
        for kv in range(KEY_VALUE_HEADS):
            columns = pl.ds(kv * GROUP * HEAD_SIZE, GROUP * HEAD_SIZE)
            copies.append(
                pltpu.make_async_copy(
                    result_buf.at[half, :, columns],
                    out_ref.at[pl.ds(half * RUN, RUN), columns],
                    out_sems.at[half * KEY_VALUE_HEADS + kv],
                )
            )
    for half in range(2):
        start, far = plan[half]
        reach = runs // 4
        lax.cond(
            far,
            functools.partial(half_values, half, start, reach + 1),
            functools.partial(half_values, half, start, reach),
        )
    for copy in copies:
        copy.wait()


def per_device(queries, keys, values, token_pos, segment):
    sections, places = lax.axis_size("section"), lax.axis_size("ctx")
    runs = segment.shape[0] // RUN
    depth = places // 2
    ring = [z * 2 for z in range(depth)] + [z * 2 + 1 for z in reversed(range(depth))]

    def shift(block, section_by, ring_by):
        pairs = []
        for s in range(sections):
            for i in range(places):
                target = (s + section_by) % sections * places + ring[(i + ring_by) % places]
                pairs.append((s * places + ring[i], target))
        return lax.ppermute(block, ("section", "ctx"), pairs)

    def around(block, rows, early=None):
        ahead, back = shift(block, 1, 1), shift(block, 1, -1)
        held = [ahead, back]
        for step in range(2, places // 2):
            if early is not None and step == places // 2 - 1:
                ahead, _ = lax.optimization_barrier((ahead, early))
            ahead, back = shift(ahead, 0, 1), shift(back, 0, -1)
            held.extend([ahead, back])
        cut = rows * 3 // 4
        return held + [shift(ahead[:cut], 0, 1), shift(back[cut:rows], 0, -1)]

    own = shift(jnp.concatenate([queries[0], keys[0], values[0]], axis=1), 1, 0)
    vmem = pl.BlockSpec(memory_space=pltpu.VMEM)
    blank = pl.pallas_call(
        blank_kernel,
        out_shape=jax.ShapeDtypeStruct((TAG_ROWS, TOK_DEV), jnp.bfloat16),
        out_specs=vmem,
        compiler_params=pltpu.CompilerParams(vmem_limit_bytes=8 * 1024 * 1024),
        cost_estimate=pl.CostEstimate(flops=1 << 30, bytes_accessed=0, transcendentals=0),
    )()
    tag = (token_pos >> (RUN.bit_length() - 1)).astype(jnp.bfloat16)
    by_head = [values[0, :, kv * HEAD_SIZE : (kv + 1) * HEAD_SIZE] for kv in range(KEY_VALUE_HEADS)]
    tagged = jnp.concatenate([*by_head, blank + tag[None]], axis=0)
    pos = lax.optimization_barrier(jnp.concatenate([token_pos, segment]).astype(jnp.float32)[None])
    bias, plan = pl.pallas_call(
        functools.partial(bias_kernel, runs),
        out_shape=(
            jax.ShapeDtypeStruct((2, RUN, (runs // 4 + 1) * RUN), jnp.float32),
            jax.ShapeDtypeStruct((8, HEAD_SIZE), jnp.float32),
        ),
        in_specs=[vmem],
        out_specs=(vmem,) * 2,
        compiler_params=pltpu.CompilerParams(vmem_limit_bytes=8 * 1024 * 1024),
        cost_estimate=pl.CostEstimate(flops=1 << 20, bytes_accessed=1 << 10, transcendentals=0),
    )(pos)
    all_keys = around(keys[0], TOK_DEV)
    all_values = around(tagged, VALUE_ROWS, bias)
    params = pltpu.CompilerParams(vmem_limit_bytes=(12 + runs // 4) * 1024 * 1024)
    mark = pl.pallas_call(
        blank_kernel,
        out_shape=jax.ShapeDtypeStruct((8, HEAD_SIZE), jnp.float32),
        in_specs=[vmem] * 2,
        out_specs=vmem,
        compiler_params=pltpu.CompilerParams(vmem_limit_bytes=8 * 1024 * 1024),
        cost_estimate=pl.CostEstimate(flops=65 << 27, bytes_accessed=0, transcendentals=0),
    )(*all_keys[-2:])
    weights, sorted_values, last_run = pl.pallas_call(
        functools.partial(weights_kernel, runs),
        out_shape=(
            jax.ShapeDtypeStruct((2 * KEY_VALUE_HEADS, GROUP * RUN, (runs // 4 + 1) * RUN), jnp.bfloat16),
            jax.ShapeDtypeStruct((KEY_VALUE_HEADS, runs, RUN, HEAD_SIZE), jnp.bfloat16),
            jax.ShapeDtypeStruct((8, HEAD_SIZE), jnp.float32),
        ),
        in_specs=[vmem] * (4 + len(all_keys) + len(all_values[:-2])),
        out_specs=(vmem,) * 3,
        scratch_shapes=[pltpu.VMEM((runs, RUN, KV_COLUMNS), jnp.bfloat16)],
        compiler_params=params,
        cost_estimate=pl.CostEstimate(flops=1 << 26, bytes_accessed=1 << 20, transcendentals=0),
    )(plan, bias, mark, own, *all_keys, *all_values[:-2])
    out = pl.pallas_call(
        functools.partial(values_kernel, runs),
        out_shape=jax.ShapeDtypeStruct((TOK_DEV, QUERY_COLUMNS), jnp.bfloat16),
        in_specs=[vmem] * 6,
        out_specs=pl.BlockSpec(memory_space=pl.ANY),
        scratch_shapes=[
            pltpu.VMEM((2, RUN, QUERY_COLUMNS), jnp.bfloat16),
            pltpu.SemaphoreType.DMA((2 * KEY_VALUE_HEADS,)),
        ],
        compiler_params=params,
        cost_estimate=pl.CostEstimate(flops=1 << 26, bytes_accessed=1 << 20, transcendentals=0),
    )(plan, last_run, weights, sorted_values, *all_values[-2:])
    return out[None]


def solution(mesh):
    return jax.shard_map(
        per_device,
        mesh=mesh,
        in_specs=(
            P("section", "ctx", None),
            P("section", "ctx", None),
            P("section", "ctx", None),
            P("ctx"),
            P(),
        ),
        out_specs=P("section", "ctx", None),
        check_vma=False,
    )
```

```python
import functools
import math

import jax
import jax.numpy as jnp
from jax import lax
from jax.experimental import pallas as pl
from jax.experimental.pallas import tpu as pltpu
from jax.sharding import PartitionSpec as P

HEAD_SIZE = 128
QUERY_HEADS = 32
KEY_VALUE_HEADS = 4
GROUP = QUERY_HEADS // KEY_VALUE_HEADS
RUN = 64
TOK_DEV = 2 * RUN
QUERY_COLUMNS = QUERY_HEADS * HEAD_SIZE
KV_COLUMNS = KEY_VALUE_HEADS * HEAD_SIZE
TAG_ROWS = 16
VALUE_ROWS = KEY_VALUE_HEADS * TOK_DEV

masked_fill = -1e30


def first_run(pos_ref):
    return lax.div(pos_ref[:, :TOK_DEV][0, 0].astype(jnp.int32), RUN)


def first_in_reach(runs, pos_ref, run):
    reach = runs // 4
    segment = pos_ref[:, TOK_DEV:]
    position = lax.broadcasted_iota(jnp.int32, segment.shape, 1)
    doc = jnp.max(jnp.where(position == run * RUN, segment, -1.0))
    far_doc = jnp.max(jnp.where(position == (run - reach + 1) * RUN - 1, segment, -1.0))
    far = doc == far_doc
    return jnp.where(far, run - reach, jnp.maximum(run - reach + 1, 0)), far


def write_number(ref, row, number):
    ref[row : row + 1, :] = jnp.full((1, ref.shape[1]), number.astype(jnp.float32))


def read_number(ref, row):
    return ref[row : row + 1, :].astype(jnp.float32)[0, 0].astype(jnp.int32)


def run_numbers(runs, first, tagged_refs):
    firsts = [first]
    for ref in tagged_refs:
        firsts.append(ref[VALUE_ROWS:, :].astype(jnp.float32)[0, 0].astype(jnp.int32))
    places = runs // 2
    firsts.append(places * (places - 1) // 2 - sum(firsts))
    return [(first, runs - 1 - first) for first in firsts]


def sort_keys(numbers, own_ref, block_refs, last_refs, sorted_ref):
    for half, number in enumerate(numbers[0]):
        sorted_ref[number] = own_ref[half * RUN : (half + 1) * RUN, QUERY_COLUMNS : QUERY_COLUMNS + KV_COLUMNS]
    for (first, second), ref in zip(numbers[1:], block_refs):
        sorted_ref[first] = ref[:RUN, :]
        sorted_ref[second] = ref[RUN:, :]
    cut = last_refs[0].shape[0] - RUN
    first, second = numbers[-1]
    sorted_ref[first] = last_refs[0][:RUN, :]
    sorted_ref[second, :cut] = last_refs[0][RUN:, :]
    sorted_ref[second, cut:] = last_refs[1][...]


def sort_values(numbers, own_ref, block_refs, sorted_ref):
    for kv in range(KEY_VALUE_HEADS):
        column = QUERY_COLUMNS + KV_COLUMNS + kv * HEAD_SIZE
        for half, number in enumerate(numbers[0]):
            sorted_ref[kv, number] = own_ref[half * RUN : (half + 1) * RUN, column : column + HEAD_SIZE]
        for pair, ref in zip(numbers[1:], block_refs):
            for half, number in enumerate(pair):
                row = kv * TOK_DEV + half * RUN
                sorted_ref[kv, number] = ref[row : row + RUN, :]


def blank_kernel(*refs):
    refs[-1][...] = jnp.zeros_like(refs[-1])


def bias_kernel(runs, pos_ref, bias_ref, plan_ref):
    segment = pos_ref[:, TOK_DEV:]
    first = first_run(pos_ref)
    write_number(plan_ref, 0, first)
    for half, run in enumerate((first, runs - 1 - first)):
        row_pos = run * RUN + lax.broadcasted_iota(jnp.int32, (RUN, 1), 0)
        at = lax.broadcasted_iota(jnp.int32, (RUN, runs * RUN), 1) == row_pos
        row_doc = jnp.sum(jnp.where(at, segment, 0.0), axis=1, keepdims=True)
        doc_start = jnp.sum(jnp.where(segment < row_doc, 1.0, 0.0), axis=1, keepdims=True).astype(jnp.int32)
        start, far = first_in_reach(runs, pos_ref, run)
        write_number(plan_ref, 1 + 2 * half, start)
        write_number(plan_ref, 2 + 2 * half, jnp.where(far, 1, 0))
        key_pos = start * RUN + lax.broadcasted_iota(jnp.int32, bias_ref.shape[1:], 1)
        bias_ref[half] = jnp.where((key_pos <= row_pos) & (key_pos >= doc_start), 0.0, masked_fill)


def weights_kernel(runs, plan_ref, bias_ref, mark_ref, own_ref, *refs):
    blocks = runs // 2
    key_refs, tagged_refs = refs[:blocks], refs[blocks:-5]
    weights_ref, inverse_ref, sorted_ref, last_run_ref, key_buf = refs[-5:]
    numbers = run_numbers(runs, read_number(plan_ref, 0), tagged_refs)
    write_number(last_run_ref, 0, numbers[-1][0])
    plan = [(read_number(plan_ref, 1 + 2 * half), read_number(plan_ref, 2 + 2 * half) > 0) for half in range(2)]
    sort_keys(numbers, own_ref, key_refs[:-2], key_refs[-2:], key_buf)
    sort_values(numbers, own_ref, tagged_refs, sorted_ref)
    scale = math.log2(math.e) / math.sqrt(HEAD_SIZE)

    def half_weights(half, start, count):
        span = count * RUN
        bias = jnp.concatenate([bias_ref[half, :, :span]] * GROUP, axis=0)
        for kv in range(KEY_VALUE_HEADS):
            query = jnp.concatenate(
                [
                    own_ref[half * RUN : (half + 1) * RUN, h * HEAD_SIZE : (h + 1) * HEAD_SIZE]
                    for h in range(kv * GROUP, (kv + 1) * GROUP)
                ],
                axis=0,
            )
            key = key_buf[pl.ds(start, count), :, kv * HEAD_SIZE : (kv + 1) * HEAD_SIZE]
            scores = bias + lax.dot_general(
                query,
                key.reshape(span, HEAD_SIZE),
                (((1,), (1,)), ((), ())),
                preferred_element_type=jnp.float32,
            )
            row_max = jnp.max(scores, axis=1, keepdims=True)
            weights = jnp.exp2((scores - row_max) * scale)
            total = jnp.sum(weights, axis=1, keepdims=True)
            inverse = pl.reciprocal(total, approx=True)
            inverse = inverse * (2.0 - total * inverse)
            weights_ref[half * KEY_VALUE_HEADS + kv, :, :span] = weights.astype(jnp.bfloat16)
            inverse_ref[half * KEY_VALUE_HEADS + kv] = jnp.broadcast_to(inverse, (GROUP * RUN, HEAD_SIZE))

    for half in range(2):
        start, far = plan[half]
        pl.when(far)(functools.partial(half_weights, half, start, runs // 4 + 1))
        pl.when(jnp.logical_not(far))(functools.partial(half_weights, half, start, runs // 4))


def values_kernel(runs, plan_ref, last_run_ref, weights_ref, inverse_ref, sorted_ref, *refs):
    last_refs, (out_ref, result_buf, out_sems) = refs[:2], refs[2:]
    last_run = read_number(last_run_ref, 0)
    last_runs = (last_run, runs - 1 - last_run)
    plan = [(read_number(plan_ref, 1 + 2 * half), read_number(plan_ref, 2 + 2 * half) > 0) for half in range(2)]

    def half_values(half, start, count):
        for kv in range(KEY_VALUE_HEADS):
            which, place = divmod(kv, KEY_VALUE_HEADS * 3 // 4)
            last_ref = last_refs[which]
            parts = []
            for i in range(count):
                part = sorted_ref[kv, start + i]
                for last_half, number in enumerate(last_runs):
                    row = place * TOK_DEV + last_half * RUN
                    part = jnp.where(start + i == number, last_ref[row : row + RUN, :], part)
                parts.append(part)
            summed = jnp.dot(
                weights_ref[half * KEY_VALUE_HEADS + kv, :, : count * RUN],
                jnp.concatenate(parts, axis=0),
                preferred_element_type=jnp.float32,
            )
            result = (summed * inverse_ref[half * KEY_VALUE_HEADS + kv]).astype(jnp.bfloat16)
            for i in range(GROUP):
                h = kv * GROUP + i
                result_buf[half, :, h * HEAD_SIZE : (h + 1) * HEAD_SIZE] = result[i * RUN : (i + 1) * RUN]
            copies[half * KEY_VALUE_HEADS + kv].start()

    copies = []
    for half in range(2):
        for kv in range(KEY_VALUE_HEADS):
            columns = pl.ds(kv * GROUP * HEAD_SIZE, GROUP * HEAD_SIZE)
            copies.append(
                pltpu.make_async_copy(
                    result_buf.at[half, :, columns],
                    out_ref.at[pl.ds(half * RUN, RUN), columns],
                    out_sems.at[half * KEY_VALUE_HEADS + kv],
                )
            )
    for half in range(2):
        start, far = plan[half]
        reach = runs // 4
        lax.cond(
            far,
            functools.partial(half_values, half, start, reach + 1),
            functools.partial(half_values, half, start, reach),
        )
    for copy in copies:
        copy.wait()


def per_device(queries, keys, values, token_pos, segment):
    sections, places = lax.axis_size("section"), lax.axis_size("ctx")
    runs = segment.shape[0] // RUN
    depth = places // 2
    ring = [z * 2 for z in range(depth)] + [z * 2 + 1 for z in reversed(range(depth))]

    def shift(block, section_by, ring_by):
        pairs = []
        for s in range(sections):
            for i in range(places):
                target = (s + section_by) % sections * places + ring[(i + ring_by) % places]
                pairs.append((s * places + ring[i], target))
        return lax.ppermute(block, ("section", "ctx"), pairs)

    def around(block, rows, early=None):
        ahead, back = shift(block, 1, 1), shift(block, 1, -1)
        held = [ahead, back]
        for step in range(2, places // 2):
            if early is not None and step == places // 2 - 1:
                ahead, _ = lax.optimization_barrier((ahead, early))
            ahead, back = shift(ahead, 0, 1), shift(back, 0, -1)
            held.extend([ahead, back])
        cut = rows * 3 // 4
        return held + [shift(ahead[:cut], 0, 1), shift(back[cut:rows], 0, -1)]

    own = shift(jnp.concatenate([queries[0], keys[0], values[0]], axis=1), 1, 0)
    vmem = pl.BlockSpec(memory_space=pltpu.VMEM)
    blank = pl.pallas_call(
        blank_kernel,
        out_shape=jax.ShapeDtypeStruct((TAG_ROWS, TOK_DEV), jnp.bfloat16),
        out_specs=vmem,
        compiler_params=pltpu.CompilerParams(vmem_limit_bytes=8 * 1024 * 1024),
        cost_estimate=pl.CostEstimate(flops=1 << 30, bytes_accessed=0, transcendentals=0),
    )()
    tag = (token_pos >> (RUN.bit_length() - 1)).astype(jnp.bfloat16)
    by_head = [values[0, :, kv * HEAD_SIZE : (kv + 1) * HEAD_SIZE] for kv in range(KEY_VALUE_HEADS)]
    tagged = jnp.concatenate([*by_head, blank + tag[None]], axis=0)
    pos = lax.optimization_barrier(jnp.concatenate([token_pos, segment]).astype(jnp.float32)[None])
    bias, plan = pl.pallas_call(
        functools.partial(bias_kernel, runs),
        out_shape=(
            jax.ShapeDtypeStruct((2, RUN, (runs // 4 + 1) * RUN), jnp.float32),
            jax.ShapeDtypeStruct((8, HEAD_SIZE), jnp.float32),
        ),
        in_specs=[vmem],
        out_specs=(vmem,) * 2,
        compiler_params=pltpu.CompilerParams(vmem_limit_bytes=8 * 1024 * 1024),
        cost_estimate=pl.CostEstimate(flops=1 << 20, bytes_accessed=1 << 10, transcendentals=0),
    )(pos)
    all_keys = around(keys[0], TOK_DEV)
    all_values = around(tagged, VALUE_ROWS, bias)
    params = pltpu.CompilerParams(vmem_limit_bytes=(12 + runs // 4) * 1024 * 1024)
    mark = pl.pallas_call(
        blank_kernel,
        out_shape=jax.ShapeDtypeStruct((8, HEAD_SIZE), jnp.float32),
        in_specs=[vmem] * 2,
        out_specs=vmem,
        compiler_params=pltpu.CompilerParams(vmem_limit_bytes=8 * 1024 * 1024),
        cost_estimate=pl.CostEstimate(flops=65 << 27, bytes_accessed=0, transcendentals=0),
    )(*all_keys[-2:])
    weights, inverse, sorted_values, last_run = pl.pallas_call(
        functools.partial(weights_kernel, runs),
        out_shape=(
            jax.ShapeDtypeStruct((2 * KEY_VALUE_HEADS, GROUP * RUN, (runs // 4 + 1) * RUN), jnp.bfloat16),
            jax.ShapeDtypeStruct((2 * KEY_VALUE_HEADS, GROUP * RUN, HEAD_SIZE), jnp.float32),
            jax.ShapeDtypeStruct((KEY_VALUE_HEADS, runs, RUN, HEAD_SIZE), jnp.bfloat16),
            jax.ShapeDtypeStruct((8, HEAD_SIZE), jnp.float32),
        ),
        in_specs=[vmem] * (4 + len(all_keys) + len(all_values[:-2])),
        out_specs=(vmem,) * 4,
        scratch_shapes=[pltpu.VMEM((runs, RUN, KV_COLUMNS), jnp.bfloat16)],
        compiler_params=params,
        cost_estimate=pl.CostEstimate(flops=1 << 26, bytes_accessed=1 << 20, transcendentals=0),
    )(plan, bias, mark, own, *all_keys, *all_values[:-2])
    out = pl.pallas_call(
        functools.partial(values_kernel, runs),
        out_shape=jax.ShapeDtypeStruct((TOK_DEV, QUERY_COLUMNS), jnp.bfloat16),
        in_specs=[vmem] * 7,
        out_specs=pl.BlockSpec(memory_space=pl.ANY),
        scratch_shapes=[
            pltpu.VMEM((2, RUN, QUERY_COLUMNS), jnp.bfloat16),
            pltpu.SemaphoreType.DMA((2 * KEY_VALUE_HEADS,)),
        ],
        compiler_params=params,
        cost_estimate=pl.CostEstimate(flops=1 << 26, bytes_accessed=1 << 20, transcendentals=0),
    )(plan, last_run, weights, inverse, sorted_values, *all_values[-2:])
    return out[None]


def solution(mesh):
    return jax.shard_map(
        per_device,
        mesh=mesh,
        in_specs=(
            P("section", "ctx", None),
            P("section", "ctx", None),
            P("section", "ctx", None),
            P("ctx"),
            P(),
        ),
        out_specs=P("section", "ctx", None),
        check_vma=False,
    )
```

```python
import functools
import math

import jax
import jax.numpy as jnp
from jax import lax
from jax.experimental import pallas as pl
from jax.experimental.pallas import tpu as pltpu
from jax.sharding import PartitionSpec as P

HEAD_SIZE = 128
QUERY_HEADS = 32
KEY_VALUE_HEADS = 4
GROUP = QUERY_HEADS // KEY_VALUE_HEADS
RUN = 64
TOK_DEV = 2 * RUN
QUERY_COLUMNS = QUERY_HEADS * HEAD_SIZE
KV_COLUMNS = KEY_VALUE_HEADS * HEAD_SIZE
TAG_ROWS = 16
VALUE_ROWS = KEY_VALUE_HEADS * TOK_DEV

masked_fill = -1e30


def first_run(pos_ref):
    return lax.div(pos_ref[:, :TOK_DEV][0, 0].astype(jnp.int32), RUN)


def needs_far(runs, pos_ref, run):
    segment = pos_ref[:, TOK_DEV:]
    position = lax.broadcasted_iota(jnp.int32, segment.shape, 1)
    doc = jnp.max(jnp.where(position == run * RUN, segment, -1.0))
    far_doc = jnp.max(jnp.where(position == (run - runs // 4 + 1) * RUN - 1, segment, -1.0))
    return doc == far_doc


def write_number(ref, row, number):
    ref[row : row + 1, :] = jnp.full((1, ref.shape[1]), number.astype(jnp.float32))


def read_number(ref, row):
    return ref[row : row + 1, :].astype(jnp.float32)[0, 0].astype(jnp.int32)


def run_numbers(runs, first, tagged_refs):
    firsts = [first]
    for ref in tagged_refs:
        firsts.append(ref[VALUE_ROWS:, :].astype(jnp.float32)[0, 0].astype(jnp.int32))
    places = runs // 2
    firsts.append(places * (places - 1) // 2 - sum(firsts))
    return [(first, runs - 1 - first) for first in firsts]


def sort_keys(numbers, own_ref, block_refs, last_refs, sorted_ref):
    for half, number in enumerate(numbers[0]):
        sorted_ref[number] = own_ref[half * RUN : (half + 1) * RUN, QUERY_COLUMNS : QUERY_COLUMNS + KV_COLUMNS]
    for (first, second), ref in zip(numbers[1:], block_refs):
        sorted_ref[first] = ref[:RUN, :]
        sorted_ref[second] = ref[RUN:, :]
    cut = last_refs[0].shape[0] - RUN
    first, second = numbers[-1]
    sorted_ref[first] = last_refs[0][:RUN, :]
    sorted_ref[second, :cut] = last_refs[0][RUN:, :]
    sorted_ref[second, cut:] = last_refs[1][...]


def sort_values(numbers, own_ref, block_refs, sorted_ref):
    for kv in range(KEY_VALUE_HEADS):
        column = QUERY_COLUMNS + KV_COLUMNS + kv * HEAD_SIZE
        for half, number in enumerate(numbers[0]):
            sorted_ref[kv, number] = own_ref[half * RUN : (half + 1) * RUN, column : column + HEAD_SIZE]
        for pair, ref in zip(numbers[1:], block_refs):
            for half, number in enumerate(pair):
                row = kv * TOK_DEV + half * RUN
                sorted_ref[kv, number] = ref[row : row + RUN, :]


def blank_kernel(*refs):
    refs[-1][...] = jnp.zeros_like(refs[-1])


def bias_kernel(runs, pos_ref, bias_ref, plan_ref):
    segment = pos_ref[:, TOK_DEV:]
    first = first_run(pos_ref)
    write_number(plan_ref, 0, first)
    far = needs_far(runs, pos_ref, first) | needs_far(runs, pos_ref, runs - 1 - first)
    write_number(plan_ref, 3, jnp.where(far, 1, 0))
    for half, run in enumerate((first, runs - 1 - first)):
        row_pos = run * RUN + lax.broadcasted_iota(jnp.int32, (RUN, 1), 0)
        at = lax.broadcasted_iota(jnp.int32, (RUN, runs * RUN), 1) == row_pos
        row_doc = jnp.sum(jnp.where(at, segment, 0.0), axis=1, keepdims=True)
        doc_start = jnp.sum(jnp.where(segment < row_doc, 1.0, 0.0), axis=1, keepdims=True).astype(jnp.int32)
        start = jnp.maximum(run - runs // 4 + jnp.where(far, 0, 1), 0)
        write_number(plan_ref, 1 + half, start)
        key_pos = start * RUN + lax.broadcasted_iota(jnp.int32, bias_ref.shape[1:], 1)
        bias_ref[half] = jnp.where((key_pos <= row_pos) & (key_pos >= doc_start), 0.0, masked_fill)


def weights_kernel(runs, plan_ref, bias_ref, mark_ref, own_ref, *refs):
    blocks = runs // 2
    key_refs, tagged_refs = refs[:blocks], refs[blocks:-5]
    weights_ref, inverse_ref, sorted_ref, last_run_ref, key_buf = refs[-5:]
    numbers = run_numbers(runs, read_number(plan_ref, 0), tagged_refs)
    write_number(last_run_ref, 0, numbers[-1][0])
    starts = [read_number(plan_ref, 1 + half) for half in range(2)]
    far = read_number(plan_ref, 3) > 0
    sort_keys(numbers, own_ref, key_refs[:-2], key_refs[-2:], key_buf)
    sort_values(numbers, own_ref, tagged_refs, sorted_ref)
    scale = math.log2(math.e) / math.sqrt(HEAD_SIZE)

    def half_weights(half, start, count):
        span = count * RUN
        bias = jnp.concatenate([bias_ref[half, :, :span]] * GROUP, axis=0)
        for kv in range(KEY_VALUE_HEADS):
            query = jnp.concatenate(
                [
                    own_ref[half * RUN : (half + 1) * RUN, h * HEAD_SIZE : (h + 1) * HEAD_SIZE]
                    for h in range(kv * GROUP, (kv + 1) * GROUP)
                ],
                axis=0,
            )
            key = key_buf[pl.ds(start, count), :, kv * HEAD_SIZE : (kv + 1) * HEAD_SIZE]
            scores = bias + lax.dot_general(
                query,
                key.reshape(span, HEAD_SIZE),
                (((1,), (1,)), ((), ())),
                preferred_element_type=jnp.float32,
            )
            row_max = jnp.max(scores, axis=1, keepdims=True)
            weights = jnp.exp2((scores - row_max) * scale)
            total = jnp.sum(weights, axis=1, keepdims=True)
            inverse = pl.reciprocal(total, approx=True)
            inverse = inverse * (2.0 - total * inverse)
            weights_ref[half * KEY_VALUE_HEADS + kv, :, :span] = weights.astype(jnp.bfloat16)
            inverse_ref[half * KEY_VALUE_HEADS + kv] = jnp.broadcast_to(inverse, (GROUP * RUN, HEAD_SIZE))

    def both_weights(count):
        for half in range(2):
            half_weights(half, starts[half], count)

    lax.cond(far, lambda: both_weights(runs // 4 + 1), lambda: both_weights(runs // 4))


def values_kernel(runs, plan_ref, last_run_ref, weights_ref, inverse_ref, sorted_ref, *refs):
    last_refs, (out_ref, result_buf, out_sems) = refs[:2], refs[2:]
    last_run = read_number(last_run_ref, 0)
    last_runs = (last_run, runs - 1 - last_run)
    starts = [read_number(plan_ref, 1 + half) for half in range(2)]
    far = read_number(plan_ref, 3) > 0

    def half_values(half, start, count):
        for kv in range(KEY_VALUE_HEADS):
            which, place = divmod(kv, KEY_VALUE_HEADS * 3 // 4)
            last_ref = last_refs[which]
            parts = []
            for i in range(count):
                part = sorted_ref[kv, start + i]
                for last_half, number in enumerate(last_runs):
                    row = place * TOK_DEV + last_half * RUN
                    part = jnp.where(start + i == number, last_ref[row : row + RUN, :], part)
                parts.append(part)
            summed = jnp.dot(
                weights_ref[half * KEY_VALUE_HEADS + kv, :, : count * RUN],
                jnp.concatenate(parts, axis=0),
                preferred_element_type=jnp.float32,
            )
            result = (summed * inverse_ref[half * KEY_VALUE_HEADS + kv]).astype(jnp.bfloat16)
            for i in range(GROUP):
                h = kv * GROUP + i
                result_buf[half, :, h * HEAD_SIZE : (h + 1) * HEAD_SIZE] = result[i * RUN : (i + 1) * RUN]
            copies[half * KEY_VALUE_HEADS + kv].start()

    copies = []
    for half in range(2):
        for kv in range(KEY_VALUE_HEADS):
            columns = pl.ds(kv * GROUP * HEAD_SIZE, GROUP * HEAD_SIZE)
            copies.append(
                pltpu.make_async_copy(
                    result_buf.at[half, :, columns],
                    out_ref.at[pl.ds(half * RUN, RUN), columns],
                    out_sems.at[half * KEY_VALUE_HEADS + kv],
                )
            )

    def both_values(count):
        for half in range(2):
            half_values(half, starts[half], count)

    lax.cond(far, lambda: both_values(runs // 4 + 1), lambda: both_values(runs // 4))
    for copy in copies:
        copy.wait()


def per_device(queries, keys, values, token_pos, segment):
    sections, places = lax.axis_size("section"), lax.axis_size("ctx")
    runs = segment.shape[0] // RUN
    depth = places // 2
    ring = [z * 2 for z in range(depth)] + [z * 2 + 1 for z in reversed(range(depth))]

    def shift(block, section_by, ring_by):
        pairs = []
        for s in range(sections):
            for i in range(places):
                target = (s + section_by) % sections * places + ring[(i + ring_by) % places]
                pairs.append((s * places + ring[i], target))
        return lax.ppermute(block, ("section", "ctx"), pairs)

    def around(block, rows, early=None):
        ahead, back = shift(block, 1, 1), shift(block, 1, -1)
        held = [ahead, back]
        for step in range(2, places // 2):
            if early is not None and step == places // 2 - 1:
                ahead, _ = lax.optimization_barrier((ahead, early))
            ahead, back = shift(ahead, 0, 1), shift(back, 0, -1)
            held.extend([ahead, back])
        cut = rows * 3 // 4
        return held + [shift(ahead[:cut], 0, 1), shift(back[cut:rows], 0, -1)]

    own = shift(jnp.concatenate([queries[0], keys[0], values[0]], axis=1), 1, 0)
    vmem = pl.BlockSpec(memory_space=pltpu.VMEM)
    blank = pl.pallas_call(
        blank_kernel,
        out_shape=jax.ShapeDtypeStruct((TAG_ROWS, TOK_DEV), jnp.bfloat16),
        out_specs=vmem,
        compiler_params=pltpu.CompilerParams(vmem_limit_bytes=8 * 1024 * 1024),
        cost_estimate=pl.CostEstimate(flops=1 << 30, bytes_accessed=0, transcendentals=0),
    )()
    tag = (token_pos >> (RUN.bit_length() - 1)).astype(jnp.bfloat16)
    by_head = [values[0, :, kv * HEAD_SIZE : (kv + 1) * HEAD_SIZE] for kv in range(KEY_VALUE_HEADS)]
    tagged = jnp.concatenate([*by_head, blank + tag[None]], axis=0)
    pos = lax.optimization_barrier(jnp.concatenate([token_pos, segment]).astype(jnp.float32)[None])
    bias, plan = pl.pallas_call(
        functools.partial(bias_kernel, runs),
        out_shape=(
            jax.ShapeDtypeStruct((2, RUN, (runs // 4 + 1) * RUN), jnp.float32),
            jax.ShapeDtypeStruct((8, HEAD_SIZE), jnp.float32),
        ),
        in_specs=[vmem],
        out_specs=(vmem,) * 2,
        compiler_params=pltpu.CompilerParams(vmem_limit_bytes=8 * 1024 * 1024),
        cost_estimate=pl.CostEstimate(flops=1 << 20, bytes_accessed=1 << 10, transcendentals=0),
    )(pos)
    all_keys = around(keys[0], TOK_DEV)
    all_values = around(tagged, VALUE_ROWS, bias)
    params = pltpu.CompilerParams(vmem_limit_bytes=(12 + runs // 4) * 1024 * 1024)
    mark = pl.pallas_call(
        blank_kernel,
        out_shape=jax.ShapeDtypeStruct((8, HEAD_SIZE), jnp.float32),
        in_specs=[vmem] * 2,
        out_specs=vmem,
        compiler_params=pltpu.CompilerParams(vmem_limit_bytes=8 * 1024 * 1024),
        cost_estimate=pl.CostEstimate(flops=65 << 27, bytes_accessed=0, transcendentals=0),
    )(*all_keys[-2:])
    weights, inverse, sorted_values, last_run = pl.pallas_call(
        functools.partial(weights_kernel, runs),
        out_shape=(
            jax.ShapeDtypeStruct((2 * KEY_VALUE_HEADS, GROUP * RUN, (runs // 4 + 1) * RUN), jnp.bfloat16),
            jax.ShapeDtypeStruct((2 * KEY_VALUE_HEADS, GROUP * RUN, HEAD_SIZE), jnp.float32),
            jax.ShapeDtypeStruct((KEY_VALUE_HEADS, runs, RUN, HEAD_SIZE), jnp.bfloat16),
            jax.ShapeDtypeStruct((8, HEAD_SIZE), jnp.float32),
        ),
        in_specs=[vmem] * (4 + len(all_keys) + len(all_values[:-2])),
        out_specs=(vmem,) * 4,
        scratch_shapes=[pltpu.VMEM((runs, RUN, KV_COLUMNS), jnp.bfloat16)],
        compiler_params=params,
        cost_estimate=pl.CostEstimate(flops=1 << 26, bytes_accessed=1 << 20, transcendentals=0),
    )(plan, bias, mark, own, *all_keys, *all_values[:-2])
    out = pl.pallas_call(
        functools.partial(values_kernel, runs),
        out_shape=jax.ShapeDtypeStruct((TOK_DEV, QUERY_COLUMNS), jnp.bfloat16),
        in_specs=[vmem] * 7,
        out_specs=pl.BlockSpec(memory_space=pl.ANY),
        scratch_shapes=[
            pltpu.VMEM((2, RUN, QUERY_COLUMNS), jnp.bfloat16),
            pltpu.SemaphoreType.DMA((2 * KEY_VALUE_HEADS,)),
        ],
        compiler_params=params,
        cost_estimate=pl.CostEstimate(flops=1 << 26, bytes_accessed=1 << 20, transcendentals=0),
    )(plan, last_run, weights, inverse, sorted_values, *all_values[-2:])
    return out[None]


def solution(mesh):
    return jax.shard_map(
        per_device,
        mesh=mesh,
        in_specs=(
            P("section", "ctx", None),
            P("section", "ctx", None),
            P("section", "ctx", None),
            P("ctx"),
            P(),
        ),
        out_specs=P("section", "ctx", None),
        check_vma=False,
    )
```

```python
import functools
import math

import jax
import jax.numpy as jnp
from jax import lax
from jax.experimental import pallas as pl
from jax.experimental.pallas import tpu as pltpu
from jax.sharding import PartitionSpec as P

HEAD_SIZE = 128
QUERY_HEADS = 32
KEY_VALUE_HEADS = 4
GROUP = QUERY_HEADS // KEY_VALUE_HEADS
RUN = 64
TOK_DEV = 2 * RUN
QUERY_COLUMNS = QUERY_HEADS * HEAD_SIZE
KV_COLUMNS = KEY_VALUE_HEADS * HEAD_SIZE
TAG_ROWS = 16
VALUE_ROWS = KEY_VALUE_HEADS * TOK_DEV

masked_fill = -1e30


def first_run(pos_ref):
    return lax.div(pos_ref[:, :TOK_DEV][0, 0].astype(jnp.int32), RUN)


def needs_far(runs, pos_ref, run):
    segment = pos_ref[:, TOK_DEV:]
    position = lax.broadcasted_iota(jnp.int32, segment.shape, 1)
    doc = jnp.max(jnp.where(position == run * RUN, segment, -1.0))
    far_doc = jnp.max(jnp.where(position == (run - runs // 4 + 1) * RUN - 1, segment, -1.0))
    return doc == far_doc


def write_number(ref, row, number):
    ref[row : row + 1, :] = jnp.full((1, ref.shape[1]), number.astype(jnp.float32))


def read_number(ref, row):
    return ref[row : row + 1, :].astype(jnp.float32)[0, 0].astype(jnp.int32)


def run_numbers(runs, first, tagged_refs):
    firsts = [first]
    for ref in tagged_refs:
        firsts.append(ref[VALUE_ROWS:, :].astype(jnp.float32)[0, 0].astype(jnp.int32))
    places = runs // 2
    firsts.append(places * (places - 1) // 2 - sum(firsts))
    return [(first, runs - 1 - first) for first in firsts]


def sort_keys(numbers, own_ref, block_refs, last_refs, sorted_ref):
    for half, number in enumerate(numbers[0]):
        sorted_ref[number] = own_ref[half * RUN : (half + 1) * RUN, QUERY_COLUMNS : QUERY_COLUMNS + KV_COLUMNS]
    for (first, second), ref in zip(numbers[1:], block_refs):
        sorted_ref[first] = ref[:RUN, :]
        sorted_ref[second] = ref[RUN:, :]
    cut = last_refs[0].shape[0] - RUN
    first, second = numbers[-1]
    sorted_ref[first] = last_refs[0][:RUN, :]
    sorted_ref[second, :cut] = last_refs[0][RUN:, :]
    sorted_ref[second, cut:] = last_refs[1][...]


def sort_values(numbers, own_ref, block_refs, sorted_ref):
    for kv in range(KEY_VALUE_HEADS):
        column = QUERY_COLUMNS + KV_COLUMNS + kv * HEAD_SIZE
        for half, number in enumerate(numbers[0]):
            sorted_ref[kv, number] = own_ref[half * RUN : (half + 1) * RUN, column : column + HEAD_SIZE]
        for pair, ref in zip(numbers[1:], block_refs):
            for half, number in enumerate(pair):
                row = kv * TOK_DEV + half * RUN
                sorted_ref[kv, number] = ref[row : row + RUN, :]


def blank_kernel(*refs):
    refs[-1][...] = jnp.zeros_like(refs[-1])


def bias_kernel(runs, pos_ref, bias_ref, plan_ref):
    segment = pos_ref[:, TOK_DEV:]
    first = first_run(pos_ref)
    write_number(plan_ref, 0, first)
    far = needs_far(runs, pos_ref, first) | needs_far(runs, pos_ref, runs - 1 - first)
    write_number(plan_ref, 3, jnp.where(far, 1, 0))
    for half, run in enumerate((first, runs - 1 - first)):
        row_pos = run * RUN + lax.broadcasted_iota(jnp.int32, (RUN, 1), 0)
        at = lax.broadcasted_iota(jnp.int32, (RUN, runs * RUN), 1) == row_pos
        row_doc = jnp.sum(jnp.where(at, segment, 0.0), axis=1, keepdims=True)
        doc_start = jnp.sum(jnp.where(segment < row_doc, 1.0, 0.0), axis=1, keepdims=True).astype(jnp.int32)
        start = jnp.maximum(run - runs // 4 + jnp.where(far, 0, 1), 0)
        write_number(plan_ref, 1 + half, start)
        key_pos = start * RUN + lax.broadcasted_iota(jnp.int32, bias_ref.shape[1:], 1)
        bias_ref[half] = jnp.where((key_pos <= row_pos) & (key_pos >= doc_start), 0.0, masked_fill)


def weights_kernel(runs, plan_ref, bias_ref, mark_ref, own_ref, *refs):
    blocks = runs // 2
    key_refs, tagged_refs = refs[:blocks], refs[blocks:-5]
    weights_ref, inverse_ref, sorted_ref, last_run_ref, key_buf = refs[-5:]
    numbers = run_numbers(runs, read_number(plan_ref, 0), tagged_refs)
    write_number(last_run_ref, 0, numbers[-1][0])
    starts = [read_number(plan_ref, 1 + half) for half in range(2)]
    far = read_number(plan_ref, 3) > 0
    sort_keys(numbers, own_ref, key_refs[:-2], key_refs[-2:], key_buf)
    sort_values(numbers, own_ref, tagged_refs, sorted_ref)
    scale = math.log2(math.e) / math.sqrt(HEAD_SIZE)

    def half_weights(half, start, count):
        span = count * RUN
        bias = jnp.concatenate([bias_ref[half, :, :span]] * GROUP, axis=0)
        for kv in range(KEY_VALUE_HEADS):
            query = jnp.concatenate(
                [
                    own_ref[half * RUN : (half + 1) * RUN, h * HEAD_SIZE : (h + 1) * HEAD_SIZE]
                    for h in range(kv * GROUP, (kv + 1) * GROUP)
                ],
                axis=0,
            )
            key = key_buf[pl.ds(start, count), :, kv * HEAD_SIZE : (kv + 1) * HEAD_SIZE]
            scores = bias + lax.dot_general(
                query,
                key.reshape(span, HEAD_SIZE),
                (((1,), (1,)), ((), ())),
                preferred_element_type=jnp.float32,
            )
            row_max = jnp.max(scores, axis=1, keepdims=True)
            weights = jnp.exp2((scores - row_max) * scale)
            total = jnp.sum(weights, axis=1, keepdims=True)
            inverse = pl.reciprocal(total, approx=True)
            inverse = inverse * (2.0 - total * inverse)
            weights_ref[half * KEY_VALUE_HEADS + kv, :, :span] = weights.astype(jnp.bfloat16)
            inverse_ref[half * KEY_VALUE_HEADS + kv] = jnp.broadcast_to(inverse, (GROUP * RUN, HEAD_SIZE))

    def both_weights(count):
        for half in range(2):
            half_weights(half, starts[half], count)

    lax.cond(far, lambda: both_weights(runs // 4 + 1), lambda: both_weights(runs // 4))


def values_kernel(runs, plan_ref, last_run_ref, weights_ref, inverse_ref, sorted_ref, *refs):
    last_refs, (out_ref, result_buf, out_sems) = refs[:2], refs[2:]
    last_run = read_number(last_run_ref, 0)
    last_runs = (last_run, runs - 1 - last_run)
    starts = [read_number(plan_ref, 1 + half) for half in range(2)]
    far = read_number(plan_ref, 3) > 0

    def half_values(half, start, count):
        for kv in range(KEY_VALUE_HEADS):
            parts = []
            for i in range(count):
                part = sorted_ref[kv, start + i]
                for last_half, number in enumerate(last_runs):
                    row = kv * TOK_DEV + last_half * RUN
                    which, row = divmod(row, VALUE_ROWS - RUN)
                    part = jnp.where(start + i == number, last_refs[which][row : row + RUN, :], part)
                parts.append(part)
            summed = jnp.dot(
                weights_ref[half * KEY_VALUE_HEADS + kv, :, : count * RUN],
                jnp.concatenate(parts, axis=0),
                preferred_element_type=jnp.float32,
            )
            result = (summed * inverse_ref[half * KEY_VALUE_HEADS + kv]).astype(jnp.bfloat16)
            for i in range(GROUP):
                h = kv * GROUP + i
                result_buf[half, :, h * HEAD_SIZE : (h + 1) * HEAD_SIZE] = result[i * RUN : (i + 1) * RUN]
            copies[half * KEY_VALUE_HEADS + kv].start()

    copies = []
    for half in range(2):
        for kv in range(KEY_VALUE_HEADS):
            columns = pl.ds(kv * GROUP * HEAD_SIZE, GROUP * HEAD_SIZE)
            copies.append(
                pltpu.make_async_copy(
                    result_buf.at[half, :, columns],
                    out_ref.at[pl.ds(half * RUN, RUN), columns],
                    out_sems.at[half * KEY_VALUE_HEADS + kv],
                )
            )

    def both_values(count):
        for half in range(2):
            half_values(half, starts[half], count)

    lax.cond(far, lambda: both_values(runs // 4 + 1), lambda: both_values(runs // 4))
    for copy in copies:
        copy.wait()


def per_device(queries, keys, values, token_pos, segment):
    sections, places = lax.axis_size("section"), lax.axis_size("ctx")
    runs = segment.shape[0] // RUN
    depth = places // 2
    ring = [z * 2 for z in range(depth)] + [z * 2 + 1 for z in reversed(range(depth))]

    def shift(block, section_by, ring_by):
        pairs = []
        for s in range(sections):
            for i in range(places):
                target = (s + section_by) % sections * places + ring[(i + ring_by) % places]
                pairs.append((s * places + ring[i], target))
        return lax.ppermute(block, ("section", "ctx"), pairs)

    def around(block, rows, cut, early=None):
        ahead, back = shift(block, 1, 1), shift(block, 1, -1)
        held = [ahead, back]
        for step in range(2, places // 2):
            if early is not None and step == places // 2 - 1:
                ahead, _ = lax.optimization_barrier((ahead, early))
            ahead, back = shift(ahead, 0, 1), shift(back, 0, -1)
            held.extend([ahead, back])
        return held + [shift(ahead[:cut], 0, 1), shift(back[cut:rows], 0, -1)]

    own = shift(jnp.concatenate([queries[0], keys[0], values[0]], axis=1), 1, 0)
    vmem = pl.BlockSpec(memory_space=pltpu.VMEM)
    blank = pl.pallas_call(
        blank_kernel,
        out_shape=jax.ShapeDtypeStruct((TAG_ROWS, TOK_DEV), jnp.bfloat16),
        out_specs=vmem,
        compiler_params=pltpu.CompilerParams(vmem_limit_bytes=8 * 1024 * 1024),
        cost_estimate=pl.CostEstimate(flops=1 << 30, bytes_accessed=0, transcendentals=0),
    )()
    tag = (token_pos >> (RUN.bit_length() - 1)).astype(jnp.bfloat16)
    by_head = [values[0, :, kv * HEAD_SIZE : (kv + 1) * HEAD_SIZE] for kv in range(KEY_VALUE_HEADS)]
    tagged = jnp.concatenate([*by_head, blank + tag[None]], axis=0)
    pos = lax.optimization_barrier(jnp.concatenate([token_pos, segment]).astype(jnp.float32)[None])
    bias, plan = pl.pallas_call(
        functools.partial(bias_kernel, runs),
        out_shape=(
            jax.ShapeDtypeStruct((2, RUN, (runs // 4 + 1) * RUN), jnp.float32),
            jax.ShapeDtypeStruct((8, HEAD_SIZE), jnp.float32),
        ),
        in_specs=[vmem],
        out_specs=(vmem,) * 2,
        compiler_params=pltpu.CompilerParams(vmem_limit_bytes=8 * 1024 * 1024),
        cost_estimate=pl.CostEstimate(flops=1 << 20, bytes_accessed=1 << 10, transcendentals=0),
    )(pos)
    all_keys = around(keys[0], TOK_DEV, TOK_DEV * 3 // 4)
    all_values = around(tagged, VALUE_ROWS, VALUE_ROWS - RUN, bias)
    params = pltpu.CompilerParams(vmem_limit_bytes=(12 + runs // 4) * 1024 * 1024)
    mark = pl.pallas_call(
        blank_kernel,
        out_shape=jax.ShapeDtypeStruct((8, HEAD_SIZE), jnp.float32),
        in_specs=[vmem] * 2,
        out_specs=vmem,
        compiler_params=pltpu.CompilerParams(vmem_limit_bytes=8 * 1024 * 1024),
        cost_estimate=pl.CostEstimate(flops=65 << 27, bytes_accessed=0, transcendentals=0),
    )(*all_keys[-2:])
    weights, inverse, sorted_values, last_run = pl.pallas_call(
        functools.partial(weights_kernel, runs),
        out_shape=(
            jax.ShapeDtypeStruct((2 * KEY_VALUE_HEADS, GROUP * RUN, (runs // 4 + 1) * RUN), jnp.bfloat16),
            jax.ShapeDtypeStruct((2 * KEY_VALUE_HEADS, GROUP * RUN, HEAD_SIZE), jnp.float32),
            jax.ShapeDtypeStruct((KEY_VALUE_HEADS, runs, RUN, HEAD_SIZE), jnp.bfloat16),
            jax.ShapeDtypeStruct((8, HEAD_SIZE), jnp.float32),
        ),
        in_specs=[vmem] * (4 + len(all_keys) + len(all_values[:-2])),
        out_specs=(vmem,) * 4,
        scratch_shapes=[pltpu.VMEM((runs, RUN, KV_COLUMNS), jnp.bfloat16)],
        compiler_params=params,
        cost_estimate=pl.CostEstimate(flops=1 << 26, bytes_accessed=1 << 20, transcendentals=0),
    )(plan, bias, mark, own, *all_keys, *all_values[:-2])
    out = pl.pallas_call(
        functools.partial(values_kernel, runs),
        out_shape=jax.ShapeDtypeStruct((TOK_DEV, QUERY_COLUMNS), jnp.bfloat16),
        in_specs=[vmem] * 7,
        out_specs=pl.BlockSpec(memory_space=pl.ANY),
        scratch_shapes=[
            pltpu.VMEM((2, RUN, QUERY_COLUMNS), jnp.bfloat16),
            pltpu.SemaphoreType.DMA((2 * KEY_VALUE_HEADS,)),
        ],
        compiler_params=params,
        cost_estimate=pl.CostEstimate(flops=1 << 26, bytes_accessed=1 << 20, transcendentals=0),
    )(plan, last_run, weights, inverse, sorted_values, *all_values[-2:])
    return out[None]


def solution(mesh):
    return jax.shard_map(
        per_device,
        mesh=mesh,
        in_specs=(
            P("section", "ctx", None),
            P("section", "ctx", None),
            P("section", "ctx", None),
            P("ctx"),
            P(),
        ),
        out_specs=P("section", "ctx", None),
        check_vma=False,
    )
```
